32 devices in a mesh: tm: 8 (over z, x), tile: 4 (over y, core).
Axes of the slice: x: 2, y: 2, z: 4, core: 2. Of those that a mesh axis runs over, the one named last changes fastest.
Arguments:
- features: bfloat16 [8, 8, 160, 512], P('tm', 'tile'), may hold values from -200 to 200, as said below
- norm_gain: float32 [512], replicated, may hold values from 0.1 to 1.9
- query_weight: bfloat16 [512, 512], replicated, may hold values from -7.9991455 to 7.9991455, as said below
- key_weight: bfloat16 [512, 512], replicated, may hold values from -0.25 to 0.25
- value_weight: bfloat16 [512, 512], replicated, may hold values from -0.25 to 0.25
- out_weight: bfloat16 [512, 512], replicated, may hold values from -0.5 to 0.5
- conv_weight: bfloat16 [3, 3, 3, 512, 256], replicated, may hold values from -0.0546875 to 0.0546875
- skip_weight: bfloat16 [512, 256], replicated, may hold values from -0.125 to 0.125
Outputs:
- decoded: bfloat16 [16, 8, 160, 256], P('tm', 'tile')
The draws below stay inside these ranges and needn't reach their ends.
Inputs may be any that keep to these rules, and one draw needn't show every extreme that they name: Latent features whose magnitude varies from row to row and column to column. `query_weight`: A dense projection matrix.
All inputs are finite; a program needn't handle non-finite values.
Results may differ from the reference program's by a relative error of at most 0.012.
The reference program's roundings to bfloat16 on the way (of `normed`, `weights`, `attended`, `mid` and `act`) count: a program that leaves them out, or rounds other values in their place, can miss the bound.
Values may be sent and summed in bfloat16 or wider, within the bound.
No kernel may reach another device: no remote copies, remote signals or barrier semaphores. Data moves between devices by JAX's collectives and lax.ppermute only.
A program may use at most 128 MiB of HBM per device.

```python
import jax
import jax.numpy as jnp
from jax import lax

C = 512
C2 = 256
GROUPS = 32
COLS = 160
FRAMES = 8
ROWS = 8


def draw_features(key, part):
    first_key, second_key, third_key = jax.random.split(key, 3)
    shape = (FRAMES, ROWS, COLS, C)
    row_scale = (3.0 ** (jnp.arange(ROWS, dtype=jnp.float32) / max(ROWS - 1, 1))).reshape(1, ROWS, 1, 1)
    col_scale = jnp.exp(jax.random.uniform(second_key, (1, 1, COLS, 1)) * jnp.log(3.5))
    chan_scale = jnp.exp(jax.random.uniform(third_key, (1, 1, 1, C)) * jnp.log(2.0))
    base = jnp.clip(jax.random.normal(first_key, shape), -5.0, 5.0)
    return jnp.clip(base * row_scale * col_scale * chan_scale, -200.0, 200.0).astype(jnp.bfloat16)


def draw_query_weight(key, part):
    values = jnp.clip(jax.random.normal(key, (C, C)), -6.0, 6.0) * C ** (-0.5)
    return values.astype(jnp.bfloat16)


def normal_values(rng, extent, spread, most, kind=jnp.bfloat16):
    array = spread * jax.random.normal(rng, extent, jnp.float32)
    return jnp.clip(array, min=-most, max=most).astype(kind)


def setup_inputs(seed: int = 0) -> dict:
    streams_of = jax.random.split(jax.random.key(seed), 9)
    features = draw_features(jax.random.fold_in(streams_of[8], 71), 0)
    norm_gain = jnp.clip(1.0 + 0.18 * jax.random.normal(streams_of[1], (C,), jnp.float32), 0.1, 1.9)
    query_weight = draw_query_weight(jax.random.fold_in(streams_of[8], 71), 0)
    key_weight = normal_values(streams_of[3], (C, C), C ** -0.5, 0.25)
    value_weight = normal_values(streams_of[4], (C, C), C ** -0.5, 0.25)
    out_weight = normal_values(streams_of[5], (C, C), (C // 4) ** -0.5, 0.5)
    conv_weight = normal_values(streams_of[6], (3, 3, 3, C, C2), (27 * C) ** -0.5, 0.0546875)
    skip_weight = normal_values(streams_of[7], (C, C2), (4 * C) ** -0.5, 0.125)
    return {"features": features, "norm_gain": norm_gain, "query_weight": query_weight, "key_weight": key_weight, "value_weight": value_weight, "out_weight": out_weight, "conv_weight": conv_weight, "skip_weight": skip_weight}


def frame_patches(frame):
    padded = jnp.pad(frame, ((1, 1), (1, 1), (0, 0)))
    pieces = [padded[offset_y:offset_y + ROWS, offset_x:offset_x + COLS, :] for offset_y in range(3) for offset_x in range(3)]
    return jnp.concatenate(pieces, axis=-1).reshape(ROWS * COLS, 9 * C)

def reference(features, norm_gain, query_weight, key_weight, value_weight, out_weight, conv_weight, skip_weight):
    cell_count = ROWS * COLS
    grouped = features.astype(jnp.float32).reshape(FRAMES, cell_count, GROUPS, C // GROUPS)
    mean = lax.optimization_barrier(jnp.mean(grouped, axis=(1, 3), keepdims=True))
    var = lax.optimization_barrier(jnp.mean(grouped * grouped, axis=(1, 3), keepdims=True)) - mean * mean
    normed = ((grouped - mean) * lax.rsqrt(var + 1e-06)).reshape(FRAMES, cell_count, C) * norm_gain
    normed = normed.astype(jnp.bfloat16)

    def attend(frame_normed):
        queries = jnp.dot(frame_normed, query_weight, preferred_element_type=jnp.float32).astype(jnp.bfloat16)
        key_rows = jnp.dot(frame_normed, key_weight, preferred_element_type=jnp.float32).astype(jnp.bfloat16)
        value_rows = jnp.dot(frame_normed, value_weight, preferred_element_type=jnp.float32).astype(jnp.bfloat16)
        scores = jnp.dot(queries, key_rows.T, preferred_element_type=jnp.float32) * C ** (-0.5)
        peak = lax.optimization_barrier(jnp.max(scores, axis=1, keepdims=True))
        unnormed = jnp.exp(scores - peak)
        denominator = lax.optimization_barrier(jnp.sum(unnormed, axis=1, keepdims=True))
        weights = unnormed.astype(jnp.bfloat16)
        attended = (jnp.dot(weights, value_rows, preferred_element_type=jnp.float32) / denominator).astype(jnp.bfloat16)
        return jnp.dot(attended, out_weight, preferred_element_type=jnp.float32)
    change = lax.map(attend, normed)
    mid = (features.astype(jnp.float32).reshape(FRAMES, cell_count, C) + change).astype(jnp.bfloat16)
    act = jax.nn.silu(mid.astype(jnp.float32)).astype(jnp.bfloat16).reshape(FRAMES, ROWS, COLS, C)
    before_all = jnp.concatenate([act[:1], act[:-1]], axis=0)
    taps = conv_weight.reshape(3, 9 * C, C2)

    def decode(packed):
        before, current, mid_frame = packed
        patch_before = frame_patches(before)
        patch_now = frame_patches(current)
        skip = jnp.dot(mid_frame, skip_weight, preferred_element_type=jnp.float32)
        first_tap = jnp.dot(patch_before, taps[0], preferred_element_type=jnp.float32)
        even = first_tap + jnp.dot(patch_before, taps[1], preferred_element_type=jnp.float32) + jnp.dot(patch_now, taps[2], preferred_element_type=jnp.float32) + skip
        odd = first_tap + jnp.dot(patch_now, taps[1], preferred_element_type=jnp.float32) + jnp.dot(patch_now, taps[2], preferred_element_type=jnp.float32) + skip
        return jnp.stack([even, odd], axis=0).astype(jnp.bfloat16)
    decoded = lax.map(decode, (before_all, act, mid))
    return decoded.reshape(2 * FRAMES, ROWS, COLS, C2)
```

```python
import functools

import jax
import jax.numpy as jnp
from jax import lax
from jax.experimental import pallas as pl
from jax.experimental.pallas import tpu as pltpu
from jax.sharding import PartitionSpec as P

GROUPS = 32
BF = jnp.bfloat16
F32 = jnp.float32
VMEM = pltpu.VMEM
LIMIT = 48 * 1024 * 1024


def dot(left, right):
    return jnp.dot(left, right, preferred_element_type=F32)


def dot_t(left, right):
    return lax.dot_general(left, right, (((1,), (1,)), ((), ())), preferred_element_type=F32)


def spec(space=VMEM):
    return pl.BlockSpec(memory_space=space)


def call(body, outs, scratch, cost, *args, spaces=None):
    spaces = spaces or [VMEM] * len(args)
    return pl.pallas_call(
        body,
        out_shape=outs,
        in_specs=[spec(s) for s in spaces],
        out_specs=jax.tree.map(lambda _: spec(), outs),
        scratch_shapes=scratch,
        compiler_params=pltpu.CompilerParams(vmem_limit_bytes=LIMIT),
        cost_estimate=pl.CostEstimate(flops=cost, bytes_accessed=1 << 20, transcendentals=0),
    )(*args)


def stats_body(own_ref, sib_ref, out_ref):
    total = jnp.zeros((1, own_ref.shape[1]), F32)
    squared = total
    for ref in (own_ref, sib_ref):
        block = ref[...].astype(F32)
        total += jnp.sum(block, axis=0, keepdims=True)
        squared += jnp.sum(block * block, axis=0, keepdims=True)
    out_ref[...] = jnp.concatenate(
        [total, squared, jnp.zeros((6, own_ref.shape[1]), F32)], axis=0
    )


def group_sums(sums, width):
    lane = lax.broadcasted_iota(jnp.int32, sums.shape, 1)
    size = sums.shape[1]
    step = 1
    while step < width:
        low = pltpu.roll(sums, size - step, 1)
        high = pltpu.roll(sums, step, 1)
        sums = sums + jnp.where((lane & step) == 0, low, high)
        step *= 2
    return sums


def moments(sum_refs, cells):
    sums = sum_refs[0][...]
    for ref in sum_refs[1:]:
        sums = sums + ref[...]
    width = sums.shape[1] // GROUPS
    sums = group_sums(sums, width)
    population = cells * width
    mean = sums[0:1] / population
    var = sums[1:2] / population - mean * mean
    return mean, lax.rsqrt(var + 1e-06)


def normalise(block, mean, inverse, gain):
    return ((block.astype(F32) - mean) * inverse * gain).astype(BF)


def attend(queries, keys, values, state, exponent):
    scores = dot_t(queries, keys)
    peak = jnp.max(scores, axis=1, keepdims=True)
    if state is not None:
        old_peak, old_sum, old = state
        peak = jnp.maximum(peak, old_peak)
    unnormed = jnp.exp2((scores - peak) * exponent)
    total = jnp.sum(unnormed, axis=1, keepdims=True)
    mixed = dot(unnormed.astype(BF), values)
    if state is not None:
        fade = jnp.exp2((old_peak - peak) * exponent)
        total = total + old_sum * fade
        mixed = mixed + old * fade
    return peak, total, mixed


def early_body(
    cells_all, cols, exponent, n_sums,
    place_ref, own_ref, sib_ref, *refs,
):
    sum_refs, refs = refs[:n_sums], refs[n_sums:]
    gain_ref, wq_ref, wk_ref, wv_ref, q_ref, k_ref, v_ref, peak_ref, sum_ref, mix_ref = refs
    mean, inverse = moments(sum_refs, cells_all)
    gain = gain_ref[...]
    cells = own_ref.shape[0]
    core = place_ref[0]
    own = normalise(own_ref[...], mean, inverse, gain)
    sib = normalise(sib_ref[...], mean, inverse, gain)
    near = pl.multiple_of(core * (cells - cols), 16)
    halo = normalise(sib_ref[pl.ds(near, cols), :], mean, inverse, gain)
    queries = dot(jnp.concatenate([own, halo], axis=0), wq_ref[...]).astype(BF)
    both = jnp.concatenate([own, sib], axis=0)
    keys = dot(both, wk_ref[...]).astype(BF)
    values = dot(both, wv_ref[...]).astype(BF)
    q_ref[...] = queries
    k_ref[...] = keys
    v_ref[...] = values
    peak, total, mixed = attend(queries, keys, values, None, exponent)
    peak_ref[...] = jnp.broadcast_to(peak, peak_ref.shape)
    sum_ref[...] = jnp.broadcast_to(total, sum_ref.shape)
    mix_ref[...] = mixed


def spread(act, rows, cols):
    size = act.shape[0]
    col = lax.broadcasted_iota(jnp.int32, act.shape, 0) % cols
    left = jnp.where(col == 0, 0.0, pltpu.roll(act, 1, 0))
    right = jnp.where(col == cols - 1, 0.0, pltpu.roll(act, size - 1, 0))
    return jnp.concatenate([left.astype(BF), act.astype(BF), right.astype(BF)], axis=1)


def conv(wide_ref, taps, out_cells, cols):
    total = None
    for row in range(3):
        term = dot(wide_ref[row * cols : row * cols + out_cells, :], taps(row))
        total = term if total is None else total + term
    return total


def late_body(
    cells_all, cols, exponent, n_sums, n_remote,
    place_ref, own_ref, sib_ref, *refs,
):
    sum_refs, refs = refs[:n_sums], refs[n_sums:]
    recv_refs, refs = refs[:n_remote], refs[n_remote:]
    rsib_refs, refs = refs[:n_remote], refs[n_remote:]
    (gain_ref, wq_ref, wk_ref, wv_ref, wo_ref, conv_ref, q_ref, k_ref, v_ref, peak_ref, sum_ref,
     mix_ref, part_ref, act_ref, mid_ref, wide_ref, taps_ref, sem) = refs
    copy = pltpu.make_async_copy(conv_ref.at[pl.ds(0, 2)], taps_ref, sem)
    copy.start()
    mean, inverse = moments(sum_refs, cells_all)
    gain = gain_ref[...]
    cells = own_ref.shape[0]
    core = place_ref[0]
    far = pl.multiple_of((1 - core) * (cells - cols), 16)
    first = rsib_refs[0][pl.ds(far, cols), :]
    last = rsib_refs[-1][pl.ds(far, cols), :]
    far_block = first if n_remote == 1 else jnp.where(core == 0, first, last)
    far_query = dot(normalise(far_block, mean, inverse, gain), wq_ref[...]).astype(BF)
    far_state = attend(far_query, k_ref[...], v_ref[...], None, exponent)
    state = [
        jnp.concatenate([near, new], axis=0)
        for near, new in zip(
            (peak_ref[:, 0:1], sum_ref[:, 0:1], mix_ref[...]), far_state, strict=True
        )
    ]
    queries = jnp.concatenate([q_ref[...], far_query], axis=0)
    for recv_ref, rsib_ref in zip(recv_refs, rsib_refs, strict=True):
        both = normalise(
            jnp.concatenate([recv_ref[...], rsib_ref[...]], axis=0), mean, inverse, gain
        )
        keys = dot(both, wk_ref[...]).astype(BF)
        values = dot(both, wv_ref[...]).astype(BF)
        state = attend(queries, keys, values, state, exponent)
    attended = (state[2] / state[1]).astype(BF)
    change = dot(attended, wo_ref[...])
    near = pl.multiple_of(core * (cells - cols), 16)
    base = jnp.concatenate([own_ref[...], sib_ref[pl.ds(near, cols), :], far_block], axis=0)
    mid = (base.astype(F32) + change).astype(BF)
    mid_ref[...] = mid[:cells]
    act = jax.nn.silu(mid.astype(F32))
    inside = place_ref[1] != 0
    near_act = act[cells : cells + cols]
    far_act = jnp.where(inside, act[cells + cols :], 0.0)
    above = jnp.where(core == 0, far_act, near_act)
    below = jnp.where(core == 0, near_act, far_act)
    act = jnp.concatenate([above, act[:cells], below], axis=0).astype(BF)
    act_ref[...] = act
    wide_ref[...] = spread(act.astype(F32), cells // cols + 2, cols)
    copy.wait()
    first_tap = conv(wide_ref, lambda row: taps_ref[0, row], cells, cols)
    second_tap = conv(wide_ref, lambda row: taps_ref[1, row], cells, cols)
    part_ref[0] = (first_tap + second_tap).astype(BF)
    part_ref[1] = first_tap.astype(BF)


def now_body(cols, act_ref, mid_ref, conv_ref, skip_ref, out_ref, wide_ref, taps_ref, sem):
    copy = pltpu.make_async_copy(conv_ref.at[pl.ds(1, 2)], taps_ref, sem)
    copy.start()
    cells = mid_ref.shape[0]
    wide_ref[...] = spread(act_ref[...].astype(F32), cells // cols + 2, cols)
    skip = dot(mid_ref[...], skip_ref[...])
    copy.wait()
    second_tap = conv(wide_ref, lambda row: taps_ref[0, row], cells, cols)
    last_tap = conv(wide_ref, lambda row: taps_ref[1, row], cells, cols) + skip
    out_ref[0] = last_tap
    out_ref[1] = last_tap + second_tap


def per_device(
    features,
    norm_gain,
    query_weight,
    key_weight,
    value_weight,
    out_weight,
    conv_weight,
    skip_weight,
):
    _, tile_rows, cols, channels = features.shape
    out_channels = conv_weight.shape[-1]
    cells = tile_rows * cols
    devices = lax.axis_size("tile")
    chips = devices // 2
    me = lax.axis_index("tile")
    core = me % 2
    swap = [(i, i ^ 1) for i in range(devices)]
    own = features.reshape(cells, channels)

    def turned(array, by):
        return lax.ppermute(array, "tile", [(i, (i + 2 * by) % devices) for i in range(devices)])

    recv = [turned(own, by) for by in range(1, chips)]
    sib = lax.ppermute(own, "tile", swap)
    rsib = [lax.ppermute(block, "tile", swap) for block in recv]
    sums = call(
        stats_body, jax.ShapeDtypeStruct((8, channels), F32), [], 1 << 22, own, sib
    )
    sums = [sums] + [turned(sums, by) for by in range(1, chips)]

    gain = norm_gain.reshape(1, channels)
    exponent = channels ** (-0.5) * 1.4426950408889634
    outside = jnp.where(core == 0, me == 0, me == devices - 1)
    place = jnp.stack([core, 1 - outside.astype(jnp.int32)]).astype(jnp.int32)
    near = cells + cols
    shapes = [
        jax.ShapeDtypeStruct((near, channels), BF),
        jax.ShapeDtypeStruct((2 * cells, channels), BF),
        jax.ShapeDtypeStruct((2 * cells, channels), BF),
        jax.ShapeDtypeStruct((near, 128), F32),
        jax.ShapeDtypeStruct((near, 128), F32),
        jax.ShapeDtypeStruct((near, channels), F32),
    ]
    n_sums = len(sums)
    early = call(
        functools.partial(early_body, devices * cells, cols, exponent, n_sums),
        shapes,
        [],
        2 * 10**9,
        place, own, sib, *sums, gain, query_weight, key_weight, value_weight,
        spaces=[pltpu.SMEM] + [VMEM] * (6 + n_sums),
    )
    taps = conv_weight.reshape(3, 3, 3 * channels, out_channels)
    wide = VMEM((cells + 2 * cols, 3 * channels), BF)
    held = VMEM((2, 3, 3 * channels, out_channels), BF)
    part, act, mid = call(
        functools.partial(late_body, devices * cells, cols, exponent, n_sums, chips - 1),
        [
            jax.ShapeDtypeStruct((2, cells, out_channels), BF),
            jax.ShapeDtypeStruct((cells + 2 * cols, channels), BF),
            jax.ShapeDtypeStruct((cells, channels), BF),
        ],
        [wide, held, pltpu.SemaphoreType.DMA],
        4 * 10**9,
        place, own, sib, *sums, *recv, *rsib, gain, query_weight, key_weight, value_weight,
        out_weight, taps, *early,
        spaces=[pltpu.SMEM] + [VMEM] * (2 + n_sums + 2 * (chips - 1) + 5) + [pl.ANY] + [VMEM] * 6,
    )
    spans = lax.axis_size("tm")
    arrived = lax.ppermute(part, "tm", [(i, i + 1) for i in range(spans - 1)])
    now = call(
        functools.partial(now_body, cols),
        jax.ShapeDtypeStruct((2, cells, out_channels), F32),
        [wide, held, pltpu.SemaphoreType.DMA],
        2 * 10**9,
        act, mid, taps, skip_weight,
        spaces=[VMEM, VMEM, pl.ANY, VMEM],
    )
    before = jnp.where(lax.axis_index("tm") == 0, part, arrived)
    decoded = (now + before.astype(F32)).astype(BF)
    return decoded.reshape(2, tile_rows, cols, out_channels)


def solution(mesh):
    in_specs = (P("tm", "tile", None, None), P(), P(), P(), P(), P(), P(), P())
    out_specs = P("tm", "tile", None, None)
    return jax.shard_map(
        per_device, mesh=mesh, in_specs=in_specs, out_specs=out_specs, check_vma=False
    )
```

```python
import functools

import jax
import jax.numpy as jnp
from jax import lax
from jax.experimental import pallas as pl
from jax.experimental.pallas import tpu as pltpu
from jax.sharding import PartitionSpec as P

GROUPS = 32
BF = jnp.bfloat16
F32 = jnp.float32
VMEM = pltpu.VMEM
LIMIT = 20 * 1024 * 1024


def dot(left, right):
    return jnp.dot(left, right, preferred_element_type=F32)


def dot_t(left, right):
    return lax.dot_general(left, right, (((1,), (1,)), ((), ())), preferred_element_type=F32)


def spec(space=VMEM):
    return pl.BlockSpec(memory_space=space)


def call(body, outs, scratch, cost, *args, spaces=None):
    spaces = spaces or [VMEM] * len(args)
    return pl.pallas_call(
        body,
        out_shape=outs,
        in_specs=[spec(s) for s in spaces],
        out_specs=jax.tree.map(lambda _: spec(), outs),
        scratch_shapes=scratch,
        compiler_params=pltpu.CompilerParams(vmem_limit_bytes=LIMIT),
        cost_estimate=pl.CostEstimate(flops=cost, bytes_accessed=1 << 20, transcendentals=0),
    )(*args)


def stats_body(own_ref, sib_ref, out_ref):
    total = jnp.zeros((1, own_ref.shape[1]), F32)
    squared = total
    for ref in (own_ref, sib_ref):
        block = ref[...].astype(F32)
        total += jnp.sum(block, axis=0, keepdims=True)
        squared += jnp.sum(block * block, axis=0, keepdims=True)
    out_ref[...] = jnp.concatenate(
        [total, squared, jnp.zeros((6, own_ref.shape[1]), F32)], axis=0
    )


def group_sums(sums, width):
    lane = lax.broadcasted_iota(jnp.int32, sums.shape, 1)
    size = sums.shape[1]
    step = 1
    while step < width:
        low = pltpu.roll(sums, size - step, 1)
        high = pltpu.roll(sums, step, 1)
        sums = sums + jnp.where((lane & step) == 0, low, high)
        step *= 2
    return sums


def moments(sum_refs, cells):
    sums = sum_refs[0][...]
    for ref in sum_refs[1:]:
        sums = sums + ref[...]
    width = sums.shape[1] // GROUPS
    sums = group_sums(sums, width)
    population = cells * width
    mean = sums[0:1] / population
    var = sums[1:2] / population - mean * mean
    return mean, lax.rsqrt(var + 1e-06)


def normalise(block, mean, inverse, gain):
    return ((block.astype(F32) - mean) * inverse * gain).astype(BF)


def attend(queries, keys, values, state, exponent):
    scores = dot_t(queries, keys)
    peak = jnp.max(scores, axis=1, keepdims=True)
    if state is not None:
        old_peak, old_sum, old = state
        peak = jnp.maximum(peak, old_peak)
    unnormed = jnp.exp2((scores - peak) * exponent)
    total = jnp.sum(unnormed, axis=1, keepdims=True)
    mixed = dot(unnormed.astype(BF), values)
    if state is not None:
        fade = jnp.exp2((old_peak - peak) * exponent)
        total = total + old_sum * fade
        mixed = mixed + old * fade
    return peak, total, mixed


def save_state(state, peak_ref, sum_ref, mix_ref):
    peak, total, mixed = state
    peak_ref[...] = jnp.broadcast_to(peak, peak_ref.shape)
    sum_ref[...] = jnp.broadcast_to(total, sum_ref.shape)
    mix_ref[...] = mixed


def load_state(peak_ref, sum_ref, mix_ref):
    return peak_ref[:, 0:1], sum_ref[:, 0:1], mix_ref[...]


def early_body(
    cells_all, cols, exponent, n_sums,
    place_ref, own_ref, sib_ref, *refs,
):
    sum_refs, refs = refs[:n_sums], refs[n_sums:]
    gain_ref, refs = refs[0], refs[1:]
    hbm_refs, refs = refs[:6], refs[6:]
    norm_ref, q_ref, k_ref, v_ref, peak_ref, sum_ref, mix_ref, refs = *refs[:7], refs[7:]
    held_refs, sems = refs[:6], refs[6]
    copies = [
        pltpu.make_async_copy(source, target, sems.at[i])
        for i, (source, target) in enumerate(zip(hbm_refs, held_refs, strict=True))
    ]
    for copy in copies:
        copy.start()
    wq_ref, wk_ref, wv_ref = held_refs[:3]
    mean, inverse = moments(sum_refs, cells_all)
    gain = gain_ref[...]
    norm_ref[...] = jnp.concatenate(
        [mean, inverse, gain, jnp.zeros((5, mean.shape[1]), F32)], axis=0
    )
    cells = own_ref.shape[0]
    core = place_ref[0]
    own = normalise(own_ref[...], mean, inverse, gain)
    sib = normalise(sib_ref[...], mean, inverse, gain)
    near = pl.multiple_of(core * (cells - cols), 16)
    halo = normalise(sib_ref[pl.ds(near, cols), :], mean, inverse, gain)
    both = jnp.concatenate([own, sib], axis=0)
    copies[0].wait()
    q_ref[...] = dot(jnp.concatenate([own, halo], axis=0), wq_ref[...]).astype(BF)
    copies[1].wait()
    k_ref[...] = dot(both, wk_ref[...]).astype(BF)
    copies[2].wait()
    v_ref[...] = dot(both, wv_ref[...]).astype(BF)
    state = attend(q_ref[...], k_ref[...], v_ref[...], None, exponent)
    save_state(state, peak_ref, sum_ref, mix_ref)
    for copy in copies[3:]:
        copy.wait()


def normal_of(norm_ref):
    return norm_ref[0:1], norm_ref[1:2], norm_ref[2:3]


def keys_body(block_ref, norm_ref, wk_ref, wv_ref, kv_ref):
    cells = block_ref.shape[0]
    normed = normalise(block_ref[...], *normal_of(norm_ref))
    kv_ref[:cells] = dot(normed, wk_ref[...]).astype(BF)
    kv_ref[cells:] = dot(normed, wv_ref[...]).astype(BF)


def join_body(
    cols, exponent,
    place_ref, first_ref, last_ref, norm_ref, wq_ref, q_ref, k_ref, v_ref, peak_ref, sum_ref,
    mix_ref, kv_ref, all_q_ref, all_peak_ref, all_sum_ref, all_mix_ref,
):
    cells = first_ref.shape[0]
    core = place_ref[0]
    far = pl.multiple_of((1 - core) * (cells - cols), 16)
    block = jnp.where(core == 0, first_ref[pl.ds(far, cols), :], last_ref[pl.ds(far, cols), :])
    near = q_ref.shape[0]
    far_q = dot(normalise(block, *normal_of(norm_ref)), wq_ref[...]).astype(BF)
    all_q_ref[:near] = q_ref[...]
    all_q_ref[near:] = far_q
    far_state = attend(far_q, k_ref[...], v_ref[...], None, exponent)
    state = [
        jnp.concatenate([old, new], axis=0)
        for old, new in zip(load_state(peak_ref, sum_ref, mix_ref), far_state, strict=True)
    ]
    state = attend(all_q_ref[...], kv_ref[:cells], kv_ref[cells:], state, exponent)
    save_state(state, all_peak_ref, all_sum_ref, all_mix_ref)


def more_body(
    exponent, q_ref, peak_ref, sum_ref, mix_ref, kv_ref, new_peak_ref, new_sum_ref, new_mix_ref
):
    cells = kv_ref.shape[0] // 2
    state = load_state(peak_ref, sum_ref, mix_ref)
    state = attend(q_ref[...], kv_ref[:cells], kv_ref[cells:], state, exponent)
    save_state(state, new_peak_ref, new_sum_ref, new_mix_ref)


def spread(act, cols):
    size = act.shape[0]
    col = lax.broadcasted_iota(jnp.int32, act.shape, 0) % cols
    left = jnp.where(col == 0, 0.0, pltpu.roll(act, 1, 0))
    right = jnp.where(col == cols - 1, 0.0, pltpu.roll(act, size - 1, 0))
    return jnp.concatenate([left.astype(BF), act.astype(BF), right.astype(BF)], axis=1)


def conv(wide_ref, taps, out_cells, cols):
    total = None
    for row in range(3):
        term = dot(wide_ref[row * cols : row * cols + out_cells, :], taps(row))
        total = term if total is None else total + term
    return total


def late_body(
    cols, exponent,
    place_ref, own_ref, sib_ref, first_ref, last_ref, q_ref, peak_ref, sum_ref, mix_ref, kv_ref,
    wo_ref, taps_ref, part_ref, wide_ref, mid_ref,
):
    cells = own_ref.shape[0]
    core = place_ref[0]
    state = load_state(peak_ref, sum_ref, mix_ref)
    _, total, mixed = attend(q_ref[...], kv_ref[:cells], kv_ref[cells:], state, exponent)
    change = dot((mixed / total).astype(BF), wo_ref[...])
    near = pl.multiple_of(core * (cells - cols), 16)
    far = pl.multiple_of((1 - core) * (cells - cols), 16)
    far_block = jnp.where(core == 0, first_ref[pl.ds(far, cols), :], last_ref[pl.ds(far, cols), :])
    base = jnp.concatenate([own_ref[...], sib_ref[pl.ds(near, cols), :], far_block], axis=0)
    mid = (base.astype(F32) + change).astype(BF)
    mid_ref[...] = mid[:cells]
    act = jax.nn.silu(mid.astype(F32)).astype(BF).astype(F32)
    near_act = act[cells : cells + cols]
    far_act = jnp.where(place_ref[1] != 0, act[cells + cols :], 0.0)
    above = jnp.where(core == 0, far_act, near_act)
    below = jnp.where(core == 0, near_act, far_act)
    wide_ref[...] = spread(jnp.concatenate([above, act[:cells], below], axis=0), cols)
    first_tap = conv(wide_ref, lambda row: taps_ref[0, row], cells, cols)
    second_tap = conv(wide_ref, lambda row: taps_ref[1, row], cells, cols)
    part_ref[0] = (first_tap + second_tap).astype(BF)
    part_ref[1] = first_tap.astype(BF)


def now_body(cols, wide_ref, mid_ref, taps_ref, skip_ref, out_ref):
    cells = mid_ref.shape[0]
    skip = dot(mid_ref[...], skip_ref[...])
    second_tap = conv(wide_ref, lambda row: taps_ref[1, row], cells, cols)
    last_tap = conv(wide_ref, lambda row: taps_ref[2, row], cells, cols) + skip
    out_ref[0] = last_tap
    out_ref[1] = last_tap + second_tap


def per_device(
    features,
    norm_gain,
    query_weight,
    key_weight,
    value_weight,
    out_weight,
    conv_weight,
    skip_weight,
):
    _, tile_rows, cols, channels = features.shape
    out_channels = conv_weight.shape[-1]
    cells = tile_rows * cols
    devices = lax.axis_size("tile")
    chips = devices // 2
    me = lax.axis_index("tile")
    core = me % 2
    swap = [(i, i ^ 1) for i in range(devices)]
    own = features.reshape(cells, channels)

    def turned(array, by, flip):
        pairs = [(i, ((i + 2 * by) % devices) ^ flip) for i in range(devices)]
        return lax.ppermute(array, "tile", pairs)

    recv = [turned(own, by, 1) for by in range(1, chips)]
    sib = lax.ppermute(own, "tile", swap)
    sums = call(
        stats_body, jax.ShapeDtypeStruct((8, channels), F32), [], 1 << 22, own, sib
    )
    sums = [sums] + [turned(sums, by, 0) for by in range(1, chips)]

    gain = norm_gain.reshape(1, channels)
    exponent = channels ** (-0.5) * 1.4426950408889634
    outside = jnp.where(core == 0, me == 0, me == devices - 1)
    place = jnp.stack([core, 1 - outside.astype(jnp.int32)]).astype(jnp.int32)
    near = cells + cols
    every = near + cols
    taps = conv_weight.reshape(3, 3, 3 * channels, out_channels)
    weights = [query_weight, key_weight, value_weight, out_weight, taps, skip_weight]

    def state_shapes(rows):
        return [
            jax.ShapeDtypeStruct((rows, 128), F32),
            jax.ShapeDtypeStruct((rows, 128), F32),
            jax.ShapeDtypeStruct((rows, channels), F32),
        ]

    n_sums = len(sums)
    norm, q, k, v, *rest = call(
        functools.partial(early_body, devices * cells, cols, exponent, n_sums),
        [
            jax.ShapeDtypeStruct((8, channels), F32),
            jax.ShapeDtypeStruct((near, channels), BF),
            jax.ShapeDtypeStruct((2 * cells, channels), BF),
            jax.ShapeDtypeStruct((2 * cells, channels), BF),
            *state_shapes(near),
            *[jax.ShapeDtypeStruct(w.shape, w.dtype) for w in weights],
        ],
        [pltpu.SemaphoreType.DMA((len(weights),))],
        2 * 10**9,
        place, own, sib, *sums, gain, *[pltpu.with_memory_space_constraint(w, pltpu.HBM) for w in weights],
        spaces=[pltpu.SMEM] + [VMEM] * (3 + n_sums) + [pltpu.HBM] * len(weights),
    )
    state, (wq, wk, wv, wo, taps, ws) = rest[:3], rest[3:]

    kv = [
        call(
            keys_body, jax.ShapeDtypeStruct((2 * cells, channels), BF), [], 10**9,
            block, norm, wk, wv,
        )
        for block in recv
    ]
    rkv = [lax.ppermute(block, "tile", swap) for block in kv]
    q, *state = call(
        functools.partial(join_body, cols, exponent),
        [jax.ShapeDtypeStruct((every, channels), BF), *state_shapes(every)],
        [],
        2 * 10**9,
        place, recv[0], recv[-1], norm, wq, q, k, v, *state, kv[0],
        spaces=[pltpu.SMEM] + [VMEM] * 11,
    )
    for block in kv[1:] + rkv[:-1]:
        state = call(
            functools.partial(more_body, exponent), state_shapes(every), [], 10**9,
            q, *state, block,
        )
    part, wide, mid = call(
        functools.partial(late_body, cols, exponent),
        [
            jax.ShapeDtypeStruct((2, cells, out_channels), BF),
            jax.ShapeDtypeStruct((every, 3 * channels), BF),
            jax.ShapeDtypeStruct((cells, channels), BF),
        ],
        [],
        4 * 10**9,
        place, own, sib, recv[0], recv[-1], q, *state, rkv[-1], wo, taps,
        spaces=[pltpu.SMEM] + [VMEM] * 11,
    )
    spans = lax.axis_size("tm")
    arrived = lax.ppermute(part, "tm", [(i, i + 1) for i in range(spans - 1)])
    now = call(
        functools.partial(now_body, cols),
        jax.ShapeDtypeStruct((2, cells, out_channels), F32),
        [],
        2 * 10**9,
        wide, mid, taps, ws,
    )
    before = jnp.where(lax.axis_index("tm") == 0, part, arrived)
    decoded = (now + before.astype(F32)).astype(BF)
    return decoded.reshape(2, tile_rows, cols, out_channels)


def solution(mesh):
    in_specs = (P("tm", "tile", None, None), P(), P(), P(), P(), P(), P(), P())
    out_specs = P("tm", "tile", None, None)
    return jax.shard_map(
        per_device, mesh=mesh, in_specs=in_specs, out_specs=out_specs, check_vma=False
    )
```

```python
import functools

import jax
import jax.numpy as jnp
from jax import lax
from jax.experimental import pallas as pl
from jax.experimental.pallas import tpu as pltpu
from jax.sharding import PartitionSpec as P

GROUPS = 32
BF = jnp.bfloat16
F32 = jnp.float32
VMEM = pltpu.VMEM
LIMIT = 20 * 1024 * 1024
PIECES = 4


def dot(left, right):
    return jnp.dot(left, right, preferred_element_type=F32)


def dot_t(left, right):
    return lax.dot_general(left, right, (((1,), (1,)), ((), ())), preferred_element_type=F32)


def spec(space=VMEM):
    return pl.BlockSpec(memory_space=space)


def hbm(array):
    return pltpu.with_memory_space_constraint(array, pltpu.HBM)


def call(body, outs, scratch, cost, *args, spaces=None):
    spaces = spaces or [VMEM] * len(args)
    return pl.pallas_call(
        body,
        out_shape=outs,
        in_specs=[spec(s) for s in spaces],
        out_specs=jax.tree.map(lambda _: spec(), outs),
        scratch_shapes=scratch,
        compiler_params=pltpu.CompilerParams(vmem_limit_bytes=LIMIT),
        cost_estimate=pl.CostEstimate(flops=cost, bytes_accessed=1 << 20, transcendentals=0),
    )(*args)


def stats_body(features_ref, sums_ref, own_ref, sems):
    rows = own_ref.shape[0] // PIECES
    copies = []
    for i in range(PIECES):
        piece = pl.ds(i * rows, rows)
        copies.append(
            pltpu.make_async_copy(features_ref.at[piece], own_ref.at[piece], sems.at[i])
        )
        copies[-1].start()
    total = jnp.zeros((1, own_ref.shape[1]), F32)
    squared = total
    for i in range(PIECES):
        copies[i].wait()
        block = own_ref[i * rows : (i + 1) * rows].astype(F32)
        total += jnp.sum(block, axis=0, keepdims=True)
        squared += jnp.sum(block * block, axis=0, keepdims=True)
    sums_ref[...] = jnp.concatenate(
        [total, squared, jnp.zeros((6, own_ref.shape[1]), F32)], axis=0
    )


def group_sums(sums, width):
    lane = lax.broadcasted_iota(jnp.int32, sums.shape, 1)
    size = sums.shape[1]
    step = 1
    while step < width:
        low = pltpu.roll(sums, size - step, 1)
        high = pltpu.roll(sums, step, 1)
        sums = sums + jnp.where((lane & step) == 0, low, high)
        step *= 2
    return sums


def moments(sum_refs, cells):
    sums = 0.0
    for ref in sum_refs:
        for first in range(0, ref.shape[0], 8):
            sums = sums + ref[first : first + 8]
    width = sums.shape[1] // GROUPS
    sums = group_sums(sums, width)
    population = cells * width
    mean = sums[0:1] / population
    var = sums[1:2] / population - mean * mean
    return mean, lax.rsqrt(var + 1e-06)


def normalise(block, mean, inverse, gain):
    return ((block.astype(F32) - mean) * inverse * gain).astype(BF)


def attend(queries, keys, values, exponent, peak_ref, sum_ref, mix_ref):
    scores = dot_t(queries, keys)
    peak = jnp.max(scores, axis=1, keepdims=True)
    unnormed = jnp.exp2((scores - peak) * exponent)
    peak_ref[...] = jnp.broadcast_to(peak, peak_ref.shape)
    sum_ref[...] = jnp.broadcast_to(jnp.sum(unnormed, axis=1, keepdims=True), sum_ref.shape)
    mix_ref[...] = dot(unnormed.astype(BF), values)


def merge(old, new, out_refs, exponent, last):
    peak = jnp.maximum(old[0][...], new[0][...])
    fade_old = jnp.exp2((old[0][...] - peak) * exponent)
    fade_new = jnp.exp2((new[0][...] - peak) * exponent)
    total = old[1][...] * fade_old + new[1][...] * fade_new
    if last:
        scale = 1.0 / total
        fade_old = fade_old * scale
        fade_new = fade_new * scale
    else:
        out_refs[0][...] = peak
        out_refs[1][...] = total
    width = peak.shape[1]
    for first in range(0, old[2].shape[1], width):
        lanes = slice(first, first + width)
        mixed = old[2][:, lanes] * fade_old + new[2][:, lanes] * fade_new
        out_refs[-1][:, lanes] = mixed.astype(out_refs[-1].dtype)


def early_body(
    cells_all, cols, exponent, n_sums,
    place_ref, own_ref, sib_ref, *refs,
):
    sum_refs, refs = refs[:n_sums], refs[n_sums:]
    hbm_refs, refs = refs[:6], refs[6:]
    norm_ref, q_ref, k_ref, v_ref, *state_refs = refs[:7]
    held_refs, gain_ref, sems = refs[7:12], refs[12], refs[13]
    sources = (*hbm_refs[:5], hbm_refs[5].at[pl.ds(0, 2)])
    copies = [
        pltpu.make_async_copy(source, target, sems.at[i])
        for i, (source, target) in enumerate(zip(sources, (gain_ref, *held_refs), strict=True))
    ]
    for copy in copies[:4]:
        copy.start()
    wq_ref, wk_ref, wv_ref = held_refs[:3]
    mean, inverse = moments(sum_refs, cells_all)
    copies[0].wait()
    gain = gain_ref[...]
    norm_ref[...] = jnp.concatenate(
        [mean, inverse, gain, jnp.zeros((5, mean.shape[1]), F32)], axis=0
    )
    cells = own_ref.shape[0]
    core = place_ref[0]
    own = normalise(own_ref[...], mean, inverse, gain)
    sib = normalise(sib_ref[...], mean, inverse, gain)
    near = pl.multiple_of(core * (cells - cols), 16)
    halo = normalise(sib_ref[pl.ds(near, cols), :], mean, inverse, gain)
    both = jnp.concatenate([own, sib], axis=0)
    for copy in copies[1:4]:
        copy.wait()
    for copy in copies[4:]:
        copy.start()
    q_ref[...] = dot(jnp.concatenate([own, halo], axis=0), wq_ref[...]).astype(BF)
    k_ref[...] = dot(both, wk_ref[...]).astype(BF)
    v_ref[...] = dot(both, wv_ref[...]).astype(BF)
    attend(q_ref[...], k_ref[...], v_ref[...], exponent, *state_refs)
    for copy in copies[4:]:
        copy.wait()


def normal_of(norm_ref):
    return norm_ref[0:1], norm_ref[1:2], norm_ref[2:3]


def far_rows(place_ref, first_ref, last_ref, cols):
    core = place_ref[0]
    far = pl.multiple_of((1 - core) * (first_ref.shape[0] - cols), 16)
    first = first_ref[pl.ds(far, cols), :]
    if last_ref is None:
        return first
    return jnp.where(core == 0, first, last_ref[pl.ds(far, cols), :])


def project(block_ref, norm_ref, wk_ref, wv_ref, k_ref, v_ref):
    normed = normalise(block_ref[...], *normal_of(norm_ref))
    k_ref[...] = dot(normed, wk_ref[...]).astype(BF)
    v_ref[...] = dot(normed, wv_ref[...]).astype(BF)


def join_body(cols, exponent, single, place_ref, *refs):
    first_ref, refs = refs[0], refs[1:]
    last_ref, refs = (None, refs) if single else (refs[0], refs[1:])
    (norm_ref, wq_ref, wk_ref, wv_ref, q_ref, k_ref, v_ref, peak_ref, sum_ref, mix_ref,
     all_q_ref, all_peak_ref, all_sum_ref, all_mix_ref, new_k_ref, new_v_ref) = refs
    near = q_ref.shape[0]
    far_q = dot(
        normalise(far_rows(place_ref, first_ref, last_ref, cols), *normal_of(norm_ref)),
        wq_ref[...],
    ).astype(BF)
    project(first_ref, norm_ref, wk_ref, wv_ref, new_k_ref, new_v_ref)
    all_q_ref[:near] = q_ref[...]
    all_q_ref[near:] = far_q
    every = (all_peak_ref, all_sum_ref, all_mix_ref)
    for old, new in zip((peak_ref, sum_ref, mix_ref), every, strict=True):
        new[:near] = old[...]
    attend(
        far_q, k_ref[...], v_ref[...], exponent, *[ref.at[pl.ds(near, cols)] for ref in every]
    )


def more_body(exponent, block_ref, norm_ref, wk_ref, wv_ref, q_ref, *refs):
    old, out, new = refs[:3], refs[3:6], refs[6:9]
    k_ref, v_ref = refs[9:]
    project(block_ref, norm_ref, wk_ref, wv_ref, k_ref, v_ref)
    attend(q_ref[...], k_ref[...], v_ref[...], exponent, *new)
    merge(old, new, out, exponent, False)


def spread(act, cols):
    size = act.shape[0]
    col = lax.broadcasted_iota(jnp.int32, act.shape, 0) % cols
    left = jnp.where(col == 0, 0.0, pltpu.roll(act, 1, 0))
    right = jnp.where(col == cols - 1, 0.0, pltpu.roll(act, size - 1, 0))
    return jnp.concatenate([left.astype(BF), act.astype(BF), right.astype(BF)], axis=1)


def conv(wide_ref, taps, out_cells, cols):
    total = None
    for row in range(3):
        term = dot(wide_ref[row * cols : row * cols + out_cells, :], taps(row))
        total = term if total is None else total + term
    return total


def late_body(cols, exponent, single, place_ref, own_ref, sib_ref, *refs):
    first_ref, refs = refs[0], refs[1:]
    last_ref, refs = (None, refs) if single else (refs[0], refs[1:])
    (block_ref, norm_ref, q_ref, peak_ref, sum_ref, mix_ref, k_ref, v_ref, wk_ref, wv_ref, wo_ref,
     taps_ref, part_ref, wide_ref, mid_ref, keys_ref, values_ref, *new, attended_ref) = refs
    cells = own_ref.shape[0]
    core = place_ref[0]
    keys_ref[:cells] = k_ref[...]
    values_ref[:cells] = v_ref[...]
    rest = pl.ds(cells, cells)
    project(block_ref, norm_ref, wk_ref, wv_ref, keys_ref.at[rest], values_ref.at[rest])
    attend(q_ref[...], keys_ref[...], values_ref[...], exponent, *new)
    merge((peak_ref, sum_ref, mix_ref), new, (attended_ref,), exponent, True)
    change = dot(attended_ref[...], wo_ref[...])
    near = pl.multiple_of(core * (cells - cols), 16)
    far_block = far_rows(place_ref, first_ref, last_ref, cols)
    base = jnp.concatenate([own_ref[...], sib_ref[pl.ds(near, cols), :], far_block], axis=0)
    mid = (base.astype(F32) + change).astype(BF)
    mid_ref[...] = mid[:cells]
    act = jax.nn.silu(mid.astype(F32)).astype(BF).astype(F32)
    near_act = act[cells : cells + cols]
    far_act = jnp.where(place_ref[1] != 0, act[cells + cols :], 0.0)
    above = jnp.where(core == 0, far_act, near_act)
    below = jnp.where(core == 0, near_act, far_act)
    wide_ref[...] = spread(jnp.concatenate([above, act[:cells], below], axis=0), cols)
    first_tap = conv(wide_ref, lambda row: taps_ref[0, row], cells, cols)
    second_tap = conv(wide_ref, lambda row: taps_ref[1, row], cells, cols)
    part_ref[0] = (first_tap + second_tap).astype(BF)
    part_ref[1] = first_tap.astype(BF)


def now_body(cols, wide_ref, mid_ref, conv_ref, skip_ref, out_ref, taps_ref, skip_held_ref, sems):
    copies = [
        pltpu.make_async_copy(skip_ref, skip_held_ref, sems.at[0]),
        pltpu.make_async_copy(conv_ref.at[pl.ds(1, 2)], taps_ref, sems.at[1]),
    ]
    for copy in copies:
        copy.start()
    cells = mid_ref.shape[0]
    copies[0].wait()
    skip = dot(mid_ref[...], skip_held_ref[...])
    copies[1].wait()
    second_tap = conv(wide_ref, lambda row: taps_ref[0, row], cells, cols)
    last_tap = conv(wide_ref, lambda row: taps_ref[1, row], cells, cols) + skip
    out_ref[0] = last_tap
    out_ref[1] = last_tap + second_tap


def per_device(
    features,
    norm_gain,
    query_weight,
    key_weight,
    value_weight,
    out_weight,
    conv_weight,
    skip_weight,
):
    _, tile_rows, cols, channels = features.shape
    out_channels = conv_weight.shape[-1]
    cells = tile_rows * cols
    devices = lax.axis_size("tile")
    chips = devices // 2
    me = lax.axis_index("tile")
    core = me % 2
    swap = [(i, i ^ 1) for i in range(devices)]
    own = features.reshape(cells, channels)

    def turned(array, by, flip):
        pairs = [(i, ((i + 2 * by) % devices) ^ flip) for i in range(devices)]
        return lax.ppermute(array, "tile", pairs)

    sib = lax.ppermute(own, "tile", swap)
    sums, own = call(
        stats_body,
        [jax.ShapeDtypeStruct((8, channels), F32), jax.ShapeDtypeStruct(own.shape, BF)],
        [pltpu.SemaphoreType.DMA((PIECES,))],
        1 << 22,
        hbm(own),
        spaces=[pltpu.HBM],
    )
    sums = [sums] + [turned(sums, by, 1) for by in range(1, chips)]
    recv = [turned(own, by, 1) for by in range(1, chips)]
    sums = jnp.concatenate(sums, axis=0)
    sums = [sums, lax.ppermute(sums, "tile", swap)]

    exponent = channels ** (-0.5) * 1.4426950408889634
    outside = jnp.where(core == 0, me == 0, me == devices - 1)
    place = jnp.stack([core, 1 - outside.astype(jnp.int32)]).astype(jnp.int32)
    near = cells + cols
    every = near + cols
    taps = conv_weight.reshape(3, 3, 3 * channels, out_channels)
    weights = [norm_gain.reshape(1, channels), query_weight, key_weight, value_weight, out_weight]
    first_taps = (2, *taps.shape[1:])

    def rows_of(rows, kind=BF, width=channels):
        return jax.ShapeDtypeStruct((rows, width), kind)

    def state_of(rows):
        return [rows_of(rows, F32, 128), rows_of(rows, F32, 128), rows_of(rows, F32)]

    def scratch_of(shapes):
        return [VMEM(shape.shape, shape.dtype) for shape in shapes]

    n_sums = len(sums)
    norm, q, k, v, *rest = call(
        functools.partial(early_body, devices * cells, cols, exponent, n_sums),
        [
            rows_of(8, F32),
            rows_of(near),
            rows_of(2 * cells),
            rows_of(2 * cells),
            *state_of(near),
            *[jax.ShapeDtypeStruct(w.shape, w.dtype) for w in weights[1:]],
            jax.ShapeDtypeStruct(first_taps, BF),
        ],
        [VMEM((1, channels), F32), pltpu.SemaphoreType.DMA((len(weights) + 1,))],
        2 * 10**9,
        place, own, sib, *sums, *[hbm(w) for w in weights], hbm(taps),
        spaces=[pltpu.SMEM] + [VMEM] * (2 + n_sums) + [pltpu.HBM] * (len(weights) + 1),
    )
    state, (wq, wk, wv, wo, held_taps) = rest[:3], rest[3:]

    *recv, norm = lax.optimization_barrier((*recv, norm))
    rsib = [lax.ppermute(block, "tile", swap) for block in recv]
    ends = recv[:1] if chips == 2 else [recv[0], recv[-1]]
    q, *state, new_k, new_v = call(
        functools.partial(join_body, cols, exponent, chips == 2),
        [rows_of(every), *state_of(every), rows_of(cells), rows_of(cells)],
        [],
        2 * 10**9,
        place, *ends, norm, wq, wk, wv, q, k, v, *state,
        spaces=[pltpu.SMEM] + [VMEM] * (10 + len(ends)),
    )
    for block in recv[1:] + rsib[:-1]:
        state = call(
            functools.partial(more_body, exponent),
            state_of(every),
            scratch_of([*state_of(every), rows_of(cells), rows_of(cells)]),
            10**9,
            block, norm, wk, wv, q, *state,
        )
    part, wide, mid = call(
        functools.partial(late_body, cols, exponent, chips == 2),
        [
            jax.ShapeDtypeStruct((2, cells, out_channels), BF),
            rows_of(every, BF, 3 * channels),
            rows_of(cells),
        ],
        scratch_of([rows_of(2 * cells), rows_of(2 * cells), *state_of(every), rows_of(every)]),
        4 * 10**9,
        place, own, sib, *ends, rsib[-1], norm, q, *state, new_k, new_v, wk, wv, wo, held_taps,
        spaces=[pltpu.SMEM] + [VMEM] * (14 + len(ends)),
    )
    spans = lax.axis_size("tm")
    arrived = lax.ppermute(part, "tm", [(i, i + 1) for i in range(spans - 1)])
    now = call(
        functools.partial(now_body, cols),
        jax.ShapeDtypeStruct((2, cells, out_channels), F32),
        [VMEM(first_taps, BF), VMEM(skip_weight.shape, BF), pltpu.SemaphoreType.DMA((2,))],
        2 * 10**9,
        wide, mid, hbm(taps), hbm(skip_weight),
        spaces=[VMEM, VMEM, pltpu.HBM, pltpu.HBM],
    )
    before = jnp.where(lax.axis_index("tm") == 0, part, arrived)
    decoded = (now + before.astype(F32)).astype(BF)
    return decoded.reshape(2, tile_rows, cols, out_channels)


def solution(mesh):
    in_specs = (P("tm", "tile", None, None), P(), P(), P(), P(), P(), P(), P())
    out_specs = P("tm", "tile", None, None)
    return jax.shard_map(
        per_device, mesh=mesh, in_specs=in_specs, out_specs=out_specs, check_vma=False
    )
```

```python
import functools

import jax
import jax.numpy as jnp
from jax import lax
from jax.experimental import pallas as pl
from jax.experimental.pallas import tpu as pltpu
from jax.sharding import PartitionSpec as P

GROUPS = 32
BF = jnp.bfloat16
F32 = jnp.float32
VMEM = pltpu.VMEM
LIMIT = 20 * 1024 * 1024
SHARE = 1 << 16
PAD = 16


def dot(left, right):
    return jnp.dot(left, right, preferred_element_type=F32)


def dot_t(left, right):
    return lax.dot_general(left, right, (((1,), (1,)), ((), ())), preferred_element_type=F32)


def spec(space=VMEM):
    return pl.BlockSpec(memory_space=space)


def hbm(array):
    return pltpu.with_memory_space_constraint(array, pltpu.HBM)


def call(body, outs, scratch, cost, *args, spaces=None):
    spaces = spaces or [VMEM] * len(args)
    return pl.pallas_call(
        body,
        out_shape=outs,
        in_specs=[spec(s) for s in spaces],
        out_specs=jax.tree.map(lambda _: spec(), outs),
        scratch_shapes=scratch,
        compiler_params=pltpu.CompilerParams(vmem_limit_bytes=LIMIT),
        cost_estimate=pl.CostEstimate(flops=cost // SHARE, bytes_accessed=1 << 10, transcendentals=0),
    )(*args)


def stats_body(cols, place_ref, features_ref, sums_ref, own_ref, edge_ref, rest_ref, sems):
    cells = own_ref.shape[0]
    core = place_ref[0]
    edge = pl.multiple_of(core * (cells - cols), 16)
    rest = pl.multiple_of((1 - core) * cols, 16)
    parts = [
        (features_ref.at[pl.ds(edge, cols)], edge_ref),
        (features_ref.at[pl.ds(rest, cells - cols)], rest_ref.at[pl.ds(0, cells - cols)]),
        (features_ref, own_ref),
    ]
    copies = [pltpu.make_async_copy(*part, sems.at[i]) for i, part in enumerate(parts)]
    for copy in copies:
        copy.start()
    total = jnp.zeros((1, own_ref.shape[1]), F32)
    squared = total
    rest_ref[cells - cols :] = jnp.zeros((PAD, own_ref.shape[1]), BF)
    for copy, (_, ref) in zip(copies[:2], parts[:2], strict=True):
        copy.wait()
        block = ref[...].astype(F32)
        total += jnp.sum(block, axis=0, keepdims=True)
        squared += jnp.sum(block * block, axis=0, keepdims=True)
    sums_ref[...] = jnp.concatenate(
        [total, squared, jnp.zeros((6, own_ref.shape[1]), F32)], axis=0
    )
    copies[2].wait()


def group_sums(sums, width):
    lane = lax.broadcasted_iota(jnp.int32, sums.shape, 1)
    size = sums.shape[1]
    step = 1
    while step < width:
        low = pltpu.roll(sums, size - step, 1)
        high = pltpu.roll(sums, step, 1)
        sums = sums + jnp.where((lane & step) == 0, low, high)
        step *= 2
    return sums


def moments(sum_refs, cells):
    sums = 0.0
    for ref in sum_refs:
        for first in range(0, ref.shape[0], 8):
            sums = sums + ref[first : first + 8]
    width = sums.shape[1] // GROUPS
    sums = group_sums(sums, width)
    population = cells * width
    mean = sums[0:1] / population
    var = sums[1:2] / population - mean * mean
    return mean, lax.rsqrt(var + 1e-06)


def normalise(block, mean, inverse, gain):
    return ((block.astype(F32) - mean) * inverse * gain).astype(BF)


def attend(queries, keys, values, exponent, peak_ref, sum_ref, mix_ref):
    scores = dot_t(queries, keys)
    peak = jnp.max(scores, axis=1, keepdims=True)
    unnormed = jnp.exp2((scores - peak) * exponent)
    peak_ref[...] = jnp.broadcast_to(peak, peak_ref.shape)
    sum_ref[...] = jnp.broadcast_to(jnp.sum(unnormed, axis=1, keepdims=True), sum_ref.shape)
    mix_ref[...] = dot(unnormed.astype(BF), values)


def merge(old, new, out_refs, exponent, last):
    peak = jnp.maximum(old[0][...], new[0][...])
    fade_old = jnp.exp2((old[0][...] - peak) * exponent)
    fade_new = jnp.exp2((new[0][...] - peak) * exponent)
    total = old[1][...] * fade_old + new[1][...] * fade_new
    if last:
        scale = 1.0 / total
        fade_old = fade_old * scale
        fade_new = fade_new * scale
    else:
        out_refs[0][...] = peak
        out_refs[1][...] = total
    width = peak.shape[1]
    for first in range(0, old[2].shape[1], width):
        lanes = slice(first, first + width)
        mixed = old[2][:, lanes] * fade_old + new[2][:, lanes] * fade_new
        out_refs[-1][:, lanes] = mixed.astype(out_refs[-1].dtype)


def early_body(
    cells_all, cols, exponent, n_sums,
    place_ref, own_ref, sib_ref, *refs,
):
    sum_refs, refs = refs[:n_sums], refs[n_sums:]
    hbm_refs, refs = refs[:6], refs[6:]
    norm_ref, q_ref, k_ref, v_ref, *state_refs = refs[:7]
    held_refs, gain_ref, sems = refs[7:12], refs[12], refs[13]
    sources = (*hbm_refs[:5], hbm_refs[5].at[pl.ds(0, 2)])
    copies = [
        pltpu.make_async_copy(source, target, sems.at[i])
        for i, (source, target) in enumerate(zip(sources, (gain_ref, *held_refs), strict=True))
    ]
    for copy in copies[:4]:
        copy.start()
    wq_ref, wk_ref, wv_ref = held_refs[:3]
    mean, inverse = moments(sum_refs, cells_all)
    copies[0].wait()
    gain = gain_ref[...]
    norm_ref[...] = jnp.concatenate(
        [mean, inverse, gain, jnp.zeros((5, mean.shape[1]), F32)], axis=0
    )
    cells = own_ref.shape[0]
    core = place_ref[0]
    own = normalise(own_ref[...], mean, inverse, gain)
    sib = normalise(sib_ref[...], mean, inverse, gain)
    near = pl.multiple_of(core * (cells - cols), 16)
    halo = normalise(sib_ref[pl.ds(near, cols), :], mean, inverse, gain)
    both = jnp.concatenate([own, sib], axis=0)
    for copy in copies[1:4]:
        copy.wait()
    for copy in copies[4:]:
        copy.start()
    q_ref[...] = dot(jnp.concatenate([own, halo], axis=0), wq_ref[...]).astype(BF)
    k_ref[...] = dot(both, wk_ref[...]).astype(BF)
    v_ref[...] = dot(both, wv_ref[...]).astype(BF)
    attend(q_ref[...], k_ref[...], v_ref[...], exponent, *state_refs)
    for copy in copies[4:]:
        copy.wait()


def normal_of(norm_ref):
    return norm_ref[0:1], norm_ref[1:2], norm_ref[2:3]


def project(blocks, norm_ref, wk_ref, wv_ref, k_ref, v_ref):
    block = jnp.concatenate([block[...] for block in blocks], axis=0)
    normed = normalise(block, *normal_of(norm_ref))
    k_ref[...] = dot(normed, wk_ref[...]).astype(BF)
    v_ref[...] = dot(normed, wv_ref[...]).astype(BF)


def keys_body(block_ref, norm_ref, wk_ref, wv_ref, k_ref, v_ref):
    project([block_ref.at[pl.ds(0, k_ref.shape[0])]], norm_ref, wk_ref, wv_ref, k_ref, v_ref)


def join_body(exponent, single, place_ref, recv_ref, rsib_ref, *refs):
    last_ref, refs = (rsib_ref, refs) if single else (refs[0], refs[1:])
    (norm_ref, wq_ref, wk_ref, wv_ref, q_ref, k_ref, v_ref, peak_ref, sum_ref, mix_ref,
     far_ref, all_q_ref, *refs) = refs
    out, every, new, (new_k_ref, new_v_ref) = refs[:3], refs[3:6], refs[6:9], refs[9:]
    near = q_ref.shape[0]
    far = rsib_ref[...]
    if not single:
        far = jnp.where(place_ref[0] == 0, far, last_ref[...])
    far_ref[...] = far
    far_q = dot(normalise(far, *normal_of(norm_ref)), wq_ref[...]).astype(BF)
    project([recv_ref, rsib_ref], norm_ref, wk_ref, wv_ref, new_k_ref, new_v_ref)
    all_q_ref[:near] = q_ref[...]
    all_q_ref[near:] = far_q
    for old_ref, every_ref in zip((peak_ref, sum_ref, mix_ref), every, strict=True):
        every_ref[:near] = old_ref[...]
    tail = pl.ds(near, far.shape[0])
    attend(far_q, k_ref[...], v_ref[...], exponent, *[ref.at[tail] for ref in every])
    attend(all_q_ref[...], new_k_ref[...], new_v_ref[...], exponent, *new)
    merge(every, new, out, exponent, False)


def more_body(exponent, recv_ref, rsib_ref, norm_ref, wk_ref, wv_ref, q_ref, *refs):
    old, out, new = refs[:3], refs[3:6], refs[6:9]
    k_ref, v_ref = refs[9:]
    blocks = [ref.at[pl.ds(0, k_ref.shape[0] // 2)] for ref in (recv_ref, rsib_ref)]
    project(blocks, norm_ref, wk_ref, wv_ref, k_ref, v_ref)
    attend(q_ref[...], k_ref[...], v_ref[...], exponent, *new)
    merge(old, new, out, exponent, False)


def spread(act, cols):
    size = act.shape[0]
    col = lax.broadcasted_iota(jnp.int32, act.shape, 0) % cols
    left = jnp.where(col == 0, 0.0, pltpu.roll(act, 1, 0))
    right = jnp.where(col == cols - 1, 0.0, pltpu.roll(act, size - 1, 0))
    return jnp.concatenate([left.astype(BF), act.astype(BF), right.astype(BF)], axis=1)


def conv(wide_ref, taps, out_cells, cols):
    total = None
    for row in range(3):
        term = dot(wide_ref[row * cols : row * cols + out_cells, :], taps(row))
        total = term if total is None else total + term
    return total


def late_body(
    cols, exponent,
    place_ref, own_ref, sib_ref, far_ref, block_ref, norm_ref, q_ref, peak_ref, sum_ref, mix_ref,
    k_ref, v_ref, wk_ref, wv_ref, wo_ref, taps_ref,
    odd_ref, first_ref, wide_ref, mid_ref,
    keys_ref, values_ref, new_peak_ref, new_sum_ref, new_mix_ref, attended_ref,
):
    cells = own_ref.shape[0]
    core = place_ref[0]
    half = k_ref.shape[0]
    keys_ref[:half] = k_ref[...]
    values_ref[:half] = v_ref[...]
    rest = pl.ds(half, half)
    block = block_ref.at[pl.ds(0, half)]
    project([block], norm_ref, wk_ref, wv_ref, keys_ref.at[rest], values_ref.at[rest])
    new = (new_peak_ref, new_sum_ref, new_mix_ref)
    attend(q_ref[...], keys_ref[...], values_ref[...], exponent, *new)
    merge((peak_ref, sum_ref, mix_ref), new, (attended_ref,), exponent, True)
    change = dot(attended_ref[...], wo_ref[...])
    near = pl.multiple_of(core * (cells - cols), 16)
    base = jnp.concatenate([own_ref[...], sib_ref[pl.ds(near, cols), :], far_ref[...]], axis=0)
    mid = (base.astype(F32) + change).astype(BF)
    mid_ref[...] = mid[:cells]
    act = jax.nn.silu(mid.astype(F32)).astype(BF).astype(F32)
    near_act = act[cells : cells + cols]
    far_act = jnp.where(place_ref[1] != 0, act[cells + cols :], 0.0)
    above = jnp.where(core == 0, far_act, near_act)
    below = jnp.where(core == 0, near_act, far_act)
    wide_ref[...] = spread(jnp.concatenate([above, act[:cells], below], axis=0), cols)
    first_tap = conv(wide_ref, lambda row: taps_ref[0, row], cells, cols)
    odd_ref[:cells] = first_tap.astype(BF)
    odd_ref[cells:] = jnp.zeros((PAD, odd_ref.shape[1]), BF)
    first_ref[...] = first_tap


def even_body(cols, wide_ref, first_ref, taps_ref, even_ref):
    cells = first_ref.shape[0]
    second_tap = conv(wide_ref, lambda row: taps_ref[1, row], cells, cols)
    even_ref[...] = (first_ref[...] + second_tap).astype(BF)


def now_body(cols, wide_ref, mid_ref, conv_ref, skip_ref, out_ref, taps_ref, skip_held_ref, sems):
    copies = [
        pltpu.make_async_copy(skip_ref, skip_held_ref, sems.at[0]),
        pltpu.make_async_copy(conv_ref.at[pl.ds(1, 2)], taps_ref, sems.at[1]),
    ]
    for copy in copies:
        copy.start()
    cells = mid_ref.shape[0]
    copies[0].wait()
    skip = dot(mid_ref[...], skip_held_ref[...])
    copies[1].wait()
    second_tap = conv(wide_ref, lambda row: taps_ref[0, row], cells, cols)
    last_tap = conv(wide_ref, lambda row: taps_ref[1, row], cells, cols) + skip
    out_ref[0] = last_tap
    out_ref[1] = last_tap + second_tap


def last_body(which, place_ref, now_ref, own_ref, arrived_ref, *refs):
    out_ref, sum_ref, sem = refs[-3:]
    cells = sum_ref.shape[0]
    before = jnp.where(place_ref[2] != 0, own_ref[:cells], arrived_ref[:cells])
    sum_ref[...] = (now_ref[which] + before.astype(F32)).astype(BF)
    copy = pltpu.make_async_copy(sum_ref, out_ref.at[which], sem)
    copy.start()
    copy.wait()


def per_device(
    features,
    norm_gain,
    query_weight,
    key_weight,
    value_weight,
    out_weight,
    conv_weight,
    skip_weight,
):
    _, tile_rows, cols, channels = features.shape
    out_channels = conv_weight.shape[-1]
    cells = tile_rows * cols
    devices = lax.axis_size("tile")
    chips = devices // 2
    me = lax.axis_index("tile")
    core = me % 2
    own = features.reshape(cells, channels)

    def turned(array, by):
        return lax.ppermute(array, "tile", [(i, (i + 2 * by) % devices) for i in range(devices)])

    def swapped(array):
        return lax.ppermute(array, "tile", [(i, i ^ 1) for i in range(devices)])

    def rows_of(rows, kind=BF, width=channels):
        return jax.ShapeDtypeStruct((rows, width), kind)

    def state_of(rows):
        return [rows_of(rows, F32, 128), rows_of(rows, F32, 128), rows_of(rows, F32)]

    def scratch_of(shapes):
        return [VMEM(shape.shape, shape.dtype) for shape in shapes]

    outside = jnp.where(core == 0, me == 0, me == devices - 1)
    first_span = lax.axis_index("tm") == 0
    place = jnp.stack([core, 1 - outside.astype(jnp.int32), first_span.astype(jnp.int32)])
    place = place.astype(jnp.int32)
    sib = swapped(own)
    sums, own, edge, rest = call(
        functools.partial(stats_body, cols),
        [rows_of(8, F32), rows_of(cells), rows_of(cols), rows_of(cells - cols + PAD)],
        [pltpu.SemaphoreType.DMA((3,))],
        1 << 22,
        place, hbm(own),
        spaces=[pltpu.SMEM, pltpu.HBM],
    )
    shifts = range(1, chips)
    sums = jnp.concatenate([sums] + [turned(sums, by) for by in shifts], axis=0)
    recv_edge = [turned(edge, by) for by in shifts]
    recv_rest = [turned(rest, by) for by in shifts]
    sums = [sums, swapped(sums)]

    exponent = channels ** (-0.5) * 1.4426950408889634
    near = cells + cols
    every = near + cols
    taps = conv_weight.reshape(3, 3, 3 * channels, out_channels)
    weights = [norm_gain.reshape(1, channels), query_weight, key_weight, value_weight, out_weight]
    first_taps = (2, *taps.shape[1:])

    n_sums = len(sums)
    norm, q, k, v, *rest = call(
        functools.partial(early_body, devices * cells, cols, exponent, n_sums),
        [
            rows_of(8, F32),
            rows_of(near),
            rows_of(2 * cells),
            rows_of(2 * cells),
            *state_of(near),
            *[jax.ShapeDtypeStruct(w.shape, w.dtype) for w in weights[1:]],
            jax.ShapeDtypeStruct(first_taps, BF),
        ],
        [VMEM((1, channels), F32), pltpu.SemaphoreType.DMA((len(weights) + 1,))],
        2 * 10**9,
        place, own, sib, *sums, *[hbm(w) for w in weights], hbm(taps),
        spaces=[pltpu.SMEM] + [VMEM] * (2 + n_sums) + [pltpu.HBM] * (len(weights) + 1),
    )
    state, (wq, wk, wv, wo, held_taps) = rest[:3], rest[3:]

    *recv_edge, norm = lax.optimization_barrier((*recv_edge, norm))
    rsib_edge = [swapped(block) for block in recv_edge]
    ends = rsib_edge[:1] if chips == 2 else [rsib_edge[0], rsib_edge[-1]]
    far, q, *state = call(
        functools.partial(join_body, exponent, chips == 2),
        [rows_of(cols), rows_of(every), *state_of(every)],
        scratch_of([*state_of(every), *state_of(every), rows_of(2 * cols), rows_of(2 * cols)]),
        2 * 10**9,
        place, recv_edge[0], *ends, norm, wq, wk, wv, q, k, v, *state,
        spaces=[pltpu.SMEM] + [VMEM] * (11 + len(ends)),
    )
    *recv_rest, state[0] = lax.optimization_barrier((*recv_rest, state[0]))
    rsib_rest = [swapped(block) for block in recv_rest]
    pairs = [*zip(recv_edge, rsib_edge, strict=True)][1:]
    pairs += [*zip(recv_rest, rsib_rest, strict=True)][:-1]
    for pair in pairs:
        held = rows_of(2 * (pair[0].shape[0] // cols * cols))
        state = call(
            functools.partial(more_body, exponent),
            state_of(every),
            scratch_of([*state_of(every), held, held]),
            10**9,
            *pair, norm, wk, wv, q, *state,
        )
    last = rows_of(cells - cols)
    last_k, last_v = call(keys_body, [last, last], [], 10**8, recv_rest[-1], norm, wk, wv)
    both = rows_of(2 * (cells - cols))
    odd, first, wide, mid = call(
        functools.partial(late_body, cols, exponent),
        [
            rows_of(cells + PAD, BF, out_channels),
            rows_of(cells, F32, out_channels),
            rows_of(every, BF, 3 * channels),
            rows_of(cells),
        ],
        scratch_of([both, both, *state_of(every), rows_of(every)]),
        4 * 10**9,
        place, own, sib, far, rsib_rest[-1], norm, q, *state, last_k, last_v, wk, wv, wo,
        held_taps,
        spaces=[pltpu.SMEM] + [VMEM] * 15,
    )
    spans = lax.axis_size("tm")
    arrived_odd = lax.ppermute(odd, "tm", [(i, (i + 1) % spans) for i in range(spans)])
    even = call(
        functools.partial(even_body, cols), rows_of(cells, BF, out_channels), [], 8 * 10**8,
        wide, first, held_taps,
    )
    arrived_even = lax.ppermute(even, "tm", [(i, i + 1) for i in range(spans - 1)])
    now = call(
        functools.partial(now_body, cols),
        jax.ShapeDtypeStruct((2, cells, out_channels), F32),
        [VMEM(first_taps, BF), VMEM(skip_weight.shape, BF), pltpu.SemaphoreType.DMA((2,))],
        2 * 10**9,
        wide, mid, hbm(taps), hbm(skip_weight),
        spaces=[VMEM, VMEM, pltpu.HBM, pltpu.HBM],
    )
    result = jax.ShapeDtypeStruct((2, cells, out_channels), BF)
    decoded = None
    for which, own_part, arrived in ((1, odd, arrived_odd), (0, even, arrived_even)):
        operands = [place, now, own_part, arrived]
        decoded = pl.pallas_call(
            functools.partial(last_body, which),
            out_shape=result,
            in_specs=[spec(pltpu.SMEM)] + [spec()] * 3 + [spec(pl.ANY)] * (decoded is not None),
            out_specs=spec(pl.ANY),
            input_output_aliases={} if decoded is None else {4: 0},
            scratch_shapes=[VMEM((cells, out_channels), BF), pltpu.SemaphoreType.DMA],
            compiler_params=pltpu.CompilerParams(vmem_limit_bytes=LIMIT),
            cost_estimate=pl.CostEstimate(flops=1, bytes_accessed=1 << 10, transcendentals=0),
        )(*operands, *([] if decoded is None else [decoded]))
    return decoded.reshape(2, tile_rows, cols, out_channels)


def solution(mesh):
    in_specs = (P("tm", "tile", None, None), P(), P(), P(), P(), P(), P(), P())
    out_specs = P("tm", "tile", None, None)
    return jax.shard_map(
        per_device, mesh=mesh, in_specs=in_specs, out_specs=out_specs, check_vma=False
    )
```

```python
import functools

import jax
import jax.numpy as jnp
from jax import lax
from jax.experimental import pallas as pl
from jax.experimental.pallas import tpu as pltpu
from jax.sharding import PartitionSpec as P

GROUPS = 32
BF = jnp.bfloat16
F32 = jnp.float32
VMEM = pltpu.VMEM
LIMIT = 12 * 1024 * 1024
PIECES = 4
PAD = 16
SHARE = 1 << 16


def dot(left, right):
    return jnp.dot(left, right, preferred_element_type=F32)


def dot_t(left, right):
    return lax.dot_general(left, right, (((1,), (1,)), ((), ())), preferred_element_type=F32)


def spec(space=VMEM):
    return pl.BlockSpec(memory_space=space)


def hbm(array):
    return pltpu.with_memory_space_constraint(array, pltpu.HBM)


def call(body, outs, scratch, cost, *args, spaces=None):
    spaces = spaces or [VMEM] * len(args)
    return pl.pallas_call(
        body,
        out_shape=outs,
        in_specs=[spec(s) for s in spaces],
        out_specs=jax.tree.map(lambda _: spec(), outs),
        scratch_shapes=scratch,
        compiler_params=pltpu.CompilerParams(vmem_limit_bytes=LIMIT),
        cost_estimate=pl.CostEstimate(flops=cost // SHARE, bytes_accessed=1 << 10, transcendentals=0),
    )(*args)


def stats_body(features_ref, sums_ref, own_ref, sems):
    rows = own_ref.shape[0] // PIECES
    copies = []
    for i in range(PIECES):
        piece = pl.ds(i * rows, rows)
        copies.append(
            pltpu.make_async_copy(features_ref.at[piece], own_ref.at[piece], sems.at[i])
        )
        copies[-1].start()
    total = jnp.zeros((1, own_ref.shape[1]), F32)
    squared = total
    for i in range(PIECES):
        copies[i].wait()
        block = own_ref[i * rows : (i + 1) * rows].astype(F32)
        total += jnp.sum(block, axis=0, keepdims=True)
        squared += jnp.sum(block * block, axis=0, keepdims=True)
    sums_ref[...] = jnp.concatenate(
        [total, squared, jnp.zeros((6, own_ref.shape[1]), F32)], axis=0
    )


def group_sums(sums, width):
    lane = lax.broadcasted_iota(jnp.int32, sums.shape, 1)
    size = sums.shape[1]
    step = 1
    while step < width:
        low = pltpu.roll(sums, size - step, 1)
        high = pltpu.roll(sums, step, 1)
        sums = sums + jnp.where((lane & step) == 0, low, high)
        step *= 2
    return sums


def moments(sum_refs, cells):
    sums = 0.0
    for ref in sum_refs:
        for first in range(0, ref.shape[0], 8):
            sums = sums + ref[first : first + 8]
    width = sums.shape[1] // GROUPS
    sums = group_sums(sums, width)
    population = cells * width
    mean = sums[0:1] / population
    var = sums[1:2] / population - mean * mean
    return mean, lax.rsqrt(var + 1e-06)


def normalise(block, mean, inverse, gain):
    return ((block.astype(F32) - mean) * inverse * gain).astype(BF)


def attend(queries, keys, values, exponent, peak_ref, sum_ref, mix_ref):
    scores = dot_t(queries, keys)
    peak = jnp.max(scores, axis=1, keepdims=True)
    unnormed = jnp.exp2((scores - peak) * exponent)
    peak_ref[...] = jnp.broadcast_to(peak, peak_ref.shape)
    sum_ref[...] = jnp.broadcast_to(jnp.sum(unnormed, axis=1, keepdims=True), sum_ref.shape)
    mix_ref[...] = dot(unnormed.astype(BF), values)


def merge(old, new, out_refs, exponent, last):
    peak = jnp.maximum(old[0][...], new[0][...])
    fade_old = jnp.exp2((old[0][...] - peak) * exponent)
    fade_new = jnp.exp2((new[0][...] - peak) * exponent)
    total = old[1][...] * fade_old + new[1][...] * fade_new
    if last:
        scale = 1.0 / total
        fade_old = fade_old * scale
        fade_new = fade_new * scale
    else:
        out_refs[0][...] = peak
        out_refs[1][...] = total
    width = peak.shape[1]
    for first in range(0, old[2].shape[1], width):
        lanes = slice(first, first + width)
        mixed = old[2][:, lanes] * fade_old + new[2][:, lanes] * fade_new
        out_refs[-1][:, lanes] = mixed.astype(out_refs[-1].dtype)


def stage_body(*refs):
    refs, sems = refs[1:-1], refs[-1]
    count = len(refs) // 2
    copies = [
        pltpu.make_async_copy(refs[i], refs[count + i], sems.at[i]) for i in range(count)
    ]
    for copy in copies:
        copy.start()
    for copy in copies:
        copy.wait()


def early_body(
    cells_all, cols, exponent, n_sums,
    place_ref, own_ref, sib_ref, *refs,
):
    sum_refs, refs = refs[:n_sums], refs[n_sums:]
    gain_ref, wq_ref, wk_ref, wv_ref, wo_hbm_ref, taps_hbm_ref, refs = *refs[:6], refs[6:]
    norm_ref, q_ref, k_ref, v_ref, *state_refs = refs[:7]
    wo_ref, taps_ref, sems = refs[7:]
    copies = [
        pltpu.make_async_copy(wo_hbm_ref, wo_ref, sems.at[0]),
        pltpu.make_async_copy(taps_hbm_ref, taps_ref, sems.at[1]),
    ]
    for copy in copies:
        copy.start()
    mean, inverse = moments(sum_refs, cells_all)
    gain = gain_ref[...]
    norm_ref[...] = jnp.concatenate(
        [mean, inverse, gain, jnp.zeros((5, mean.shape[1]), F32)], axis=0
    )
    cells = own_ref.shape[0]
    core = place_ref[0]
    own = normalise(own_ref[...], mean, inverse, gain)
    sib = normalise(sib_ref[...], mean, inverse, gain)
    near = pl.multiple_of(core * (cells - cols), 16)
    halo = normalise(sib_ref[pl.ds(near, cols), :], mean, inverse, gain)
    both = jnp.concatenate([own, sib], axis=0)
    q_ref[...] = dot(jnp.concatenate([own, halo], axis=0), wq_ref[...]).astype(BF)
    k_ref[...] = dot(both, wk_ref[...]).astype(BF)
    v_ref[...] = dot(both, wv_ref[...]).astype(BF)
    attend(q_ref[...], k_ref[...], v_ref[...], exponent, *state_refs)
    for copy in copies:
        copy.wait()


def normal_of(norm_ref):
    return norm_ref[0:1], norm_ref[1:2], norm_ref[2:3]


def far_rows(place_ref, first_ref, last_ref, cols):
    core = place_ref[0]
    far = pl.multiple_of((1 - core) * (first_ref.shape[0] - cols), 16)
    first = first_ref[pl.ds(far, cols), :]
    if last_ref is None:
        return first
    return jnp.where(core == 0, first, last_ref[pl.ds(far, cols), :])


def project(block_ref, norm_ref, wk_ref, wv_ref, k_ref, v_ref):
    normed = normalise(block_ref[...], *normal_of(norm_ref))
    k_ref[...] = dot(normed, wk_ref[...]).astype(BF)
    v_ref[...] = dot(normed, wv_ref[...]).astype(BF)


def join_body(cols, exponent, single, place_ref, *refs):
    first_ref, refs = refs[0], refs[1:]
    last_ref, refs = (None, refs) if single else (refs[0], refs[1:])
    (norm_ref, wq_ref, wk_ref, wv_ref, q_ref, k_ref, v_ref, peak_ref, sum_ref, mix_ref,
     far_ref, all_q_ref, all_peak_ref, all_sum_ref, all_mix_ref, new_k_ref, new_v_ref) = refs
    near = q_ref.shape[0]
    far = far_rows(place_ref, first_ref, last_ref, cols)
    far_ref[...] = far
    far_q = dot(normalise(far, *normal_of(norm_ref)), wq_ref[...]).astype(BF)
    project(first_ref, norm_ref, wk_ref, wv_ref, new_k_ref, new_v_ref)
    all_q_ref[:near] = q_ref[...]
    all_q_ref[near:] = far_q
    every = (all_peak_ref, all_sum_ref, all_mix_ref)
    for old, new in zip((peak_ref, sum_ref, mix_ref), every, strict=True):
        new[:near] = old[...]
    attend(
        far_q, k_ref[...], v_ref[...], exponent, *[ref.at[pl.ds(near, cols)] for ref in every]
    )


def more_body(exponent, block_ref, norm_ref, wk_ref, wv_ref, q_ref, *refs):
    old, out, new = refs[:3], refs[3:6], refs[6:9]
    k_ref, v_ref = refs[9:]
    project(block_ref, norm_ref, wk_ref, wv_ref, k_ref, v_ref)
    attend(q_ref[...], k_ref[...], v_ref[...], exponent, *new)
    merge(old, new, out, exponent, False)


def spread(act, cols):
    size = act.shape[0]
    col = lax.broadcasted_iota(jnp.int32, act.shape, 0) % cols
    left = jnp.where(col == 0, 0.0, pltpu.roll(act, 1, 0))
    right = jnp.where(col == cols - 1, 0.0, pltpu.roll(act, size - 1, 0))
    return jnp.concatenate([left.astype(BF), act.astype(BF), right.astype(BF)], axis=1)


def conv(wide_ref, taps, out_cells, cols):
    total = None
    for row in range(3):
        term = dot(wide_ref[row * cols : row * cols + out_cells, :], taps(row))
        total = term if total is None else total + term
    return total


def late_body(
    cols, exponent,
    place_ref, own_ref, sib_ref, far_ref, block_ref, norm_ref, q_ref, peak_ref, sum_ref, mix_ref,
    k_ref, v_ref, wk_ref, wv_ref, wo_ref, taps_ref,
    even_ref, odd_ref, wide_ref, mid_ref,
    keys_ref, values_ref, new_peak_ref, new_sum_ref, new_mix_ref, attended_ref,
):
    cells = own_ref.shape[0]
    core = place_ref[0]
    keys_ref[:cells] = k_ref[...]
    values_ref[:cells] = v_ref[...]
    rest = pl.ds(cells, cells)
    project(block_ref, norm_ref, wk_ref, wv_ref, keys_ref.at[rest], values_ref.at[rest])
    new = (new_peak_ref, new_sum_ref, new_mix_ref)
    attend(q_ref[...], keys_ref[...], values_ref[...], exponent, *new)
    merge((peak_ref, sum_ref, mix_ref), new, (attended_ref,), exponent, True)
    change = dot(attended_ref[...], wo_ref[...])
    near = pl.multiple_of(core * (cells - cols), 16)
    base = jnp.concatenate([own_ref[...], sib_ref[pl.ds(near, cols), :], far_ref[...]], axis=0)
    mid = (base.astype(F32) + change).astype(BF)
    mid_ref[...] = mid[:cells]
    act = jax.nn.silu(mid.astype(F32)).astype(BF).astype(F32)
    far_act = jnp.where(place_ref[1] != 0, act[cells + cols :], 0.0)
    above = pl.multiple_of(core * (cells + cols), 16)
    below = pl.multiple_of((1 - core) * (cells + cols), 16)
    wide_ref[cols : cols + cells] = spread(act[:cells], cols)
    wide_ref[pl.ds(below, cols), :] = spread(act[cells : cells + cols], cols)
    wide_ref[pl.ds(above, cols), :] = spread(far_act, cols)
    first_tap = conv(wide_ref, lambda row: taps_ref[0, row], cells, cols)
    second_tap = conv(wide_ref, lambda row: taps_ref[1, row], cells, cols)
    even_ref[...] = (first_tap + second_tap).astype(BF)
    odd_ref[:cells] = first_tap.astype(BF)
    odd_ref[cells:] = jnp.zeros((PAD, odd_ref.shape[1]), BF)


def now_body(cols, wide_ref, mid_ref, taps_ref, skip_hbm_ref, out_ref, skip_ref, sem):
    copy = pltpu.make_async_copy(skip_hbm_ref, skip_ref, sem)
    copy.start()
    cells = mid_ref.shape[0]
    second_tap = conv(wide_ref, lambda row: taps_ref[1, row], cells, cols)
    last_tap = conv(wide_ref, lambda row: taps_ref[2, row], cells, cols)
    copy.wait()
    last_tap = last_tap + dot(mid_ref[...], skip_ref[...])
    out_ref[0] = last_tap
    out_ref[1] = last_tap + second_tap


def odd_body(place_ref, now_ref, own_ref, arrived_ref, sum_ref):
    cells = now_ref.shape[1]
    before = jnp.where(place_ref[2] != 0, own_ref[:cells], arrived_ref[:cells])
    sum_ref[0] = now_ref[0]
    sum_ref[1] = now_ref[1] + before.astype(F32)


def per_device(
    features,
    norm_gain,
    query_weight,
    key_weight,
    value_weight,
    out_weight,
    conv_weight,
    skip_weight,
):
    _, tile_rows, cols, channels = features.shape
    out_channels = conv_weight.shape[-1]
    cells = tile_rows * cols
    devices = lax.axis_size("tile")
    chips = devices // 2
    me = lax.axis_index("tile")
    core = me % 2
    swap = [(i, i ^ 1) for i in range(devices)]
    own = features.reshape(cells, channels)

    def turned(array, by, flip):
        pairs = [(i, ((i + 2 * by) % devices) ^ flip) for i in range(devices)]
        return lax.ppermute(array, "tile", pairs)

    sib = lax.ppermute(own, "tile", swap)
    sums, own = call(
        stats_body,
        [jax.ShapeDtypeStruct((8, channels), F32), jax.ShapeDtypeStruct(own.shape, BF)],
        [pltpu.SemaphoreType.DMA((PIECES,))],
        1 << 22,
        hbm(own),
        spaces=[pltpu.HBM],
    )
    sums = [sums] + [turned(sums, by, 1) for by in range(1, chips)]
    recv = [turned(own, by, 1) for by in range(1, chips)]
    sums = jnp.concatenate(sums, axis=0)
    sums = [sums, lax.ppermute(sums, "tile", swap)]

    exponent = channels ** (-0.5) * 1.4426950408889634
    outside = jnp.where(core == 0, me == 0, me == devices - 1)
    first_span = lax.axis_index("tm") == 0
    place = jnp.stack([core, 1 - outside.astype(jnp.int32), first_span.astype(jnp.int32)])
    place = place.astype(jnp.int32)
    near = cells + cols
    every = near + cols
    taps = conv_weight.reshape(3, 3, 3 * channels, out_channels)
    weights = [norm_gain.reshape(1, channels), query_weight, key_weight, value_weight]
    held = call(
        stage_body,
        [jax.ShapeDtypeStruct(w.shape, w.dtype) for w in weights],
        [pltpu.SemaphoreType.DMA((len(weights),))],
        1 << 20,
        sums[0], *[hbm(w) for w in weights],
        spaces=[VMEM] + [pltpu.HBM] * len(weights),
    )
    _, wq, wk, wv = held

    def rows_of(rows, kind=BF, width=channels):
        return jax.ShapeDtypeStruct((rows, width), kind)

    def state_of(rows):
        return [rows_of(rows, F32, 128), rows_of(rows, F32, 128), rows_of(rows, F32)]

    def scratch_of(shapes):
        return [VMEM(shape.shape, shape.dtype) for shape in shapes]

    n_sums = len(sums)
    norm, q, k, v, *rest = call(
        functools.partial(early_body, devices * cells, cols, exponent, n_sums),
        [
            rows_of(8, F32),
            rows_of(near),
            rows_of(2 * cells),
            rows_of(2 * cells),
            *state_of(near),
            *[jax.ShapeDtypeStruct(w.shape, w.dtype) for w in (out_weight, taps)],
        ],
        [pltpu.SemaphoreType.DMA((2,))],
        2 * 10**9,
        place, own, sib, *sums, *held, hbm(out_weight), hbm(taps),
        spaces=[pltpu.SMEM] + [VMEM] * (6 + n_sums) + [pltpu.HBM] * 2,
    )
    state, (wo, held_taps) = rest[:3], rest[3:]

    *recv, norm = lax.optimization_barrier((*recv, norm))
    rsib = [lax.ppermute(block, "tile", swap) for block in recv]
    ends = recv[:1] if chips == 2 else [recv[0], recv[-1]]
    far, q, *state, new_k, new_v = call(
        functools.partial(join_body, cols, exponent, chips == 2),
        [rows_of(cols), rows_of(every), *state_of(every), rows_of(cells), rows_of(cells)],
        [],
        2 * 10**9,
        place, *ends, norm, wq, wk, wv, q, k, v, *state,
        spaces=[pltpu.SMEM] + [VMEM] * (10 + len(ends)),
    )
    for block in recv[1:] + rsib[:-1]:
        state = call(
            functools.partial(more_body, exponent),
            state_of(every),
            scratch_of([*state_of(every), rows_of(cells), rows_of(cells)]),
            10**9,
            block, norm, wk, wv, q, *state,
        )
    even, odd, wide, mid = call(
        functools.partial(late_body, cols, exponent),
        [
            rows_of(cells, BF, out_channels),
            rows_of(cells + PAD, BF, out_channels),
            rows_of(every, BF, 3 * channels),
            rows_of(cells),
        ],
        scratch_of([rows_of(2 * cells), rows_of(2 * cells), *state_of(every), rows_of(every)]),
        4 * 10**9,
        place, own, sib, far, rsib[-1], norm, q, *state, new_k, new_v, wk, wv, wo, held_taps,
        spaces=[pltpu.SMEM] + [VMEM] * 15,
    )
    spans = lax.axis_size("tm")
    arrived_odd = lax.ppermute(odd, "tm", [(i, (i + 1) % spans) for i in range(spans)])
    arrived_even = lax.ppermute(even, "tm", [(i, i + 1) for i in range(spans - 1)])
    both = jax.ShapeDtypeStruct((2, cells, out_channels), F32)
    now = call(
        functools.partial(now_body, cols),
        both,
        [VMEM(skip_weight.shape, BF), pltpu.SemaphoreType.DMA],
        2 * 10**9,
        wide, mid, held_taps, hbm(skip_weight),
        spaces=[VMEM, VMEM, VMEM, pltpu.HBM],
    )
    total = call(
        odd_body, both, [], 1, place, now, odd, arrived_odd, spaces=[pltpu.SMEM] + [VMEM] * 3
    )
    total, arrived_even = lax.optimization_barrier((total, arrived_even))
    before = jnp.where(first_span, even, arrived_even).astype(F32)
    is_even = lax.broadcasted_iota(jnp.int32, both.shape, 0) == 0
    decoded = (total + jnp.where(is_even, before, 0.0)).astype(BF)
    return decoded.reshape(2, tile_rows, cols, out_channels)


def solution(mesh):
    in_specs = (P("tm", "tile", None, None), P(), P(), P(), P(), P(), P(), P())
    out_specs = P("tm", "tile", None, None)
    return jax.shard_map(
        per_device, mesh=mesh, in_specs=in_specs, out_specs=out_specs, check_vma=False
    )
```

```python
import functools

import jax
import jax.numpy as jnp
from jax import lax
from jax.experimental import pallas as pl
from jax.experimental.pallas import tpu as pltpu
from jax.sharding import PartitionSpec as P

GROUPS = 32
BF = jnp.bfloat16
F32 = jnp.float32
VMEM = pltpu.VMEM
LIMIT = 12 * 1024 * 1024
PIECES = 4
PAD = 16
STATS_COST = 1 << 6
STAGE_COST = 1 << 4
EARLY_COST = 2 * 10**9
JOIN_COST = LATE_COST = NOW_COST = 1 << 15


def dot(left, right):
    return jnp.dot(left, right, preferred_element_type=F32)


def dot_t(left, right):
    return lax.dot_general(left, right, (((1,), (1,)), ((), ())), preferred_element_type=F32)


def spec(space=VMEM):
    return pl.BlockSpec(memory_space=space)


def hbm(array):
    return pltpu.with_memory_space_constraint(array, pltpu.HBM)


def call(body, outs, scratch, cost, *args, spaces=None):
    spaces = spaces or [VMEM] * len(args)
    return pl.pallas_call(
        body,
        out_shape=outs,
        in_specs=[spec(s) for s in spaces],
        out_specs=jax.tree.map(lambda _: spec(), outs),
        scratch_shapes=scratch,
        compiler_params=pltpu.CompilerParams(vmem_limit_bytes=LIMIT),
        cost_estimate=pl.CostEstimate(flops=cost, bytes_accessed=1 << 10, transcendentals=0),
    )(*args)


def core_index():
    return lax.axis_index("tile") % 2


def far_is_inside():
    me = lax.axis_index("tile")
    core = me % 2
    last = lax.axis_size("tile") - 1
    return me != core * last


def stats_body(features_ref, sums_ref, own_ref, sems):
    rows = own_ref.shape[0] // PIECES
    copies = []
    for i in range(PIECES):
        piece = pl.ds(i * rows, rows)
        copies.append(
            pltpu.make_async_copy(features_ref.at[piece], own_ref.at[piece], sems.at[i])
        )
        copies[-1].start()
    total = jnp.zeros((1, own_ref.shape[1]), F32)
    squared = total
    for i in range(PIECES):
        copies[i].wait()
        block = own_ref[i * rows : (i + 1) * rows].astype(F32)
        total += jnp.sum(block, axis=0, keepdims=True)
        squared += jnp.sum(block * block, axis=0, keepdims=True)
    sums_ref[...] = jnp.concatenate(
        [total, squared, jnp.zeros((6, own_ref.shape[1]), F32)], axis=0
    )


def group_sums(sums, width):
    lane = lax.broadcasted_iota(jnp.int32, sums.shape, 1)
    size = sums.shape[1]
    step = 1
    while step < width:
        low = pltpu.roll(sums, size - step, 1)
        high = pltpu.roll(sums, step, 1)
        sums = sums + jnp.where((lane & step) == 0, low, high)
        step *= 2
    return sums


def moments(sum_refs, cells):
    sums = 0.0
    for ref in sum_refs:
        for first in range(0, ref.shape[0], 8):
            sums = sums + ref[first : first + 8]
    width = sums.shape[1] // GROUPS
    sums = group_sums(sums, width)
    population = cells * width
    mean = sums[0:1] / population
    var = sums[1:2] / population - mean * mean
    return mean, lax.rsqrt(var + 1e-06)


def normalise(block, mean, inverse, gain):
    return ((block.astype(F32) - mean) * inverse * gain).astype(BF)


def attend(queries, keys, values, exponent, peak_ref, sum_ref, mix_ref):
    scores = dot_t(queries, keys)
    peak = jnp.max(scores, axis=1, keepdims=True)
    unnormed = jnp.exp2((scores - peak) * exponent)
    peak_ref[...] = jnp.broadcast_to(peak, peak_ref.shape)
    sum_ref[...] = jnp.broadcast_to(jnp.sum(unnormed, axis=1, keepdims=True), sum_ref.shape)
    mix_ref[...] = dot(unnormed.astype(BF), values)


def merge(old, new, out_refs, exponent, last):
    peak = jnp.maximum(old[0][...], new[0][...])
    fade_old = jnp.exp2((old[0][...] - peak) * exponent)
    fade_new = jnp.exp2((new[0][...] - peak) * exponent)
    total = old[1][...] * fade_old + new[1][...] * fade_new
    if last:
        scale = 1.0 / total
        fade_old = fade_old * scale
        fade_new = fade_new * scale
    else:
        out_refs[0][...] = peak
        out_refs[1][...] = total
    width = peak.shape[1]
    for first in range(0, old[2].shape[1], width):
        lanes = slice(first, first + width)
        mixed = old[2][:, lanes] * fade_old + new[2][:, lanes] * fade_new
        out_refs[-1][:, lanes] = mixed.astype(out_refs[-1].dtype)


def stage_body(*refs):
    refs, sems = refs[1:-1], refs[-1]
    count = len(refs) // 2
    copies = [
        pltpu.make_async_copy(refs[i], refs[count + i], sems.at[i]) for i in range(count)
    ]
    for copy in copies:
        copy.start()
    for copy in copies:
        copy.wait()


def early_body(
    cells_all, cols, exponent, n_sums,
    own_ref, sib_ref, *refs,
):
    sum_refs, refs = refs[:n_sums], refs[n_sums:]
    gain_ref, wq_ref, wk_ref, wv_ref, wo_hbm_ref, taps_hbm_ref, refs = *refs[:6], refs[6:]
    norm_ref, q_ref, k_ref, v_ref, *state_refs = refs[:7]
    wo_ref, taps_ref, sems = refs[7:]
    copies = [
        pltpu.make_async_copy(wo_hbm_ref, wo_ref, sems.at[0]),
        pltpu.make_async_copy(taps_hbm_ref.at[pl.ds(0, 2)], taps_ref, sems.at[1]),
    ]
    for copy in copies:
        copy.start()
    mean, inverse = moments(sum_refs, cells_all)
    gain = gain_ref[...]
    norm_ref[...] = jnp.concatenate(
        [mean, inverse, gain, jnp.zeros((5, mean.shape[1]), F32)], axis=0
    )
    cells = own_ref.shape[0]
    core = core_index()
    own = normalise(own_ref[...], mean, inverse, gain)
    sib = normalise(sib_ref[...], mean, inverse, gain)
    near = pl.multiple_of(core * (cells - cols), 16)
    halo = normalise(sib_ref[pl.ds(near, cols), :], mean, inverse, gain)
    both = jnp.concatenate([own, sib], axis=0)
    q_ref[...] = dot(jnp.concatenate([own, halo], axis=0), wq_ref[...]).astype(BF)
    k_ref[...] = dot(both, wk_ref[...]).astype(BF)
    v_ref[...] = dot(both, wv_ref[...]).astype(BF)
    attend(q_ref[...], k_ref[...], v_ref[...], exponent, *state_refs)
    for copy in copies:
        copy.wait()


def normal_of(norm_ref):
    return norm_ref[0:1], norm_ref[1:2], norm_ref[2:3]


def far_rows(first_ref, last_ref, cols):
    core = core_index()
    far = pl.multiple_of((1 - core) * (first_ref.shape[0] - cols), 16)
    first = first_ref[pl.ds(far, cols), :]
    if last_ref is None:
        return first
    return jnp.where(core == 0, first, last_ref[pl.ds(far, cols), :])


def project(block_ref, norm_ref, wk_ref, wv_ref, k_ref, v_ref):
    normed = normalise(block_ref[...], *normal_of(norm_ref))
    k_ref[...] = dot(normed, wk_ref[...]).astype(BF)
    v_ref[...] = dot(normed, wv_ref[...]).astype(BF)


def join_body(cols, exponent, single, *refs):
    first_ref, refs = refs[0], refs[1:]
    last_ref, refs = (None, refs) if single else (refs[0], refs[1:])
    (norm_ref, wq_ref, wk_ref, wv_ref, q_ref, k_ref, v_ref, peak_ref, sum_ref, mix_ref,
     far_ref, all_q_ref, all_peak_ref, all_sum_ref, all_mix_ref, new_k_ref, new_v_ref) = refs
    near = q_ref.shape[0]
    far = far_rows(first_ref, last_ref, cols)
    far_ref[...] = far
    far_q = dot(normalise(far, *normal_of(norm_ref)), wq_ref[...]).astype(BF)
    project(first_ref, norm_ref, wk_ref, wv_ref, new_k_ref, new_v_ref)
    all_q_ref[:near] = q_ref[...]
    all_q_ref[near:] = far_q
    every = (all_peak_ref, all_sum_ref, all_mix_ref)
    for old, new in zip((peak_ref, sum_ref, mix_ref), every, strict=True):
        new[:near] = old[...]
    attend(
        far_q, k_ref[...], v_ref[...], exponent, *[ref.at[pl.ds(near, cols)] for ref in every]
    )


def more_body(exponent, block_ref, norm_ref, wk_ref, wv_ref, q_ref, *refs):
    old, out, new = refs[:3], refs[3:6], refs[6:9]
    k_ref, v_ref = refs[9:]
    project(block_ref, norm_ref, wk_ref, wv_ref, k_ref, v_ref)
    attend(q_ref[...], k_ref[...], v_ref[...], exponent, *new)
    merge(old, new, out, exponent, False)


def spread(act, cols):
    size = act.shape[0]
    col = lax.broadcasted_iota(jnp.int32, act.shape, 0) % cols
    left = jnp.where(col == 0, 0.0, pltpu.roll(act, 1, 0))
    right = jnp.where(col == cols - 1, 0.0, pltpu.roll(act, size - 1, 0))
    return jnp.concatenate([left.astype(BF), act.astype(BF), right.astype(BF)], axis=1)


def conv(wide_ref, taps, out_cells, cols):
    total = None
    for row in range(3):
        term = dot(wide_ref[row * cols : row * cols + out_cells, :], taps(row))
        total = term if total is None else total + term
    return total


def late_body(
    cols, exponent,
    own_ref, sib_ref, far_ref, block_ref, norm_ref, q_ref, peak_ref, sum_ref, mix_ref,
    k_ref, v_ref, wk_ref, wv_ref, wo_ref, taps_ref,
    even_ref, odd_ref, second_ref, wide_ref, mid_ref,
    keys_ref, values_ref, new_peak_ref, new_sum_ref, new_mix_ref, attended_ref,
):
    cells = own_ref.shape[0]
    core = core_index()
    keys_ref[:cells] = k_ref[...]
    values_ref[:cells] = v_ref[...]
    rest = pl.ds(cells, cells)
    project(block_ref, norm_ref, wk_ref, wv_ref, keys_ref.at[rest], values_ref.at[rest])
    new = (new_peak_ref, new_sum_ref, new_mix_ref)
    attend(q_ref[...], keys_ref[...], values_ref[...], exponent, *new)
    merge((peak_ref, sum_ref, mix_ref), new, (attended_ref,), exponent, True)
    change = dot(attended_ref[...], wo_ref[...])
    near = pl.multiple_of(core * (cells - cols), 16)
    base = jnp.concatenate([own_ref[...], sib_ref[pl.ds(near, cols), :], far_ref[...]], axis=0)
    mid = (base.astype(F32) + change).astype(BF)
    mid_ref[...] = mid[:cells]
    act = jax.nn.silu(mid.astype(F32)).astype(BF).astype(F32)
    far_act = jnp.where(far_is_inside(), act[cells + cols :], 0.0)
    above = pl.multiple_of(core * (cells + cols), 16)
    below = pl.multiple_of((1 - core) * (cells + cols), 16)
    wide_ref[cols : cols + cells] = spread(act[:cells], cols)
    wide_ref[pl.ds(below, cols), :] = spread(act[cells : cells + cols], cols)
    wide_ref[pl.ds(above, cols), :] = spread(far_act, cols)
    first_tap = conv(wide_ref, lambda row: taps_ref[0, row], cells, cols)
    second_tap = conv(wide_ref, lambda row: taps_ref[1, row], cells, cols)
    second_ref[...] = second_tap
    even_ref[...] = (first_tap + second_tap).astype(BF)
    odd_ref[:cells] = first_tap.astype(BF)
    odd_ref[cells:] = jnp.zeros((PAD, odd_ref.shape[1]), BF)


def now_body(
    cols, wide_ref, mid_ref, second_ref, taps_ref, skip_hbm_ref, out_ref, tap_ref, skip_ref, sems
):
    copies = [
        pltpu.make_async_copy(skip_hbm_ref, skip_ref, sems.at[0]),
        pltpu.make_async_copy(taps_ref.at[2], tap_ref, sems.at[1]),
    ]
    for copy in copies:
        copy.start()
    cells = mid_ref.shape[0]
    copies[0].wait()
    skip = dot(mid_ref[...], skip_ref[...])
    copies[1].wait()
    last_tap = conv(wide_ref, lambda row: tap_ref[row], cells, cols) + skip
    out_ref[0] = last_tap
    out_ref[1] = last_tap + second_ref[...]


def odd_body(now_ref, own_ref, arrived_ref, sum_ref):
    cells = now_ref.shape[1]
    before = jnp.where(lax.axis_index("tm") == 0, own_ref[:cells], arrived_ref[:cells])
    sum_ref[0] = now_ref[0]
    sum_ref[1] = now_ref[1] + before.astype(F32)


def per_device(
    features,
    norm_gain,
    query_weight,
    key_weight,
    value_weight,
    out_weight,
    conv_weight,
    skip_weight,
):
    _, tile_rows, cols, channels = features.shape
    out_channels = conv_weight.shape[-1]
    cells = tile_rows * cols
    devices = lax.axis_size("tile")
    chips = devices // 2
    swap = [(i, i ^ 1) for i in range(devices)]
    own = features.reshape(cells, channels)

    def turned(array, by, flip):
        pairs = [(i, ((i + 2 * by) % devices) ^ flip) for i in range(devices)]
        return lax.ppermute(array, "tile", pairs)

    sib = lax.ppermute(own, "tile", swap)
    sums, own = call(
        stats_body,
        [jax.ShapeDtypeStruct((8, channels), F32), jax.ShapeDtypeStruct(own.shape, BF)],
        [pltpu.SemaphoreType.DMA((PIECES,))],
        STATS_COST,
        hbm(own),
        spaces=[pltpu.HBM],
    )
    sums = [sums] + [turned(sums, by, 1) for by in range(1, chips)]
    recv = [turned(own, by, 1) for by in range(1, chips)]
    sums = jnp.concatenate(sums, axis=0)
    sums = [sums, lax.ppermute(sums, "tile", swap)]

    exponent = channels ** (-0.5) * 1.4426950408889634
    first_span = lax.axis_index("tm") == 0
    near = cells + cols
    every = near + cols
    taps = conv_weight.reshape(3, 3, 3 * channels, out_channels)
    first_taps = (2, *taps.shape[1:])
    weights = [norm_gain.reshape(1, channels), query_weight, key_weight, value_weight]
    held = call(
        stage_body,
        [jax.ShapeDtypeStruct(w.shape, w.dtype) for w in weights],
        [pltpu.SemaphoreType.DMA((len(weights),))],
        STAGE_COST,
        sums[0], *[hbm(w) for w in weights],
        spaces=[VMEM] + [pltpu.HBM] * len(weights),
    )
    _, wq, wk, wv = held

    def rows_of(rows, kind=BF, width=channels):
        return jax.ShapeDtypeStruct((rows, width), kind)

    def state_of(rows):
        return [rows_of(rows, F32, 128), rows_of(rows, F32, 128), rows_of(rows, F32)]

    def scratch_of(shapes):
        return [VMEM(shape.shape, shape.dtype) for shape in shapes]

    n_sums = len(sums)
    norm, q, k, v, *rest = call(
        functools.partial(early_body, devices * cells, cols, exponent, n_sums),
        [
            rows_of(8, F32),
            rows_of(near),
            rows_of(2 * cells),
            rows_of(2 * cells),
            *state_of(near),
            jax.ShapeDtypeStruct(out_weight.shape, BF),
            jax.ShapeDtypeStruct(first_taps, BF),
        ],
        [pltpu.SemaphoreType.DMA((2,))],
        EARLY_COST,
        own, sib, *sums, *held, hbm(out_weight), hbm(taps),
        spaces=[VMEM] * (6 + n_sums) + [pltpu.HBM] * 2,
    )
    state, (wo, held_taps) = rest[:3], rest[3:]

    *recv, norm = lax.optimization_barrier((*recv, norm))
    rsib = [lax.ppermute(block, "tile", swap) for block in recv]
    ends = recv[:1] if chips == 2 else [recv[0], recv[-1]]
    far, q, *state, new_k, new_v = call(
        functools.partial(join_body, cols, exponent, chips == 2),
        [rows_of(cols), rows_of(every), *state_of(every), rows_of(cells), rows_of(cells)],
        [],
        JOIN_COST,
        *ends, norm, wq, wk, wv, q, k, v, *state,
    )
    for block in recv[1:] + rsib[:-1]:
        state = call(
            functools.partial(more_body, exponent),
            state_of(every),
            scratch_of([*state_of(every), rows_of(cells), rows_of(cells)]),
            10**9,
            block, norm, wk, wv, q, *state,
        )
    even, odd, second, wide, mid = call(
        functools.partial(late_body, cols, exponent),
        [
            rows_of(cells, BF, out_channels),
            rows_of(cells + PAD, BF, out_channels),
            rows_of(cells, F32, out_channels),
            rows_of(every, BF, 3 * channels),
            rows_of(cells),
        ],
        scratch_of([rows_of(2 * cells), rows_of(2 * cells), *state_of(every), rows_of(every)]),
        LATE_COST,
        own, sib, far, rsib[-1], norm, q, *state, new_k, new_v, wk, wv, wo, held_taps,
    )
    spans = lax.axis_size("tm")
    arrived_odd = lax.ppermute(odd, "tm", [(i, (i + 1) % spans) for i in range(spans)])
    arrived_even = lax.ppermute(even, "tm", [(i, i + 1) for i in range(spans - 1)])
    both = jax.ShapeDtypeStruct((2, cells, out_channels), F32)
    now = call(
        functools.partial(now_body, cols),
        both,
        [
            VMEM(taps.shape[1:], BF),
            VMEM(skip_weight.shape, BF),
            pltpu.SemaphoreType.DMA((2,)),
        ],
        NOW_COST,
        wide, mid, second, hbm(taps), hbm(skip_weight),
        spaces=[VMEM] * 3 + [pltpu.HBM] * 2,
    )
    total = call(
        odd_body, both, [], 1, now, odd, arrived_odd
    )
    total, arrived_even = lax.optimization_barrier((total, arrived_even))
    before = jnp.where(first_span, even, arrived_even).astype(F32)
    is_even = lax.broadcasted_iota(jnp.int32, both.shape, 0) == 0
    decoded = (total + jnp.where(is_even, before, 0.0)).astype(BF)
    return decoded.reshape(2, tile_rows, cols, out_channels)


def solution(mesh):
    in_specs = (P("tm", "tile", None, None), P(), P(), P(), P(), P(), P(), P())
    out_specs = P("tm", "tile", None, None)
    return jax.shard_map(
        per_device, mesh=mesh, in_specs=in_specs, out_specs=out_specs, check_vma=False
    )
```

```python
import functools

import jax
import jax.numpy as jnp
from jax import lax
from jax.experimental import pallas as pl
from jax.experimental.pallas import tpu as pltpu
from jax.sharding import PartitionSpec as P

GROUPS = 32
BF = jnp.bfloat16
F32 = jnp.float32
VMEM = pltpu.VMEM
LIMIT = 12 * 1024 * 1024
PIECES = 8
STATS_COST = 1 << 6
STAGE_COST = 1 << 4
EARLY_COST = 2 * 10**9
JOIN_COST = LATE_COST = NOW_COST = 1 << 15


def dot(left, right):
    return jnp.dot(left, right, preferred_element_type=F32)


def dot_t(left, right):
    return lax.dot_general(left, right, (((1,), (1,)), ((), ())), preferred_element_type=F32)


def spec(space=VMEM):
    return pl.BlockSpec(memory_space=space)


def hbm(array):
    return pltpu.with_memory_space_constraint(array, pltpu.HBM)


def call(body, outs, scratch, cost, *args, spaces=None):
    spaces = spaces or [VMEM] * len(args)
    return pl.pallas_call(
        body,
        out_shape=outs,
        in_specs=[spec(s) for s in spaces],
        out_specs=jax.tree.map(lambda _: spec(), outs),
        scratch_shapes=scratch,
        compiler_params=pltpu.CompilerParams(vmem_limit_bytes=LIMIT),
        cost_estimate=pl.CostEstimate(flops=cost, bytes_accessed=1 << 10, transcendentals=0),
    )(*args)


def core_index():
    return lax.axis_index("tile") % 2


def far_is_inside():
    me = lax.axis_index("tile")
    core = me % 2
    last = lax.axis_size("tile") - 1
    return me != core * last


def stats_body(features_ref, sums_ref, own_ref, sems):
    rows = own_ref.shape[0] // PIECES
    copies = []
    for i in range(PIECES):
        piece = pl.ds(i * rows, rows)
        copies.append(
            pltpu.make_async_copy(features_ref.at[piece], own_ref.at[piece], sems.at[i])
        )
        copies[-1].start()
    total = jnp.zeros((1, own_ref.shape[1]), F32)
    squared = total
    for i in range(PIECES):
        copies[i].wait()
        block = own_ref[i * rows : (i + 1) * rows].astype(F32)
        total += jnp.sum(block, axis=0, keepdims=True)
        squared += jnp.sum(block * block, axis=0, keepdims=True)
    sums_ref[...] = jnp.concatenate(
        [total, squared, jnp.zeros((6, own_ref.shape[1]), F32)], axis=0
    )


def group_sums(sums, width):
    lane = lax.broadcasted_iota(jnp.int32, sums.shape, 1)
    size = sums.shape[1]
    step = 1
    while step < width:
        low = pltpu.roll(sums, size - step, 1)
        high = pltpu.roll(sums, step, 1)
        sums = sums + jnp.where((lane & step) == 0, low, high)
        step *= 2
    return sums


def moments(sum_refs, cells):
    sums = 0.0
    for ref in sum_refs:
        for first in range(0, ref.shape[0], 8):
            sums = sums + ref[first : first + 8]
    width = sums.shape[1] // GROUPS
    sums = group_sums(sums, width)
    population = cells * width
    mean = sums[0:1] / population
    var = sums[1:2] / population - mean * mean
    return mean, lax.rsqrt(var + 1e-06)


def normalise(block, mean, inverse, gain):
    return ((block.astype(F32) - mean) * inverse * gain).astype(BF)


def attend(queries, keys, values, exponent, peak_ref, sum_ref, mix_ref):
    scores = dot_t(queries, keys)
    peak = jnp.max(scores, axis=1, keepdims=True)
    unnormed = jnp.exp2((scores - peak) * exponent)
    peak_ref[...] = jnp.broadcast_to(peak, peak_ref.shape)
    sum_ref[...] = jnp.broadcast_to(jnp.sum(unnormed, axis=1, keepdims=True), sum_ref.shape)
    mix_ref[...] = dot(unnormed.astype(BF), values)


def merge(old, new, out_refs, exponent, last):
    peak = jnp.maximum(old[0][...], new[0][...])
    fade_old = jnp.exp2((old[0][...] - peak) * exponent)
    fade_new = jnp.exp2((new[0][...] - peak) * exponent)
    total = old[1][...] * fade_old + new[1][...] * fade_new
    if last:
        scale = 1.0 / total
        fade_old = fade_old * scale
        fade_new = fade_new * scale
    else:
        out_refs[0][...] = peak
        out_refs[1][...] = total
    width = peak.shape[1]
    for first in range(0, old[2].shape[1], width):
        lanes = slice(first, first + width)
        mixed = old[2][:, lanes] * fade_old + new[2][:, lanes] * fade_new
        out_refs[-1][:, lanes] = mixed.astype(out_refs[-1].dtype)


def stage_body(*refs):
    refs, sems = refs[1:-1], refs[-1]
    count = len(refs) // 2
    copies = [
        pltpu.make_async_copy(refs[i], refs[count + i], sems.at[i]) for i in range(count)
    ]
    for copy in copies:
        copy.start()
    for copy in copies:
        copy.wait()


def early_body(
    cells_all, cols, exponent, n_sums,
    own_ref, sib_ref, *refs,
):
    sum_refs, refs = refs[:n_sums], refs[n_sums:]
    gain_ref, wq_ref, wk_ref, wv_ref, wo_hbm_ref, taps_hbm_ref, refs = *refs[:6], refs[6:]
    norm_ref, q_ref, k_ref, v_ref, *state_refs = refs[:7]
    wo_ref, taps_ref, sems = refs[7:]
    copies = [
        pltpu.make_async_copy(wo_hbm_ref, wo_ref, sems.at[0]),
        pltpu.make_async_copy(taps_hbm_ref.at[pl.ds(0, 2)], taps_ref, sems.at[1]),
    ]
    for copy in copies:
        copy.start()
    mean, inverse = moments(sum_refs, cells_all)
    gain = gain_ref[...]
    norm_ref[...] = jnp.concatenate(
        [mean, inverse, gain, jnp.zeros((5, mean.shape[1]), F32)], axis=0
    )
    cells = own_ref.shape[0]
    core = core_index()
    own = normalise(own_ref[...], mean, inverse, gain)
    sib = normalise(sib_ref[...], mean, inverse, gain)
    near = pl.multiple_of(core * (cells - cols), 16)
    halo = normalise(sib_ref[pl.ds(near, cols), :], mean, inverse, gain)
    both = jnp.concatenate([own, sib], axis=0)
    q_ref[...] = dot(jnp.concatenate([own, halo], axis=0), wq_ref[...]).astype(BF)
    k_ref[...] = dot(both, wk_ref[...]).astype(BF)
    v_ref[...] = dot(both, wv_ref[...]).astype(BF)
    attend(q_ref[...], k_ref[...], v_ref[...], exponent, *state_refs)
    for copy in copies:
        copy.wait()


def normal_of(norm_ref):
    return norm_ref[0:1], norm_ref[1:2], norm_ref[2:3]


def far_rows(first_ref, last_ref, cols):
    core = core_index()
    far = pl.multiple_of((1 - core) * (first_ref.shape[0] - cols), 16)
    first = first_ref[pl.ds(far, cols), :]
    if last_ref is None:
        return first
    return jnp.where(core == 0, first, last_ref[pl.ds(far, cols), :])


def project(block_ref, norm_ref, wk_ref, wv_ref, k_ref, v_ref):
    normed = normalise(block_ref[...], *normal_of(norm_ref))
    k_ref[...] = dot(normed, wk_ref[...]).astype(BF)
    v_ref[...] = dot(normed, wv_ref[...]).astype(BF)


def join_body(cols, exponent, single, *refs):
    first_ref, refs = refs[0], refs[1:]
    last_ref, refs = (None, refs) if single else (refs[0], refs[1:])
    (norm_ref, wq_ref, wk_ref, wv_ref, q_ref, k_ref, v_ref, peak_ref, sum_ref, mix_ref,
     far_ref, all_q_ref, all_peak_ref, all_sum_ref, all_mix_ref, new_k_ref, new_v_ref) = refs
    near = q_ref.shape[0]
    far = far_rows(first_ref, last_ref, cols)
    far_ref[...] = far
    far_q = dot(normalise(far, *normal_of(norm_ref)), wq_ref[...]).astype(BF)
    project(first_ref, norm_ref, wk_ref, wv_ref, new_k_ref, new_v_ref)
    all_q_ref[:near] = q_ref[...]
    all_q_ref[near:] = far_q
    every = (all_peak_ref, all_sum_ref, all_mix_ref)
    for old, new in zip((peak_ref, sum_ref, mix_ref), every, strict=True):
        new[:near] = old[...]
    attend(
        far_q, k_ref[...], v_ref[...], exponent, *[ref.at[pl.ds(near, cols)] for ref in every]
    )


def more_body(exponent, block_ref, norm_ref, wk_ref, wv_ref, q_ref, *refs):
    old, out, new = refs[:3], refs[3:6], refs[6:9]
    k_ref, v_ref = refs[9:]
    project(block_ref, norm_ref, wk_ref, wv_ref, k_ref, v_ref)
    attend(q_ref[...], k_ref[...], v_ref[...], exponent, *new)
    merge(old, new, out, exponent, False)


def spread(act, cols):
    size = act.shape[0]
    col = lax.broadcasted_iota(jnp.int32, act.shape, 0) % cols
    left = jnp.where(col == 0, 0.0, pltpu.roll(act, 1, 0))
    right = jnp.where(col == cols - 1, 0.0, pltpu.roll(act, size - 1, 0))
    return jnp.concatenate([left.astype(BF), act.astype(BF), right.astype(BF)], axis=1)


def conv(wide_ref, taps, out_cells, cols):
    total = None
    for row in range(3):
        term = dot(wide_ref[row * cols : row * cols + out_cells, :], taps(row))
        total = term if total is None else total + term
    return total


def late_body(
    cols, exponent,
    own_ref, sib_ref, far_ref, block_ref, norm_ref, q_ref, peak_ref, sum_ref, mix_ref,
    k_ref, v_ref, wk_ref, wv_ref, wo_ref, taps_ref,
    even_ref, odd_ref, second_ref, wide_ref, mid_ref,
    keys_ref, values_ref, new_peak_ref, new_sum_ref, new_mix_ref, attended_ref,
):
    cells = own_ref.shape[0]
    core = core_index()
    keys_ref[:cells] = k_ref[...]
    values_ref[:cells] = v_ref[...]
    rest = pl.ds(cells, cells)
    project(block_ref, norm_ref, wk_ref, wv_ref, keys_ref.at[rest], values_ref.at[rest])
    new = (new_peak_ref, new_sum_ref, new_mix_ref)
    attend(q_ref[...], keys_ref[...], values_ref[...], exponent, *new)
    merge((peak_ref, sum_ref, mix_ref), new, (attended_ref,), exponent, True)
    change = dot(attended_ref[...], wo_ref[...])
    near = pl.multiple_of(core * (cells - cols), 16)
    base = jnp.concatenate([own_ref[...], sib_ref[pl.ds(near, cols), :], far_ref[...]], axis=0)
    mid = (base.astype(F32) + change).astype(BF)
    mid_ref[...] = mid[:cells]
    act = jax.nn.silu(mid.astype(F32)).astype(BF).astype(F32)
    far_act = jnp.where(far_is_inside(), act[cells + cols :], 0.0)
    above = pl.multiple_of(core * (cells + cols), 16)
    below = pl.multiple_of((1 - core) * (cells + cols), 16)
    wide_ref[cols : cols + cells] = spread(act[:cells], cols)
    wide_ref[pl.ds(below, cols), :] = spread(act[cells : cells + cols], cols)
    wide_ref[pl.ds(above, cols), :] = spread(far_act, cols)
    first_tap = conv(wide_ref, lambda row: taps_ref[0, row], cells, cols)
    second_tap = conv(wide_ref, lambda row: taps_ref[1, row], cells, cols)
    second_ref[...] = second_tap
    even_ref[...] = (first_tap + second_tap).astype(BF)
    odd_ref[...] = first_tap.astype(BF)


def now_body(
    cols, wide_ref, mid_ref, second_ref, taps_ref, skip_hbm_ref, out_ref, tap_ref, skip_ref, sems
):
    copies = [
        pltpu.make_async_copy(skip_hbm_ref, skip_ref, sems.at[0]),
        pltpu.make_async_copy(taps_ref.at[2], tap_ref, sems.at[1]),
    ]
    for copy in copies:
        copy.start()
    cells = mid_ref.shape[0]
    copies[0].wait()
    skip = dot(mid_ref[...], skip_ref[...])
    copies[1].wait()
    last_tap = conv(wide_ref, lambda row: tap_ref[row], cells, cols) + skip
    out_ref[0] = last_tap
    out_ref[1] = last_tap + second_ref[...]


def odd_body(now_ref, own_ref, arrived_ref, sum_ref):
    before = jnp.where(lax.axis_index("tm") == 0, own_ref[...], arrived_ref[...])
    sum_ref[...] = (now_ref[1] + before.astype(F32)).astype(BF)


def last_body(odd_ref, now_ref, own_ref, arrived_ref, out_ref, even_ref, sems):
    odd_copy = pltpu.make_async_copy(odd_ref, out_ref.at[1], sems.at[1])
    odd_copy.start()
    before = jnp.where(lax.axis_index("tm") == 0, own_ref[...], arrived_ref[...])
    even_ref[...] = (now_ref[0] + before.astype(F32)).astype(BF)
    even_copy = pltpu.make_async_copy(even_ref, out_ref.at[0], sems.at[0])
    even_copy.start()
    odd_copy.wait()
    even_copy.wait()


def per_device(
    features,
    norm_gain,
    query_weight,
    key_weight,
    value_weight,
    out_weight,
    conv_weight,
    skip_weight,
):
    _, tile_rows, cols, channels = features.shape
    out_channels = conv_weight.shape[-1]
    cells = tile_rows * cols
    devices = lax.axis_size("tile")
    chips = devices // 2
    swap = [(i, i ^ 1) for i in range(devices)]
    own = features.reshape(cells, channels)

    def turned(array, by, flip):
        pairs = [(i, ((i + 2 * by) % devices) ^ flip) for i in range(devices)]
        return lax.ppermute(array, "tile", pairs)

    sib = lax.ppermute(own, "tile", swap)
    sums, own = call(
        stats_body,
        [jax.ShapeDtypeStruct((8, channels), F32), jax.ShapeDtypeStruct(own.shape, BF)],
        [pltpu.SemaphoreType.DMA((PIECES,))],
        STATS_COST,
        hbm(own),
        spaces=[pltpu.HBM],
    )
    sums = [sums] + [turned(sums, by, 1) for by in range(1, chips)]
    recv = [turned(own, by, 1) for by in range(1, chips)]
    sums = jnp.concatenate(sums, axis=0)
    sums = [sums, lax.ppermute(sums, "tile", swap)]

    exponent = channels ** (-0.5) * 1.4426950408889634
    near = cells + cols
    every = near + cols
    taps = conv_weight.reshape(3, 3, 3 * channels, out_channels)
    first_taps = (2, *taps.shape[1:])
    weights = [norm_gain.reshape(1, channels), query_weight, key_weight, value_weight]
    held = call(
        stage_body,
        [jax.ShapeDtypeStruct(w.shape, w.dtype) for w in weights],
        [pltpu.SemaphoreType.DMA((len(weights),))],
        STAGE_COST,
        sums[0], *[hbm(w) for w in weights],
        spaces=[VMEM] + [pltpu.HBM] * len(weights),
    )
    _, wq, wk, wv = held

    def rows_of(rows, kind=BF, width=channels):
        return jax.ShapeDtypeStruct((rows, width), kind)

    def state_of(rows):
        return [rows_of(rows, F32, 128), rows_of(rows, F32, 128), rows_of(rows, F32)]

    def scratch_of(shapes):
        return [VMEM(shape.shape, shape.dtype) for shape in shapes]

    n_sums = len(sums)
    norm, q, k, v, *rest = call(
        functools.partial(early_body, devices * cells, cols, exponent, n_sums),
        [
            rows_of(8, F32),
            rows_of(near),
            rows_of(2 * cells),
            rows_of(2 * cells),
            *state_of(near),
            jax.ShapeDtypeStruct(out_weight.shape, BF),
            jax.ShapeDtypeStruct(first_taps, BF),
        ],
        [pltpu.SemaphoreType.DMA((2,))],
        EARLY_COST,
        own, sib, *sums, *held, hbm(out_weight), hbm(taps),
        spaces=[VMEM] * (6 + n_sums) + [pltpu.HBM] * 2,
    )
    state, (wo, held_taps) = rest[:3], rest[3:]

    *recv, norm = lax.optimization_barrier((*recv, norm))
    rsib = [lax.ppermute(block, "tile", swap) for block in recv]
    ends = recv[:1] if chips == 2 else [recv[0], recv[-1]]
    far, q, *state, new_k, new_v = call(
        functools.partial(join_body, cols, exponent, chips == 2),
        [rows_of(cols), rows_of(every), *state_of(every), rows_of(cells), rows_of(cells)],
        [],
        JOIN_COST,
        *ends, norm, wq, wk, wv, q, k, v, *state,
    )
    for block in recv[1:] + rsib[:-1]:
        state = call(
            functools.partial(more_body, exponent),
            state_of(every),
            scratch_of([*state_of(every), rows_of(cells), rows_of(cells)]),
            10**9,
            block, norm, wk, wv, q, *state,
        )
    even, odd, second, wide, mid = call(
        functools.partial(late_body, cols, exponent),
        [
            rows_of(cells, BF, out_channels),
            rows_of(cells, BF, out_channels),
            rows_of(cells, F32, out_channels),
            rows_of(every, BF, 3 * channels),
            rows_of(cells),
        ],
        scratch_of([rows_of(2 * cells), rows_of(2 * cells), *state_of(every), rows_of(every)]),
        LATE_COST,
        own, sib, far, rsib[-1], norm, q, *state, new_k, new_v, wk, wv, wo, held_taps,
    )
    spans = lax.axis_size("tm")
    arrived_odd = lax.ppermute(odd, "tm", [(i, (i + 1) % spans) for i in range(spans)])
    arrived_even = lax.ppermute(even, "tm", [(i, i + 1) for i in range(spans - 1)])
    both = jax.ShapeDtypeStruct((2, cells, out_channels), F32)
    now = call(
        functools.partial(now_body, cols),
        both,
        [
            VMEM(taps.shape[1:], BF),
            VMEM(skip_weight.shape, BF),
            pltpu.SemaphoreType.DMA((2,)),
        ],
        NOW_COST,
        wide, mid, second, hbm(taps), hbm(skip_weight),
        spaces=[VMEM] * 3 + [pltpu.HBM] * 2,
    )
    share = rows_of(cells, BF, out_channels)
    done_odd = call(odd_body, share, [], 1, now, odd, arrived_odd)
    done_odd, arrived_even = lax.optimization_barrier((done_odd, arrived_even))
    decoded = pl.pallas_call(
        last_body,
        out_shape=jax.ShapeDtypeStruct((2, cells, out_channels), BF),
        in_specs=[spec()] * 4,
        out_specs=spec(pltpu.HBM),
        scratch_shapes=[VMEM((cells, out_channels), BF), pltpu.SemaphoreType.DMA((2,))],
        compiler_params=pltpu.CompilerParams(vmem_limit_bytes=LIMIT),
    )(done_odd, now, even, arrived_even)
    return decoded.reshape(2, tile_rows, cols, out_channels)


def solution(mesh):
    in_specs = (P("tm", "tile", None, None), P(), P(), P(), P(), P(), P(), P())
    out_specs = P("tm", "tile", None, None)
    return jax.shard_map(
        per_device, mesh=mesh, in_specs=in_specs, out_specs=out_specs, check_vma=False
    )
```

```python
import functools

import jax
import jax.numpy as jnp
from jax import lax
from jax.experimental import pallas as pl
from jax.experimental.pallas import tpu as pltpu
from jax.sharding import PartitionSpec as P

GROUPS = 32
BF = jnp.bfloat16
F32 = jnp.float32
VMEM = pltpu.VMEM
LIMIT = 12 * 1024 * 1024
PIECES = 8
STATS_COST = 1 << 6
STAGE_COST = 1 << 4
EARLY_COST = 7 * 10**8
JOIN_COST = LATE_COST = NOW_COST = 1 << 15


def dot(left, right):
    return jnp.dot(left, right, preferred_element_type=F32)


def dot_t(left, right):
    return lax.dot_general(left, right, (((1,), (1,)), ((), ())), preferred_element_type=F32)


def spec(space=VMEM):
    return pl.BlockSpec(memory_space=space)


def hbm(array):
    return pltpu.with_memory_space_constraint(array, pltpu.HBM)


def call(body, outs, scratch, cost, *args, spaces=None):
    spaces = spaces or [VMEM] * len(args)
    return pl.pallas_call(
        body,
        out_shape=outs,
        in_specs=[spec(s) for s in spaces],
        out_specs=jax.tree.map(lambda _: spec(), outs),
        scratch_shapes=scratch,
        compiler_params=pltpu.CompilerParams(vmem_limit_bytes=LIMIT),
        cost_estimate=pl.CostEstimate(flops=cost, bytes_accessed=1 << 10, transcendentals=0),
    )(*args)


def core_index():
    return lax.axis_index("tile") % 2


def far_is_inside():
    me = lax.axis_index("tile")
    core = me % 2
    last = lax.axis_size("tile") - 1
    return me != core * last


def stats_body(features_ref, sums_ref, own_ref, first_ref, second_ref, sems):
    rows = own_ref.shape[0] // PIECES
    copies = []
    for i in range(PIECES):
        piece = pl.ds(i * rows, rows)
        copies.append(
            pltpu.make_async_copy(features_ref.at[piece], own_ref.at[piece], sems.at[i])
        )
        copies[-1].start()
    total = jnp.zeros((1, own_ref.shape[1]), F32)
    squared = total
    for i in range(PIECES):
        copies[i].wait()
        block = own_ref[i * rows : (i + 1) * rows].astype(F32)
        total += jnp.sum(block, axis=0, keepdims=True)
        squared += jnp.sum(block * block, axis=0, keepdims=True)
    sums_ref[...] = jnp.concatenate(
        [total, squared, jnp.zeros((6, own_ref.shape[1]), F32)], axis=0
    )
    first = first_ref.shape[0]
    first_ref[...] = own_ref[:first]
    second_ref[...] = own_ref[first:]


def near_rows(first_ref, second_ref, cols):
    return jnp.where(core_index() == 0, first_ref[:cols], second_ref[second_ref.shape[0] - cols :])


def group_sums(sums, width):
    lane = lax.broadcasted_iota(jnp.int32, sums.shape, 1)
    size = sums.shape[1]
    step = 1
    while step < width:
        low = pltpu.roll(sums, size - step, 1)
        high = pltpu.roll(sums, step, 1)
        sums = sums + jnp.where((lane & step) == 0, low, high)
        step *= 2
    return sums


def moments(sum_refs, cells):
    sums = 0.0
    for ref in sum_refs:
        for first in range(0, ref.shape[0], 8):
            sums = sums + ref[first : first + 8]
    width = sums.shape[1] // GROUPS
    sums = group_sums(sums, width)
    population = cells * width
    mean = sums[0:1] / population
    var = sums[1:2] / population - mean * mean
    return mean, lax.rsqrt(var + 1e-06)


def normalise(block, mean, inverse, gain):
    return ((block.astype(F32) - mean) * inverse * gain).astype(BF)


def attend(queries, keys, values, exponent, peak_ref, sum_ref, mix_ref):
    scores = dot_t(queries, keys)
    peak = jnp.max(scores, axis=1, keepdims=True)
    unnormed = jnp.exp2((scores - peak) * exponent)
    peak_ref[...] = jnp.broadcast_to(peak, peak_ref.shape)
    sum_ref[...] = jnp.broadcast_to(jnp.sum(unnormed, axis=1, keepdims=True), sum_ref.shape)
    mix_ref[...] = dot(unnormed.astype(BF), values)


def merge(old, new, out_refs, exponent, last):
    peak = jnp.maximum(old[0][...], new[0][...])
    fade_old = jnp.exp2((old[0][...] - peak) * exponent)
    fade_new = jnp.exp2((new[0][...] - peak) * exponent)
    total = old[1][...] * fade_old + new[1][...] * fade_new
    if last:
        scale = 1.0 / total
        fade_old = fade_old * scale
        fade_new = fade_new * scale
    else:
        out_refs[0][...] = peak
        out_refs[1][...] = total
    width = peak.shape[1]
    for first in range(0, old[2].shape[1], width):
        lanes = slice(first, first + width)
        mixed = old[2][:, lanes] * fade_old + new[2][:, lanes] * fade_new
        out_refs[-1][:, lanes] = mixed.astype(out_refs[-1].dtype)


def stage_body(*refs):
    refs, sems = refs[1:-1], refs[-1]
    count = len(refs) // 2
    copies = [
        pltpu.make_async_copy(refs[i], refs[count + i], sems.at[i]) for i in range(count)
    ]
    for copy in copies:
        copy.start()
    for copy in copies:
        copy.wait()


def early_body(
    cells_all, cols, exponent, n_sums,
    own_ref, sib_first_ref, sib_second_ref, *refs,
):
    sum_refs, refs = refs[:n_sums], refs[n_sums:]
    gain_ref, wq_ref, wk_ref, wv_ref, wo_hbm_ref, taps_hbm_ref, refs = *refs[:6], refs[6:]
    norm_ref, q_ref, k_ref, v_ref, *state_refs = refs[:7]
    wo_ref, taps_ref, sems = refs[7:]
    copies = [
        pltpu.make_async_copy(wo_hbm_ref, wo_ref, sems.at[0]),
        pltpu.make_async_copy(taps_hbm_ref.at[pl.ds(0, 2)], taps_ref, sems.at[1]),
    ]
    for copy in copies:
        copy.start()
    mean, inverse = moments(sum_refs, cells_all)
    gain = gain_ref[...]
    norm_ref[...] = jnp.concatenate(
        [mean, inverse, gain, jnp.zeros((5, mean.shape[1]), F32)], axis=0
    )
    own = normalise(own_ref[...], mean, inverse, gain)
    sib = jnp.concatenate([sib_first_ref[...], sib_second_ref[...]], axis=0)
    sib = normalise(sib, mean, inverse, gain)
    halo = normalise(near_rows(sib_first_ref, sib_second_ref, cols), mean, inverse, gain)
    both = jnp.concatenate([own, sib], axis=0)
    q_ref[...] = dot(jnp.concatenate([own, halo], axis=0), wq_ref[...]).astype(BF)
    k_ref[...] = dot(both, wk_ref[...]).astype(BF)
    v_ref[...] = dot(both, wv_ref[...]).astype(BF)
    attend(q_ref[...], k_ref[...], v_ref[...], exponent, *state_refs)
    for copy in copies:
        copy.wait()


def normal_of(norm_ref):
    return norm_ref[0:1], norm_ref[1:2], norm_ref[2:3]


def far_rows(first_ref, last_ref, cols):
    core = core_index()
    far = pl.multiple_of((1 - core) * (first_ref.shape[0] - cols), 16)
    first = first_ref[pl.ds(far, cols), :]
    if last_ref is None:
        return first
    return jnp.where(core == 0, first, last_ref[pl.ds(far, cols), :])


def project(block_ref, norm_ref, wk_ref, wv_ref, k_ref, v_ref):
    normed = normalise(block_ref[...], *normal_of(norm_ref))
    k_ref[...] = dot(normed, wk_ref[...]).astype(BF)
    v_ref[...] = dot(normed, wv_ref[...]).astype(BF)


def join_body(cols, exponent, single, *refs):
    first_ref, refs = refs[0], refs[1:]
    last_ref, refs = (None, refs) if single else (refs[0], refs[1:])
    (norm_ref, wq_ref, wk_ref, wv_ref, q_ref, k_ref, v_ref, peak_ref, sum_ref, mix_ref,
     far_ref, all_q_ref, all_peak_ref, all_sum_ref, all_mix_ref, new_k_ref, new_v_ref) = refs
    near = q_ref.shape[0]
    far = far_rows(first_ref, last_ref, cols)
    far_ref[...] = far
    far_q = dot(normalise(far, *normal_of(norm_ref)), wq_ref[...]).astype(BF)
    project(first_ref, norm_ref, wk_ref, wv_ref, new_k_ref, new_v_ref)
    all_q_ref[:near] = q_ref[...]
    all_q_ref[near:] = far_q
    every = (all_peak_ref, all_sum_ref, all_mix_ref)
    for old, new in zip((peak_ref, sum_ref, mix_ref), every, strict=True):
        new[:near] = old[...]
    attend(
        far_q, k_ref[...], v_ref[...], exponent, *[ref.at[pl.ds(near, cols)] for ref in every]
    )


def more_body(exponent, block_ref, norm_ref, wk_ref, wv_ref, q_ref, *refs):
    old, out, new = refs[:3], refs[3:6], refs[6:9]
    k_ref, v_ref = refs[9:]
    project(block_ref, norm_ref, wk_ref, wv_ref, k_ref, v_ref)
    attend(q_ref[...], k_ref[...], v_ref[...], exponent, *new)
    merge(old, new, out, exponent, False)


def spread(act, cols):
    size = act.shape[0]
    col = lax.broadcasted_iota(jnp.int32, act.shape, 0) % cols
    left = jnp.where(col == 0, 0.0, pltpu.roll(act, 1, 0))
    right = jnp.where(col == cols - 1, 0.0, pltpu.roll(act, size - 1, 0))
    return jnp.concatenate([left.astype(BF), act.astype(BF), right.astype(BF)], axis=1)


def conv(wide_ref, taps, out_cells, cols):
    total = None
    for row in range(3):
        term = dot(wide_ref[row * cols : row * cols + out_cells, :], taps(row))
        total = term if total is None else total + term
    return total


def late_body(
    cols, exponent,
    own_ref, sib_first_ref, sib_second_ref, far_ref, block_ref, norm_ref, q_ref, peak_ref, sum_ref, mix_ref,
    k_ref, v_ref, wk_ref, wv_ref, wo_ref, taps_ref,
    even_ref, odd_ref, second_ref, wide_ref, mid_ref,
    keys_ref, values_ref, new_peak_ref, new_sum_ref, new_mix_ref, attended_ref,
):
    cells = own_ref.shape[0]
    core = core_index()
    keys_ref[:cells] = k_ref[...]
    values_ref[:cells] = v_ref[...]
    rest = pl.ds(cells, cells)
    project(block_ref, norm_ref, wk_ref, wv_ref, keys_ref.at[rest], values_ref.at[rest])
    new = (new_peak_ref, new_sum_ref, new_mix_ref)
    attend(q_ref[...], keys_ref[...], values_ref[...], exponent, *new)
    merge((peak_ref, sum_ref, mix_ref), new, (attended_ref,), exponent, True)
    change = dot(attended_ref[...], wo_ref[...])
    near = near_rows(sib_first_ref, sib_second_ref, cols)
    base = jnp.concatenate([own_ref[...], near, far_ref[...]], axis=0)
    mid = (base.astype(F32) + change).astype(BF)
    mid_ref[...] = mid[:cells]
    act = jax.nn.silu(mid.astype(F32)).astype(BF).astype(F32)
    far_act = jnp.where(far_is_inside(), act[cells + cols :], 0.0)
    above = pl.multiple_of(core * (cells + cols), 16)
    below = pl.multiple_of((1 - core) * (cells + cols), 16)
    wide_ref[cols : cols + cells] = spread(act[:cells], cols)
    wide_ref[pl.ds(below, cols), :] = spread(act[cells : cells + cols], cols)
    wide_ref[pl.ds(above, cols), :] = spread(far_act, cols)
    first_tap = conv(wide_ref, lambda row: taps_ref[0, row], cells, cols)
    second_tap = conv(wide_ref, lambda row: taps_ref[1, row], cells, cols)
    second_ref[...] = second_tap
    even_ref[...] = (first_tap + second_tap).astype(BF)
    odd_ref[...] = first_tap.astype(BF)


def now_body(
    cols, wide_ref, mid_ref, second_ref, taps_ref, skip_hbm_ref, out_ref, tap_ref, skip_ref, sems
):
    copies = [
        pltpu.make_async_copy(skip_hbm_ref, skip_ref, sems.at[0]),
        pltpu.make_async_copy(taps_ref.at[2], tap_ref, sems.at[1]),
    ]
    for copy in copies:
        copy.start()
    cells = mid_ref.shape[0]
    copies[0].wait()
    skip = dot(mid_ref[...], skip_ref[...])
    copies[1].wait()
    last_tap = conv(wide_ref, lambda row: tap_ref[row], cells, cols) + skip
    out_ref[0] = last_tap
    out_ref[1] = last_tap + second_ref[...]


def odd_body(now_ref, own_ref, arrived_ref, sum_ref):
    before = jnp.where(lax.axis_index("tm") == 0, own_ref[...], arrived_ref[...])
    sum_ref[...] = (now_ref[1] + before.astype(F32)).astype(BF)


def last_body(odd_ref, now_ref, own_ref, arrived_ref, out_ref, even_ref, sems):
    odd_copy = pltpu.make_async_copy(odd_ref, out_ref.at[1], sems.at[1])
    odd_copy.start()
    before = jnp.where(lax.axis_index("tm") == 0, own_ref[...], arrived_ref[...])
    even_ref[...] = (now_ref[0] + before.astype(F32)).astype(BF)
    even_copy = pltpu.make_async_copy(even_ref, out_ref.at[0], sems.at[0])
    even_copy.start()
    odd_copy.wait()
    even_copy.wait()


def per_device(
    features,
    norm_gain,
    query_weight,
    key_weight,
    value_weight,
    out_weight,
    conv_weight,
    skip_weight,
):
    _, tile_rows, cols, channels = features.shape
    out_channels = conv_weight.shape[-1]
    cells = tile_rows * cols
    devices = lax.axis_size("tile")
    chips = devices // 2
    swap = [(i, i ^ 1) for i in range(devices)]
    own = features.reshape(cells, channels)

    def turned(array, by, flip):
        pairs = [(i, ((i + 2 * by) % devices) ^ flip) for i in range(devices)]
        return lax.ppermute(array, "tile", pairs)

    sums, own, first, second = call(
        stats_body,
        [
            jax.ShapeDtypeStruct((8, channels), F32),
            *[jax.ShapeDtypeStruct((n, channels), BF) for n in (cells, cols, cells - cols)],
        ],
        [pltpu.SemaphoreType.DMA((PIECES,))],
        STATS_COST,
        hbm(own),
        spaces=[pltpu.HBM],
    )
    sums = [sums] + [turned(sums, by, 1) for by in range(1, chips)]
    recv = [turned(own, by, 1) for by in range(1, chips)]
    sums = jnp.concatenate(sums, axis=0)
    first, second, sums = lax.optimization_barrier((first, second, sums))
    sib = [lax.ppermute(part, "tile", swap) for part in (first, second)]
    sums = [sums, lax.ppermute(sums, "tile", swap)]

    exponent = channels ** (-0.5) * 1.4426950408889634
    near = cells + cols
    every = near + cols
    taps = conv_weight.reshape(3, 3, 3 * channels, out_channels)
    first_taps = (2, *taps.shape[1:])
    weights = [norm_gain.reshape(1, channels), query_weight, key_weight, value_weight]
    held = call(
        stage_body,
        [jax.ShapeDtypeStruct(w.shape, w.dtype) for w in weights],
        [pltpu.SemaphoreType.DMA((len(weights),))],
        STAGE_COST,
        sums[0], *[hbm(w) for w in weights],
        spaces=[VMEM] + [pltpu.HBM] * len(weights),
    )
    _, wq, wk, wv = held

    def rows_of(rows, kind=BF, width=channels):
        return jax.ShapeDtypeStruct((rows, width), kind)

    def state_of(rows):
        return [rows_of(rows, F32, 128), rows_of(rows, F32, 128), rows_of(rows, F32)]

    def scratch_of(shapes):
        return [VMEM(shape.shape, shape.dtype) for shape in shapes]

    n_sums = len(sums)
    norm, q, k, v, *rest = call(
        functools.partial(early_body, devices * cells, cols, exponent, n_sums),
        [
            rows_of(8, F32),
            rows_of(near),
            rows_of(2 * cells),
            rows_of(2 * cells),
            *state_of(near),
            jax.ShapeDtypeStruct(out_weight.shape, BF),
            jax.ShapeDtypeStruct(first_taps, BF),
        ],
        [pltpu.SemaphoreType.DMA((2,))],
        EARLY_COST,
        own, *sib, *sums, *held, hbm(out_weight), hbm(taps),
        spaces=[VMEM] * (7 + n_sums) + [pltpu.HBM] * 2,
    )
    state, (wo, held_taps) = rest[:3], rest[3:]

    *recv, norm = lax.optimization_barrier((*recv, norm))
    rsib = [lax.ppermute(block, "tile", swap) for block in recv]
    ends = recv[:1] if chips == 2 else [recv[0], recv[-1]]
    far, q, *state, new_k, new_v = call(
        functools.partial(join_body, cols, exponent, chips == 2),
        [rows_of(cols), rows_of(every), *state_of(every), rows_of(cells), rows_of(cells)],
        [],
        JOIN_COST,
        *ends, norm, wq, wk, wv, q, k, v, *state,
    )
    for block in recv[1:] + rsib[:-1]:
        state = call(
            functools.partial(more_body, exponent),
            state_of(every),
            scratch_of([*state_of(every), rows_of(cells), rows_of(cells)]),
            10**9,
            block, norm, wk, wv, q, *state,
        )
    even, odd, second, wide, mid = call(
        functools.partial(late_body, cols, exponent),
        [
            rows_of(cells, BF, out_channels),
            rows_of(cells, BF, out_channels),
            rows_of(cells, F32, out_channels),
            rows_of(every, BF, 3 * channels),
            rows_of(cells),
        ],
        scratch_of([rows_of(2 * cells), rows_of(2 * cells), *state_of(every), rows_of(every)]),
        LATE_COST,
        own, *sib, far, rsib[-1], norm, q, *state, new_k, new_v, wk, wv, wo, held_taps,
    )
    spans = lax.axis_size("tm")
    arrived_odd = lax.ppermute(odd, "tm", [(i, (i + 1) % spans) for i in range(spans)])
    arrived_even = lax.ppermute(even, "tm", [(i, i + 1) for i in range(spans - 1)])
    both = jax.ShapeDtypeStruct((2, cells, out_channels), F32)
    now = call(
        functools.partial(now_body, cols),
        both,
        [
            VMEM(taps.shape[1:], BF),
            VMEM(skip_weight.shape, BF),
            pltpu.SemaphoreType.DMA((2,)),
        ],
        NOW_COST,
        wide, mid, second, hbm(taps), hbm(skip_weight),
        spaces=[VMEM] * 3 + [pltpu.HBM] * 2,
    )
    share = rows_of(cells, BF, out_channels)
    done_odd = call(odd_body, share, [], 1, now, odd, arrived_odd)
    done_odd, arrived_even = lax.optimization_barrier((done_odd, arrived_even))
    decoded = pl.pallas_call(
        last_body,
        out_shape=jax.ShapeDtypeStruct((2, cells, out_channels), BF),
        in_specs=[spec()] * 4,
        out_specs=spec(pltpu.HBM),
        scratch_shapes=[VMEM((cells, out_channels), BF), pltpu.SemaphoreType.DMA((2,))],
        compiler_params=pltpu.CompilerParams(vmem_limit_bytes=LIMIT),
    )(done_odd, now, even, arrived_even)
    return decoded.reshape(2, tile_rows, cols, out_channels)


def solution(mesh):
    in_specs = (P("tm", "tile", None, None), P(), P(), P(), P(), P(), P(), P())
    out_specs = P("tm", "tile", None, None)
    return jax.shard_map(
        per_device, mesh=mesh, in_specs=in_specs, out_specs=out_specs, check_vma=False
    )
```

```python
import functools

import jax
import jax.numpy as jnp
from jax import lax
from jax.experimental import pallas as pl
from jax.experimental.pallas import tpu as pltpu
from jax.sharding import PartitionSpec as P

GROUPS = 32
BF = jnp.bfloat16
F32 = jnp.float32
VMEM = pltpu.VMEM
LIMIT = 12 * 1024 * 1024
PIECES = 8
STATS_COST = 1 << 6
STAGE_COST = 1 << 4
EARLY_COST = 7 * 10**8
JOIN_COST = LATE_COST = NOW_COST = 1 << 15


def dot(left, right):
    return jnp.dot(left, right, preferred_element_type=F32)


def dot_t(left, right):
    return lax.dot_general(left, right, (((1,), (1,)), ((), ())), preferred_element_type=F32)


def spec(space=VMEM):
    return pl.BlockSpec(memory_space=space)


def hbm(array):
    return pltpu.with_memory_space_constraint(array, pltpu.HBM)


def call(body, outs, scratch, cost, *args, spaces=None):
    spaces = spaces or [VMEM] * len(args)
    return pl.pallas_call(
        body,
        out_shape=outs,
        in_specs=[spec(s) for s in spaces],
        out_specs=jax.tree.map(lambda _: spec(), outs),
        scratch_shapes=scratch,
        compiler_params=pltpu.CompilerParams(vmem_limit_bytes=LIMIT),
        cost_estimate=pl.CostEstimate(flops=cost, bytes_accessed=1 << 10, transcendentals=0),
    )(*args)


def core_index():
    return lax.axis_index("tile") % 2


def far_is_inside():
    me = lax.axis_index("tile")
    core = me % 2
    last = lax.axis_size("tile") - 1
    return me != core * last


def stats_body(features_ref, sums_ref, own_ref, first_ref, second_ref, sems):
    rows = own_ref.shape[0] // PIECES
    copies = []
    for i in range(PIECES):
        piece = pl.ds(i * rows, rows)
        copies.append(
            pltpu.make_async_copy(features_ref.at[piece], own_ref.at[piece], sems.at[i])
        )
        copies[-1].start()
    total = jnp.zeros((1, own_ref.shape[1]), F32)
    squared = total
    for i in range(PIECES):
        copies[i].wait()
        block = own_ref[i * rows : (i + 1) * rows].astype(F32)
        total += jnp.sum(block, axis=0, keepdims=True)
        squared += jnp.sum(block * block, axis=0, keepdims=True)
    sums_ref[...] = jnp.concatenate(
        [total, squared, jnp.zeros((6, own_ref.shape[1]), F32)], axis=0
    )
    first = first_ref.shape[0]
    first_ref[...] = own_ref[:first]
    second_ref[...] = own_ref[first:]


def near_rows(first_ref, second_ref, cols):
    return jnp.where(core_index() == 0, first_ref[:cols], second_ref[second_ref.shape[0] - cols :])


def group_sums(sums, width):
    lane = lax.broadcasted_iota(jnp.int32, sums.shape, 1)
    size = sums.shape[1]
    step = 1
    while step < width:
        low = pltpu.roll(sums, size - step, 1)
        high = pltpu.roll(sums, step, 1)
        sums = sums + jnp.where((lane & step) == 0, low, high)
        step *= 2
    return sums


def moments(sum_refs, cells):
    sums = 0.0
    for ref in sum_refs:
        for first in range(0, ref.shape[0], 8):
            sums = sums + ref[first : first + 8]
    width = sums.shape[1] // GROUPS
    sums = group_sums(sums, width)
    population = cells * width
    mean = sums[0:1] / population
    var = sums[1:2] / population - mean * mean
    return mean, lax.rsqrt(var + 1e-06)


def normalise(block, mean, inverse, gain):
    return ((block.astype(F32) - mean) * inverse * gain).astype(BF)


def attend(queries, keys, values, exponent, peak_ref, sum_ref, mix_ref):
    scores = dot_t(queries, keys)
    if callable(values):
        values = values()
    peak = jnp.max(scores, axis=1, keepdims=True)
    unnormed = jnp.exp2((scores - peak) * exponent)
    peak_ref[...] = jnp.broadcast_to(peak, peak_ref.shape)
    sum_ref[...] = jnp.broadcast_to(jnp.sum(unnormed, axis=1, keepdims=True), sum_ref.shape)
    mix_ref[...] = dot(unnormed.astype(BF), values)


def merge(old, new, out_refs, exponent, last):
    peak = jnp.maximum(old[0][...], new[0][...])
    fade_old = jnp.exp2((old[0][...] - peak) * exponent)
    fade_new = jnp.exp2((new[0][...] - peak) * exponent)
    total = old[1][...] * fade_old + new[1][...] * fade_new
    if last:
        scale = 1.0 / total
        fade_old = fade_old * scale
        fade_new = fade_new * scale
    else:
        out_refs[0][...] = peak
        out_refs[1][...] = total
    width = peak.shape[1]
    for first in range(0, old[2].shape[1], width):
        lanes = slice(first, first + width)
        mixed = old[2][:, lanes] * fade_old + new[2][:, lanes] * fade_new
        out_refs[-1][:, lanes] = mixed.astype(out_refs[-1].dtype)


def stage_body(*refs):
    refs, sems = refs[1:-1], refs[-1]
    count = len(refs) // 2
    copies = [
        pltpu.make_async_copy(refs[i], refs[count + i], sems.at[i]) for i in range(count)
    ]
    for copy in copies:
        copy.start()
    for copy in copies:
        copy.wait()


def early_body(
    cells_all, cols, exponent, n_sums,
    own_ref, sib_first_ref, sib_second_ref, *refs,
):
    sum_refs, refs = refs[:n_sums], refs[n_sums:]
    gain_ref, wq_ref, wk_ref, wv_ref, wo_hbm_ref, taps_hbm_ref, refs = *refs[:6], refs[6:]
    norm_ref, q_ref, k_ref, v_ref, *state_refs = refs[:7]
    wo_ref, taps_ref, sems = refs[7:]
    copies = [
        pltpu.make_async_copy(wo_hbm_ref, wo_ref, sems.at[0]),
        pltpu.make_async_copy(taps_hbm_ref.at[pl.ds(0, 2)], taps_ref, sems.at[1]),
    ]
    for copy in copies:
        copy.start()
    mean, inverse = moments(sum_refs, cells_all)
    gain = gain_ref[...]
    norm_ref[...] = jnp.concatenate(
        [mean, inverse, gain, jnp.zeros((5, mean.shape[1]), F32)], axis=0
    )
    own = normalise(own_ref[...], mean, inverse, gain)
    sib = jnp.concatenate([sib_first_ref[...], sib_second_ref[...]], axis=0)
    sib = normalise(sib, mean, inverse, gain)
    halo = normalise(near_rows(sib_first_ref, sib_second_ref, cols), mean, inverse, gain)
    both = jnp.concatenate([own, sib], axis=0)
    q_ref[...] = dot(jnp.concatenate([own, halo], axis=0), wq_ref[...]).astype(BF)
    k_ref[...] = dot(both, wk_ref[...]).astype(BF)

    def values():
        v_ref[...] = dot(both, wv_ref[...]).astype(BF)
        return v_ref[...]

    attend(q_ref[...], k_ref[...], values, exponent, *state_refs)
    for copy in copies:
        copy.wait()


def normal_of(norm_ref):
    return norm_ref[0:1], norm_ref[1:2], norm_ref[2:3]


def far_rows(first_ref, last_ref, cols):
    core = core_index()
    far = pl.multiple_of((1 - core) * (first_ref.shape[0] - cols), 16)
    first = first_ref[pl.ds(far, cols), :]
    if last_ref is None:
        return first
    return jnp.where(core == 0, first, last_ref[pl.ds(far, cols), :])


def project(block_ref, norm_ref, wk_ref, wv_ref, k_ref, v_ref):
    normed = normalise(block_ref[...], *normal_of(norm_ref))
    k_ref[...] = dot(normed, wk_ref[...]).astype(BF)
    v_ref[...] = dot(normed, wv_ref[...]).astype(BF)


def join_body(cols, exponent, single, *refs):
    first_ref, refs = refs[0], refs[1:]
    last_ref, refs = (None, refs) if single else (refs[0], refs[1:])
    (norm_ref, wq_ref, wk_ref, wv_ref, q_ref, k_ref, v_ref, peak_ref, sum_ref, mix_ref,
     far_ref, all_q_ref, all_peak_ref, all_sum_ref, all_mix_ref, new_k_ref, new_v_ref) = refs
    near = q_ref.shape[0]
    far = far_rows(first_ref, last_ref, cols)
    far_ref[...] = far
    far_q = dot(normalise(far, *normal_of(norm_ref)), wq_ref[...]).astype(BF)
    all_q_ref[:near] = q_ref[...]
    all_q_ref[near:] = far_q
    every = (all_peak_ref, all_sum_ref, all_mix_ref)
    for old, new in zip((peak_ref, sum_ref, mix_ref), every, strict=True):
        new[:near] = old[...]

    def values():
        project(first_ref, norm_ref, wk_ref, wv_ref, new_k_ref, new_v_ref)
        return v_ref[...]

    attend(far_q, k_ref[...], values, exponent, *[ref.at[pl.ds(near, cols)] for ref in every])


def more_body(exponent, block_ref, norm_ref, wk_ref, wv_ref, q_ref, *refs):
    old, out, new = refs[:3], refs[3:6], refs[6:9]
    k_ref, v_ref = refs[9:]
    project(block_ref, norm_ref, wk_ref, wv_ref, k_ref, v_ref)
    attend(q_ref[...], k_ref[...], v_ref[...], exponent, *new)
    merge(old, new, out, exponent, False)


def spread(act, cols):
    size = act.shape[0]
    col = lax.broadcasted_iota(jnp.int32, act.shape, 0) % cols
    left = jnp.where(col == 0, 0.0, pltpu.roll(act, 1, 0))
    right = jnp.where(col == cols - 1, 0.0, pltpu.roll(act, size - 1, 0))
    return jnp.concatenate([left.astype(BF), act.astype(BF), right.astype(BF)], axis=1)


def conv(wide_ref, taps, out_cells, cols):
    total = None
    for row in range(3):
        term = dot(wide_ref[row * cols : row * cols + out_cells, :], taps(row))
        total = term if total is None else total + term
    return total


def late_body(
    cols, exponent,
    own_ref, sib_first_ref, sib_second_ref, far_ref, block_ref, norm_ref, q_ref, peak_ref, sum_ref, mix_ref,
    k_ref, v_ref, wk_ref, wv_ref, wo_ref, taps_ref,
    even_ref, odd_ref, second_ref, wide_ref, mid_ref,
    keys_ref, values_ref, new_peak_ref, new_sum_ref, new_mix_ref, attended_ref,
):
    cells = own_ref.shape[0]
    core = core_index()
    normed = normalise(block_ref[...], *normal_of(norm_ref))
    keys_ref[:cells] = k_ref[...]
    keys_ref[cells:] = dot(normed, wk_ref[...]).astype(BF)

    def values():
        values_ref[:cells] = v_ref[...]
        values_ref[cells:] = dot(normed, wv_ref[...]).astype(BF)
        return values_ref[...]

    new = (new_peak_ref, new_sum_ref, new_mix_ref)
    attend(q_ref[...], keys_ref[...], values, exponent, *new)
    merge((peak_ref, sum_ref, mix_ref), new, (attended_ref,), exponent, True)
    change = dot(attended_ref[...], wo_ref[...])
    near = near_rows(sib_first_ref, sib_second_ref, cols)
    base = jnp.concatenate([own_ref[...], near, far_ref[...]], axis=0)
    mid = (base.astype(F32) + change).astype(BF)
    mid_ref[...] = mid[:cells]
    act = jax.nn.silu(mid.astype(F32)).astype(BF).astype(F32)
    far_act = jnp.where(far_is_inside(), act[cells + cols :], 0.0)
    above = pl.multiple_of(core * (cells + cols), 16)
    below = pl.multiple_of((1 - core) * (cells + cols), 16)
    for row in range(0, cells, cols):
        wide_ref[cols + row : 2 * cols + row] = spread(act[row : row + cols], cols)
    wide_ref[pl.ds(below, cols), :] = spread(act[cells : cells + cols], cols)
    wide_ref[pl.ds(above, cols), :] = spread(far_act, cols)
    first_tap = conv(wide_ref, lambda row: taps_ref[0, row], cells, cols)
    second_tap = conv(wide_ref, lambda row: taps_ref[1, row], cells, cols)
    second_ref[...] = second_tap
    even_ref[...] = (first_tap + second_tap).astype(BF)
    odd_ref[...] = first_tap.astype(BF)


def now_body(
    cols, wide_ref, mid_ref, second_ref, taps_ref, skip_hbm_ref, out_ref, tap_ref, skip_ref, sems
):
    copies = [
        pltpu.make_async_copy(skip_hbm_ref, skip_ref, sems.at[0]),
        pltpu.make_async_copy(taps_ref.at[2], tap_ref, sems.at[1]),
    ]
    for copy in copies:
        copy.start()
    cells = mid_ref.shape[0]
    copies[0].wait()
    skip = dot(mid_ref[...], skip_ref[...])
    copies[1].wait()
    last_tap = conv(wide_ref, lambda row: tap_ref[row], cells, cols) + skip
    out_ref[0] = last_tap
    out_ref[1] = last_tap + second_ref[...]


def odd_body(now_ref, own_ref, arrived_ref, sum_ref):
    before = jnp.where(lax.axis_index("tm") == 0, own_ref[...], arrived_ref[...])
    sum_ref[...] = (now_ref[1] + before.astype(F32)).astype(BF)


def last_body(odd_ref, now_ref, own_ref, arrived_ref, out_ref, even_ref, sems):
    odd_copy = pltpu.make_async_copy(odd_ref, out_ref.at[1], sems.at[1])
    odd_copy.start()
    before = jnp.where(lax.axis_index("tm") == 0, own_ref[...], arrived_ref[...])
    even_ref[...] = (now_ref[0] + before.astype(F32)).astype(BF)
    even_copy = pltpu.make_async_copy(even_ref, out_ref.at[0], sems.at[0])
    even_copy.start()
    odd_copy.wait()
    even_copy.wait()


def per_device(
    features,
    norm_gain,
    query_weight,
    key_weight,
    value_weight,
    out_weight,
    conv_weight,
    skip_weight,
):
    _, tile_rows, cols, channels = features.shape
    out_channels = conv_weight.shape[-1]
    cells = tile_rows * cols
    devices = lax.axis_size("tile")
    chips = devices // 2
    swap = [(i, i ^ 1) for i in range(devices)]
    own = features.reshape(cells, channels)

    def turned(array, by, flip):
        pairs = [(i, ((i + 2 * by) % devices) ^ flip) for i in range(devices)]
        return lax.ppermute(array, "tile", pairs)

    sums, own, first, second = call(
        stats_body,
        [
            jax.ShapeDtypeStruct((8, channels), F32),
            *[jax.ShapeDtypeStruct((n, channels), BF) for n in (cells, cols, cells - cols)],
        ],
        [pltpu.SemaphoreType.DMA((PIECES,))],
        STATS_COST,
        hbm(own),
        spaces=[pltpu.HBM],
    )
    sums = [sums] + [turned(sums, by, 1) for by in range(1, chips)]
    recv = [turned(own, by, 1) for by in range(1, chips)]
    sums = jnp.concatenate(sums, axis=0)
    first, second, sums = lax.optimization_barrier((first, second, sums))
    sib = [lax.ppermute(part, "tile", swap) for part in (first, second)]
    sums = [sums, lax.ppermute(sums, "tile", swap)]

    exponent = channels ** (-0.5) * 1.4426950408889634
    near = cells + cols
    every = near + cols
    taps = conv_weight.reshape(3, 3, 3 * channels, out_channels)
    first_taps = (2, *taps.shape[1:])
    weights = [norm_gain.reshape(1, channels), query_weight, key_weight, value_weight]
    held = call(
        stage_body,
        [jax.ShapeDtypeStruct(w.shape, w.dtype) for w in weights],
        [pltpu.SemaphoreType.DMA((len(weights),))],
        STAGE_COST,
        sums[0], *[hbm(w) for w in weights],
        spaces=[VMEM] + [pltpu.HBM] * len(weights),
    )
    _, wq, wk, wv = held

    def rows_of(rows, kind=BF, width=channels):
        return jax.ShapeDtypeStruct((rows, width), kind)

    def state_of(rows):
        return [rows_of(rows, F32, 128), rows_of(rows, F32, 128), rows_of(rows, F32)]

    def scratch_of(shapes):
        return [VMEM(shape.shape, shape.dtype) for shape in shapes]

    n_sums = len(sums)
    norm, q, k, v, *rest = call(
        functools.partial(early_body, devices * cells, cols, exponent, n_sums),
        [
            rows_of(8, F32),
            rows_of(near),
            rows_of(2 * cells),
            rows_of(2 * cells),
            *state_of(near),
            jax.ShapeDtypeStruct(out_weight.shape, BF),
            jax.ShapeDtypeStruct(first_taps, BF),
        ],
        [pltpu.SemaphoreType.DMA((2,))],
        EARLY_COST,
        own, *sib, *sums, *held, hbm(out_weight), hbm(taps),
        spaces=[VMEM] * (7 + n_sums) + [pltpu.HBM] * 2,
    )
    state, (wo, held_taps) = rest[:3], rest[3:]

    *recv, norm = lax.optimization_barrier((*recv, norm))
    rsib = [lax.ppermute(block, "tile", swap) for block in recv]
    ends = recv[:1] if chips == 2 else [recv[0], recv[-1]]
    far, q, *state, new_k, new_v = call(
        functools.partial(join_body, cols, exponent, chips == 2),
        [rows_of(cols), rows_of(every), *state_of(every), rows_of(cells), rows_of(cells)],
        [],
        JOIN_COST,
        *ends, norm, wq, wk, wv, q, k, v, *state,
    )
    for block in recv[1:] + rsib[:-1]:
        state = call(
            functools.partial(more_body, exponent),
            state_of(every),
            scratch_of([*state_of(every), rows_of(cells), rows_of(cells)]),
            10**9,
            block, norm, wk, wv, q, *state,
        )
    even, odd, second, wide, mid = call(
        functools.partial(late_body, cols, exponent),
        [
            rows_of(cells, BF, out_channels),
            rows_of(cells, BF, out_channels),
            rows_of(cells, F32, out_channels),
            rows_of(every, BF, 3 * channels),
            rows_of(cells),
        ],
        scratch_of([rows_of(2 * cells), rows_of(2 * cells), *state_of(every), rows_of(every)]),
        LATE_COST,
        own, *sib, far, rsib[-1], norm, q, *state, new_k, new_v, wk, wv, wo, held_taps,
    )
    spans = lax.axis_size("tm")
    arrived_odd = lax.ppermute(odd, "tm", [(i, (i + 1) % spans) for i in range(spans)])
    arrived_even = lax.ppermute(even, "tm", [(i, i + 1) for i in range(spans - 1)])
    both = jax.ShapeDtypeStruct((2, cells, out_channels), F32)
    now = call(
        functools.partial(now_body, cols),
        both,
        [
            VMEM(taps.shape[1:], BF),
            VMEM(skip_weight.shape, BF),
            pltpu.SemaphoreType.DMA((2,)),
        ],
        NOW_COST,
        wide, mid, second, hbm(taps), hbm(skip_weight),
        spaces=[VMEM] * 3 + [pltpu.HBM] * 2,
    )
    share = rows_of(cells, BF, out_channels)
    done_odd = call(odd_body, share, [], 1, now, odd, arrived_odd)
    done_odd, arrived_even = lax.optimization_barrier((done_odd, arrived_even))
    decoded = pl.pallas_call(
        last_body,
        out_shape=jax.ShapeDtypeStruct((2, cells, out_channels), BF),
        in_specs=[spec()] * 4,
        out_specs=spec(pltpu.HBM),
        scratch_shapes=[VMEM((cells, out_channels), BF), pltpu.SemaphoreType.DMA((2,))],
        compiler_params=pltpu.CompilerParams(vmem_limit_bytes=LIMIT),
    )(done_odd, now, even, arrived_even)
    return decoded.reshape(2, tile_rows, cols, out_channels)


def solution(mesh):
    in_specs = (P("tm", "tile", None, None), P(), P(), P(), P(), P(), P(), P())
    out_specs = P("tm", "tile", None, None)
    return jax.shard_map(
        per_device, mesh=mesh, in_specs=in_specs, out_specs=out_specs, check_vma=False
    )
```

```python
import functools

import jax
import jax.numpy as jnp
from jax import lax
from jax.experimental import pallas as pl
from jax.experimental.pallas import tpu as pltpu
from jax.sharding import PartitionSpec as P

GROUPS = 32
BF = jnp.bfloat16
F32 = jnp.float32
VMEM = pltpu.VMEM
LIMIT = 12 * 1024 * 1024
PIECES = 5
STATS_COST = 1 << 6
STAGE_COST = 1 << 4
EARLY_COST = 7 * 10**8
JOIN_COST = LATE_COST = NOW_COST = 1 << 15


def dot(left, right):
    return jnp.dot(left, right, preferred_element_type=F32)


def dot_t(left, right):
    return lax.dot_general(left, right, (((1,), (1,)), ((), ())), preferred_element_type=F32)


def spec(space=VMEM):
    return pl.BlockSpec(memory_space=space)


def hbm(array):
    return pltpu.with_memory_space_constraint(array, pltpu.HBM)


def call(body, outs, scratch, cost, *args, spaces=None):
    spaces = spaces or [VMEM] * len(args)
    return pl.pallas_call(
        body,
        out_shape=outs,
        in_specs=[spec(s) for s in spaces],
        out_specs=jax.tree.map(lambda _: spec(), outs),
        scratch_shapes=scratch,
        compiler_params=pltpu.CompilerParams(vmem_limit_bytes=LIMIT),
        cost_estimate=pl.CostEstimate(flops=cost, bytes_accessed=1 << 10, transcendentals=0),
    )(*args)


def core_index():
    return lax.axis_index("tile") % 2


def far_is_inside():
    me = lax.axis_index("tile")
    core = me % 2
    last = lax.axis_size("tile") - 1
    return me != core * last


def stats_body(features_ref, sums_ref, own_ref, first_ref, second_ref, sems):
    rows = own_ref.shape[0] // PIECES
    copies = []
    for i in range(PIECES):
        piece = pl.ds(i * rows, rows)
        copies.append(
            pltpu.make_async_copy(features_ref.at[piece], own_ref.at[piece], sems.at[i])
        )
        copies[-1].start()
    total = jnp.zeros((1, own_ref.shape[1]), F32)
    squared = total
    for i in range(PIECES):
        copies[i].wait()
        block = own_ref[i * rows : (i + 1) * rows].astype(F32)
        total += jnp.sum(block, axis=0, keepdims=True)
        squared += jnp.sum(block * block, axis=0, keepdims=True)
    sums_ref[...] = jnp.concatenate(
        [total, squared, jnp.zeros((6, own_ref.shape[1]), F32)], axis=0
    )
    first = first_ref.shape[0]
    first_ref[...] = own_ref[:first]
    second_ref[...] = own_ref[first:]


def near_rows(first_ref, second_ref, cols):
    return jnp.where(core_index() == 0, first_ref[:cols], second_ref[second_ref.shape[0] - cols :])


def group_sums(sums, width):
    lane = lax.broadcasted_iota(jnp.int32, sums.shape, 1)
    size = sums.shape[1]
    step = 1
    while step < width:
        low = pltpu.roll(sums, size - step, 1)
        high = pltpu.roll(sums, step, 1)
        sums = sums + jnp.where((lane & step) == 0, low, high)
        step *= 2
    return sums


def moments(sum_refs, cells):
    sums = 0.0
    for ref in sum_refs:
        for first in range(0, ref.shape[0], 8):
            sums = sums + ref[first : first + 8]
    width = sums.shape[1] // GROUPS
    sums = group_sums(sums, width)
    population = cells * width
    mean = sums[0:1] / population
    var = sums[1:2] / population - mean * mean
    return mean, lax.rsqrt(var + 1e-06)


def normalise(block, mean, inverse, gain):
    return ((block.astype(F32) - mean) * inverse * gain).astype(BF)


def attend(queries, keys, values, exponent, peak_ref, sum_ref, mix_ref):
    scores = dot_t(queries, keys)
    if callable(values):
        values = values()
    peak = jnp.max(scores, axis=1, keepdims=True)
    unnormed = jnp.exp2((scores - peak) * exponent)
    peak_ref[...] = jnp.broadcast_to(peak, peak_ref.shape)
    sum_ref[...] = jnp.broadcast_to(jnp.sum(unnormed, axis=1, keepdims=True), sum_ref.shape)
    mix_ref[...] = dot(unnormed.astype(BF), values)


def merge(old, new, out_refs, exponent, last):
    peak = jnp.maximum(old[0][...], new[0][...])
    fade_old = jnp.exp2((old[0][...] - peak) * exponent)
    fade_new = jnp.exp2((new[0][...] - peak) * exponent)
    total = old[1][...] * fade_old + new[1][...] * fade_new
    if last:
        scale = 1.0 / total
        fade_old = fade_old * scale
        fade_new = fade_new * scale
    else:
        out_refs[0][...] = peak
        out_refs[1][...] = total
    width = peak.shape[1]
    for first in range(0, old[2].shape[1], width):
        lanes = slice(first, first + width)
        mixed = old[2][:, lanes] * fade_old + new[2][:, lanes] * fade_new
        out_refs[-1][:, lanes] = mixed.astype(out_refs[-1].dtype)


def stage_body(*refs):
    refs, sems = refs[1:-1], refs[-1]
    count = len(refs) // 2
    copies = [
        pltpu.make_async_copy(refs[i], refs[count + i], sems.at[i]) for i in range(count)
    ]
    for copy in copies:
        copy.start()
    for copy in copies:
        copy.wait()


def early_body(
    cells_all, cols, exponent, n_sums,
    own_ref, sib_first_ref, sib_second_ref, *refs,
):
    sum_refs, refs = refs[:n_sums], refs[n_sums:]
    gain_ref, wq_ref, wk_ref, wv_ref, wo_hbm_ref, taps_hbm_ref, refs = *refs[:6], refs[6:]
    norm_ref, q_ref, k_ref, v_ref, *state_refs = refs[:7]
    wo_ref, taps_ref, sems = refs[7:]
    copies = [
        pltpu.make_async_copy(wo_hbm_ref, wo_ref, sems.at[0]),
        pltpu.make_async_copy(taps_hbm_ref.at[pl.ds(0, 2)], taps_ref, sems.at[1]),
    ]
    for copy in copies:
        copy.start()
    mean, inverse = moments(sum_refs, cells_all)
    gain = gain_ref[...]
    norm_ref[...] = jnp.concatenate(
        [mean, inverse, gain, jnp.zeros((5, mean.shape[1]), F32)], axis=0
    )
    own = normalise(own_ref[...], mean, inverse, gain)
    sib = jnp.concatenate([sib_first_ref[...], sib_second_ref[...]], axis=0)
    sib = normalise(sib, mean, inverse, gain)
    halo = normalise(near_rows(sib_first_ref, sib_second_ref, cols), mean, inverse, gain)
    both = jnp.concatenate([own, sib], axis=0)
    q_ref[...] = dot(jnp.concatenate([own, halo], axis=0), wq_ref[...]).astype(BF)
    k_ref[...] = dot(both, wk_ref[...]).astype(BF)

    def values():
        v_ref[...] = dot(both, wv_ref[...]).astype(BF)
        return v_ref[...]

    attend(q_ref[...], k_ref[...], values, exponent, *state_refs)
    for copy in copies:
        copy.wait()


def normal_of(norm_ref):
    return norm_ref[0:1], norm_ref[1:2], norm_ref[2:3]


def far_rows(first_ref, last_ref, cols):
    core = core_index()
    far = pl.multiple_of((1 - core) * (first_ref.shape[0] - cols), 16)
    first = first_ref[pl.ds(far, cols), :]
    if last_ref is None:
        return first
    return jnp.where(core == 0, first, last_ref[pl.ds(far, cols), :])


def project(block_ref, norm_ref, wk_ref, wv_ref, k_ref, v_ref):
    normed = normalise(block_ref[...], *normal_of(norm_ref))
    k_ref[...] = dot(normed, wk_ref[...]).astype(BF)
    v_ref[...] = dot(normed, wv_ref[...]).astype(BF)


def join_body(cols, exponent, single, *refs):
    first_ref, refs = refs[0], refs[1:]
    last_ref, refs = (None, refs) if single else (refs[0], refs[1:])
    (norm_ref, wq_ref, wk_ref, wv_ref, q_ref, k_ref, v_ref, peak_ref, sum_ref, mix_ref,
     far_ref, all_q_ref, all_peak_ref, all_sum_ref, all_mix_ref, new_k_ref, new_v_ref) = refs
    near = q_ref.shape[0]
    far = far_rows(first_ref, last_ref, cols)
    far_ref[...] = far
    far_q = dot(normalise(far, *normal_of(norm_ref)), wq_ref[...]).astype(BF)
    all_q_ref[:near] = q_ref[...]
    all_q_ref[near:] = far_q
    every = (all_peak_ref, all_sum_ref, all_mix_ref)
    for old, new in zip((peak_ref, sum_ref, mix_ref), every, strict=True):
        new[:near] = old[...]

    def values():
        project(first_ref, norm_ref, wk_ref, wv_ref, new_k_ref, new_v_ref)
        return v_ref[...]

    attend(far_q, k_ref[...], values, exponent, *[ref.at[pl.ds(near, cols)] for ref in every])


def more_body(exponent, block_ref, norm_ref, wk_ref, wv_ref, q_ref, *refs):
    old, out, new = refs[:3], refs[3:6], refs[6:9]
    k_ref, v_ref = refs[9:]
    project(block_ref, norm_ref, wk_ref, wv_ref, k_ref, v_ref)
    attend(q_ref[...], k_ref[...], v_ref[...], exponent, *new)
    merge(old, new, out, exponent, False)


def spread(act, cols):
    size = act.shape[0]
    col = lax.broadcasted_iota(jnp.int32, act.shape, 0) % cols
    left = jnp.where(col == 0, 0.0, pltpu.roll(act, 1, 0))
    right = jnp.where(col == cols - 1, 0.0, pltpu.roll(act, size - 1, 0))
    return jnp.concatenate([left.astype(BF), act.astype(BF), right.astype(BF)], axis=1)


def conv(wide_ref, taps, out_cells, cols):
    total = None
    for row in range(3):
        term = dot(wide_ref[row * cols : row * cols + out_cells, :], taps(row))
        total = term if total is None else total + term
    return total


def late_body(
    cols, exponent,
    own_ref, sib_first_ref, sib_second_ref, far_ref, block_ref, norm_ref, q_ref, peak_ref, sum_ref, mix_ref,
    k_ref, v_ref, wk_ref, wv_ref, wo_ref, taps_ref,
    even_ref, odd_ref, second_ref, wide_ref, mid_ref,
    keys_ref, values_ref, new_peak_ref, new_sum_ref, new_mix_ref, attended_ref,
):
    cells = own_ref.shape[0]
    core = core_index()
    normed = normalise(block_ref[...], *normal_of(norm_ref))
    keys_ref[:cells] = k_ref[...]
    keys_ref[cells:] = dot(normed, wk_ref[...]).astype(BF)

    def values():
        values_ref[:cells] = v_ref[...]
        values_ref[cells:] = dot(normed, wv_ref[...]).astype(BF)
        return values_ref[...]

    new = (new_peak_ref, new_sum_ref, new_mix_ref)
    attend(q_ref[...], keys_ref[...], values, exponent, *new)
    merge((peak_ref, sum_ref, mix_ref), new, (attended_ref,), exponent, True)
    change = dot(attended_ref[...], wo_ref[...])
    near = near_rows(sib_first_ref, sib_second_ref, cols)
    base = jnp.concatenate([own_ref[...], near, far_ref[...]], axis=0)
    mid = (base.astype(F32) + change).astype(BF)
    mid_ref[...] = mid[:cells]
    act = jax.nn.silu(mid.astype(F32)).astype(BF).astype(F32)
    far_act = jnp.where(far_is_inside(), act[cells + cols :], 0.0)
    above = pl.multiple_of(core * (cells + cols), 16)
    below = pl.multiple_of((1 - core) * (cells + cols), 16)
    for row in range(0, cells, cols):
        wide_ref[cols + row : 2 * cols + row] = spread(act[row : row + cols], cols)
    wide_ref[pl.ds(below, cols), :] = spread(act[cells : cells + cols], cols)
    wide_ref[pl.ds(above, cols), :] = spread(far_act, cols)
    first_tap = conv(wide_ref, lambda row: taps_ref[0, row], cells, cols)
    second_tap = conv(wide_ref, lambda row: taps_ref[1, row], cells, cols)
    second_ref[...] = second_tap
    even_ref[...] = (first_tap + second_tap).astype(BF)
    odd_ref[...] = first_tap.astype(BF)


def now_body(
    cols, wide_ref, mid_ref, second_ref, taps_ref, skip_hbm_ref, out_ref, tap_ref, skip_ref, sems
):
    copies = [
        pltpu.make_async_copy(skip_hbm_ref, skip_ref, sems.at[0]),
        pltpu.make_async_copy(taps_ref.at[2], tap_ref, sems.at[1]),
    ]
    for copy in copies:
        copy.start()
    cells = mid_ref.shape[0]
    copies[0].wait()
    skip = dot(mid_ref[...], skip_ref[...])
    copies[1].wait()
    last_tap = conv(wide_ref, lambda row: tap_ref[row], cells, cols) + skip
    out_ref[0] = last_tap
    out_ref[1] = last_tap + second_ref[...]


def odd_body(now_ref, own_ref, arrived_ref, sum_ref):
    before = jnp.where(lax.axis_index("tm") == 0, own_ref[...], arrived_ref[...])
    sum_ref[...] = (now_ref[1] + before.astype(F32)).astype(BF)


def last_body(odd_ref, now_ref, own_ref, arrived_ref, out_ref, even_ref, sems):
    odd_copy = pltpu.make_async_copy(odd_ref, out_ref.at[1], sems.at[1])
    odd_copy.start()
    before = jnp.where(lax.axis_index("tm") == 0, own_ref[...], arrived_ref[...])
    even_ref[...] = (now_ref[0] + before.astype(F32)).astype(BF)
    even_copy = pltpu.make_async_copy(even_ref, out_ref.at[0], sems.at[0])
    even_copy.start()
    odd_copy.wait()
    even_copy.wait()


def per_device(
    features,
    norm_gain,
    query_weight,
    key_weight,
    value_weight,
    out_weight,
    conv_weight,
    skip_weight,
):
    _, tile_rows, cols, channels = features.shape
    out_channels = conv_weight.shape[-1]
    cells = tile_rows * cols
    devices = lax.axis_size("tile")
    chips = devices // 2
    swap = [(i, i ^ 1) for i in range(devices)]
    own = features.reshape(cells, channels)

    def turned(array, by, flip):
        pairs = [(i, ((i + 2 * by) % devices) ^ flip) for i in range(devices)]
        return lax.ppermute(array, "tile", pairs)

    sums, own, first, second = call(
        stats_body,
        [
            jax.ShapeDtypeStruct((8, channels), F32),
            *[jax.ShapeDtypeStruct((n, channels), BF) for n in (cells, cols, cells - cols)],
        ],
        [pltpu.SemaphoreType.DMA((PIECES,))],
        STATS_COST,
        hbm(own),
        spaces=[pltpu.HBM],
    )
    sums = [sums] + [turned(sums, by, 1) for by in range(1, chips)]
    recv = [turned(own, by, 1) for by in range(1, chips)]
    sums = jnp.concatenate(sums, axis=0)
    first, second, sums = lax.optimization_barrier((first, second, sums))
    sib = [lax.ppermute(part, "tile", swap) for part in (first, second)]
    sums = [sums, lax.ppermute(sums, "tile", swap)]

    exponent = channels ** (-0.5) * 1.4426950408889634
    near = cells + cols
    every = near + cols
    taps = conv_weight.reshape(3, 3, 3 * channels, out_channels)
    first_taps = (2, *taps.shape[1:])
    weights = [norm_gain.reshape(1, channels), query_weight, key_weight, value_weight]
    held = call(
        stage_body,
        [jax.ShapeDtypeStruct(w.shape, w.dtype) for w in weights],
        [pltpu.SemaphoreType.DMA((len(weights),))],
        STAGE_COST,
        sums[0], *[hbm(w) for w in weights],
        spaces=[VMEM] + [pltpu.HBM] * len(weights),
    )
    _, wq, wk, wv = held

    def rows_of(rows, kind=BF, width=channels):
        return jax.ShapeDtypeStruct((rows, width), kind)

    def state_of(rows):
        return [rows_of(rows, F32, 128), rows_of(rows, F32, 128), rows_of(rows, F32)]

    def scratch_of(shapes):
        return [VMEM(shape.shape, shape.dtype) for shape in shapes]

    n_sums = len(sums)
    norm, q, k, v, *rest = call(
        functools.partial(early_body, devices * cells, cols, exponent, n_sums),
        [
            rows_of(8, F32),
            rows_of(near),
            rows_of(2 * cells),
            rows_of(2 * cells),
            *state_of(near),
            jax.ShapeDtypeStruct(out_weight.shape, BF),
            jax.ShapeDtypeStruct(first_taps, BF),
        ],
        [pltpu.SemaphoreType.DMA((2,))],
        EARLY_COST,
        own, *sib, *sums, *held, hbm(out_weight), hbm(taps),
        spaces=[VMEM] * (7 + n_sums) + [pltpu.HBM] * 2,
    )
    state, (wo, held_taps) = rest[:3], rest[3:]

    *recv, norm = lax.optimization_barrier((*recv, norm))
    rsib = [lax.ppermute(block, "tile", swap) for block in recv]
    ends = recv[:1] if chips == 2 else [recv[0], recv[-1]]
    far, q, *state, new_k, new_v = call(
        functools.partial(join_body, cols, exponent, chips == 2),
        [rows_of(cols), rows_of(every), *state_of(every), rows_of(cells), rows_of(cells)],
        [],
        JOIN_COST,
        *ends, norm, wq, wk, wv, q, k, v, *state,
    )
    for block in recv[1:] + rsib[:-1]:
        state = call(
            functools.partial(more_body, exponent),
            state_of(every),
            scratch_of([*state_of(every), rows_of(cells), rows_of(cells)]),
            10**9,
            block, norm, wk, wv, q, *state,
        )
    even, odd, second, wide, mid = call(
        functools.partial(late_body, cols, exponent),
        [
            rows_of(cells, BF, out_channels),
            rows_of(cells, BF, out_channels),
            rows_of(cells, F32, out_channels),
            rows_of(every, BF, 3 * channels),
            rows_of(cells),
        ],
        scratch_of([rows_of(2 * cells), rows_of(2 * cells), *state_of(every), rows_of(every)]),
        LATE_COST,
        own, *sib, far, rsib[-1], norm, q, *state, new_k, new_v, wk, wv, wo, held_taps,
    )
    spans = lax.axis_size("tm")
    arrived_odd = lax.ppermute(odd, "tm", [(i, (i + 1) % spans) for i in range(spans)])
    arrived_even = lax.ppermute(even, "tm", [(i, i + 1) for i in range(spans - 1)])
    both = jax.ShapeDtypeStruct((2, cells, out_channels), F32)
    now = call(
        functools.partial(now_body, cols),
        both,
        [
            VMEM(taps.shape[1:], BF),
            VMEM(skip_weight.shape, BF),
            pltpu.SemaphoreType.DMA((2,)),
        ],
        NOW_COST,
        wide, mid, second, hbm(taps), hbm(skip_weight),
        spaces=[VMEM] * 3 + [pltpu.HBM] * 2,
    )
    share = rows_of(cells, BF, out_channels)
    done_odd = call(odd_body, share, [], 1, now, odd, arrived_odd)
    done_odd, arrived_even = lax.optimization_barrier((done_odd, arrived_even))
    decoded = pl.pallas_call(
        last_body,
        out_shape=jax.ShapeDtypeStruct((2, cells, out_channels), BF),
        in_specs=[spec()] * 4,
        out_specs=spec(pltpu.HBM),
        scratch_shapes=[VMEM((cells, out_channels), BF), pltpu.SemaphoreType.DMA((2,))],
        compiler_params=pltpu.CompilerParams(vmem_limit_bytes=LIMIT),
    )(done_odd, now, even, arrived_even)
    return decoded.reshape(2, tile_rows, cols, out_channels)


def solution(mesh):
    in_specs = (P("tm", "tile", None, None), P(), P(), P(), P(), P(), P(), P())
    out_specs = P("tm", "tile", None, None)
    return jax.shard_map(
        per_device, mesh=mesh, in_specs=in_specs, out_specs=out_specs, check_vma=False
    )
```

```python
import functools

import jax
import jax.numpy as jnp
from jax import lax
from jax.experimental import pallas as pl
from jax.experimental.pallas import tpu as pltpu
from jax.sharding import PartitionSpec as P

GROUPS = 32
BF = jnp.bfloat16
F32 = jnp.float32
VMEM = pltpu.VMEM
LIMIT = 12 * 1024 * 1024
PIECES = 5
MOVED = 16
STATS_COST = 1 << 6
STAGE_COST = 1 << 4
EARLY_COST = 7 * 10**8
JOIN_COST = LATE_COST = NOW_COST = 1 << 15


def dot(left, right):
    return jnp.dot(left, right, preferred_element_type=F32)


def dot_t(left, right):
    return lax.dot_general(left, right, (((1,), (1,)), ((), ())), preferred_element_type=F32)


def spec(space=VMEM):
    return pl.BlockSpec(memory_space=space)


def hbm(array):
    return pltpu.with_memory_space_constraint(array, pltpu.HBM)


def call(body, outs, scratch, cost, *args, spaces=None):
    spaces = spaces or [VMEM] * len(args)
    return pl.pallas_call(
        body,
        out_shape=outs,
        in_specs=[spec(s) for s in spaces],
        out_specs=jax.tree.map(lambda _: spec(), outs),
        scratch_shapes=scratch,
        compiler_params=pltpu.CompilerParams(vmem_limit_bytes=LIMIT),
        cost_estimate=pl.CostEstimate(flops=cost, bytes_accessed=1 << 10, transcendentals=0),
    )(*args)


def core_index():
    return lax.axis_index("tile") % 2


def far_is_inside():
    me = lax.axis_index("tile")
    core = me % 2
    last = lax.axis_size("tile") - 1
    return me != core * last


def stats_body(features_ref, sums_ref, own_ref, first_ref, second_ref, sems):
    rows = own_ref.shape[0] // PIECES
    copies = []
    for i in range(PIECES):
        piece = pl.ds(i * rows, rows)
        copies.append(
            pltpu.make_async_copy(features_ref.at[piece], own_ref.at[piece], sems.at[i])
        )
        copies[-1].start()
    total = jnp.zeros((1, own_ref.shape[1]), F32)
    squared = total
    for i in range(PIECES):
        copies[i].wait()
        block = own_ref[i * rows : (i + 1) * rows].astype(F32)
        total += jnp.sum(block, axis=0, keepdims=True)
        squared += jnp.sum(block * block, axis=0, keepdims=True)
    sums_ref[...] = jnp.concatenate(
        [total, squared, jnp.zeros((6, own_ref.shape[1]), F32)], axis=0
    )
    first = first_ref.shape[0]
    first_ref[...] = own_ref[:first]
    second_ref[...] = own_ref[first:]


def near_rows(first_ref, second_ref, cols):
    return jnp.where(core_index() == 0, first_ref[:cols], second_ref[second_ref.shape[0] - cols :])


def group_sums(sums, width):
    lane = lax.broadcasted_iota(jnp.int32, sums.shape, 1)
    size = sums.shape[1]
    step = 1
    while step < width:
        low = pltpu.roll(sums, size - step, 1)
        high = pltpu.roll(sums, step, 1)
        sums = sums + jnp.where((lane & step) == 0, low, high)
        step *= 2
    return sums


def moments(sum_refs, cells):
    sums = 0.0
    for ref in sum_refs:
        for first in range(0, ref.shape[0], 8):
            sums = sums + ref[first : first + 8]
    width = sums.shape[1] // GROUPS
    sums = group_sums(sums, width)
    population = cells * width
    mean = sums[0:1] / population
    var = sums[1:2] / population - mean * mean
    return mean, lax.rsqrt(var + 1e-06)


def normalise(block, mean, inverse, gain):
    return ((block.astype(F32) - mean) * inverse * gain).astype(BF)


def attend(queries, keys, values, exponent, peak_ref, sum_ref, mix_ref):
    scores = dot_t(queries, keys)
    if callable(values):
        values = values()
    peak = jnp.max(scores, axis=1, keepdims=True)
    unnormed = jnp.exp2((scores - peak) * exponent)
    peak_ref[...] = jnp.broadcast_to(peak, peak_ref.shape)
    sum_ref[...] = jnp.broadcast_to(jnp.sum(unnormed, axis=1, keepdims=True), sum_ref.shape)
    mix_ref[...] = dot(unnormed.astype(BF), values)


def merge(old, new, out_refs, exponent, last):
    peak = jnp.maximum(old[0][...], new[0][...])
    fade_old = jnp.exp2((old[0][...] - peak) * exponent)
    fade_new = jnp.exp2((new[0][...] - peak) * exponent)
    total = old[1][...] * fade_old + new[1][...] * fade_new
    if last:
        scale = 1.0 / total
        fade_old = fade_old * scale
        fade_new = fade_new * scale
    else:
        out_refs[0][...] = peak
        out_refs[1][...] = total
    width = peak.shape[1]
    for first in range(0, old[2].shape[1], width):
        lanes = slice(first, first + width)
        mixed = old[2][:, lanes] * fade_old + new[2][:, lanes] * fade_new
        out_refs[-1][:, lanes] = mixed.astype(out_refs[-1].dtype)


def stage_body(*refs):
    refs, sems = refs[1:-1], refs[-1]
    count = len(refs) // 2
    copies = [
        pltpu.make_async_copy(refs[i], refs[count + i], sems.at[i]) for i in range(count)
    ]
    for copy in copies:
        copy.start()
    for copy in copies:
        copy.wait()


def early_body(
    cells_all, cols, exponent, n_sums,
    own_ref, sib_first_ref, sib_second_ref, *refs,
):
    sum_refs, refs = refs[:n_sums], refs[n_sums:]
    gain_ref, wq_ref, wk_ref, wv_ref, wo_hbm_ref, taps_hbm_ref, refs = *refs[:6], refs[6:]
    norm_ref, q_ref, k_ref, v_ref, *state_refs = refs[:7]
    wo_ref, taps_ref, sems = refs[7:]
    copies = [
        pltpu.make_async_copy(wo_hbm_ref, wo_ref, sems.at[0]),
        pltpu.make_async_copy(taps_hbm_ref.at[pl.ds(0, 2)], taps_ref, sems.at[1]),
    ]
    for copy in copies:
        copy.start()
    mean, inverse = moments(sum_refs, cells_all)
    gain = gain_ref[...]
    norm_ref[...] = jnp.concatenate(
        [mean, inverse, gain, jnp.zeros((5, mean.shape[1]), F32)], axis=0
    )
    own = normalise(own_ref[...], mean, inverse, gain)
    sib = jnp.concatenate([sib_first_ref[...], sib_second_ref[...]], axis=0)
    sib = normalise(sib, mean, inverse, gain)
    halo = normalise(near_rows(sib_first_ref, sib_second_ref, cols), mean, inverse, gain)
    both = jnp.concatenate([own, sib], axis=0)
    q_ref[...] = dot(jnp.concatenate([own, halo], axis=0), wq_ref[...]).astype(BF)
    k_ref[...] = dot(both, wk_ref[...]).astype(BF)

    def values():
        v_ref[...] = dot(both, wv_ref[...]).astype(BF)
        return v_ref[...]

    attend(q_ref[...], k_ref[...], values, exponent, *state_refs)
    for copy in copies:
        copy.wait()


def normal_of(norm_ref):
    return norm_ref[0:1], norm_ref[1:2], norm_ref[2:3]


def far_rows(first_ref, last_ref, cols):
    core = core_index()
    far = pl.multiple_of((1 - core) * (first_ref.shape[0] - cols), 16)
    first = first_ref[pl.ds(far, cols), :]
    if last_ref is None:
        return first
    return jnp.where(core == 0, first, last_ref[pl.ds(far, cols), :])


def project(block_ref, norm_ref, wk_ref, wv_ref, k_ref, v_ref):
    normed = normalise(block_ref[...], *normal_of(norm_ref))
    k_ref[...] = dot(normed, wk_ref[...]).astype(BF)
    v_ref[...] = dot(normed, wv_ref[...]).astype(BF)


def join_body(cols, exponent, single, *refs):
    first_ref, refs = refs[0], refs[1:]
    last_ref, refs = (None, refs) if single else (refs[0], refs[1:])
    (norm_ref, wq_ref, wk_ref, wv_ref, q_ref, k_ref, v_ref, peak_ref, sum_ref, mix_ref,
     far_ref, all_q_ref, all_peak_ref, all_sum_ref, all_mix_ref, new_k_ref, new_v_ref) = refs
    near = q_ref.shape[0]
    far = far_rows(first_ref, last_ref, cols)
    far_ref[...] = far
    far_q = dot(normalise(far, *normal_of(norm_ref)), wq_ref[...]).astype(BF)
    all_q_ref[:near] = q_ref[...]
    all_q_ref[near:] = far_q
    every = (all_peak_ref, all_sum_ref, all_mix_ref)
    for old, new in zip((peak_ref, sum_ref, mix_ref), every, strict=True):
        new[:near] = old[...]

    def values():
        project(first_ref, norm_ref, wk_ref, wv_ref, new_k_ref, new_v_ref)
        return v_ref[...]

    attend(far_q, k_ref[...], values, exponent, *[ref.at[pl.ds(near, cols)] for ref in every])


def more_body(exponent, block_ref, norm_ref, wk_ref, wv_ref, q_ref, *refs):
    old, out, new = refs[:3], refs[3:6], refs[6:9]
    k_ref, v_ref = refs[9:]
    project(block_ref, norm_ref, wk_ref, wv_ref, k_ref, v_ref)
    attend(q_ref[...], k_ref[...], v_ref[...], exponent, *new)
    merge(old, new, out, exponent, False)


def spread(act, cols):
    size = act.shape[0]
    col = lax.broadcasted_iota(jnp.int32, act.shape, 0) % cols
    left = jnp.where(col == 0, 0.0, pltpu.roll(act, 1, 0))
    right = jnp.where(col == cols - 1, 0.0, pltpu.roll(act, size - 1, 0))
    return jnp.concatenate([left.astype(BF), act.astype(BF), right.astype(BF)], axis=1)


def conv(wide_ref, taps, out_cells, cols):
    total = None
    for row in range(3):
        term = dot(wide_ref[row * cols : row * cols + out_cells, :], taps(row))
        total = term if total is None else total + term
    return total


def late_body(
    cols, exponent,
    own_ref, sib_first_ref, sib_second_ref, far_ref, block_ref, norm_ref, q_ref, peak_ref, sum_ref, mix_ref,
    k_ref, v_ref, wk_ref, wv_ref, wo_ref, taps_ref,
    even_ref, odd_ref, second_ref, wide_ref, mid_ref,
    keys_ref, values_ref, new_peak_ref, new_sum_ref, new_mix_ref, attended_ref,
):
    cells = own_ref.shape[0]
    core = core_index()
    normed = normalise(block_ref[...], *normal_of(norm_ref))
    keys_ref[:cells] = k_ref[...]
    keys_ref[cells:] = dot(normed, wk_ref[...]).astype(BF)

    def values():
        values_ref[:cells] = v_ref[...]
        values_ref[cells:] = dot(normed, wv_ref[...]).astype(BF)
        return values_ref[...]

    new = (new_peak_ref, new_sum_ref, new_mix_ref)
    attend(q_ref[...], keys_ref[...], values, exponent, *new)
    merge((peak_ref, sum_ref, mix_ref), new, (attended_ref,), exponent, True)
    change = dot(attended_ref[...], wo_ref[...])
    near = near_rows(sib_first_ref, sib_second_ref, cols)
    base = jnp.concatenate([own_ref[...], near, far_ref[...]], axis=0)
    mid = (base.astype(F32) + change).astype(BF)
    mid_ref[...] = mid[:cells]
    act = jax.nn.silu(mid.astype(F32)).astype(BF).astype(F32)
    far_act = jnp.where(far_is_inside(), act[cells + cols :], 0.0)
    above = pl.multiple_of(core * (cells + cols), 16)
    below = pl.multiple_of((1 - core) * (cells + cols), 16)
    for row in range(0, cells, cols):
        wide_ref[cols + row : 2 * cols + row] = spread(act[row : row + cols], cols)
    wide_ref[pl.ds(below, cols), :] = spread(act[cells : cells + cols], cols)
    wide_ref[pl.ds(above, cols), :] = spread(far_act, cols)
    first_tap = conv(wide_ref, lambda row: taps_ref[0, row], cells, cols)
    second_tap = conv(wide_ref, lambda row: taps_ref[1, row], cells, cols)
    second_ref[...] = second_tap
    even = (first_tap + second_tap).astype(BF)
    even_ref[...] = even[: cells - MOVED]
    odd_ref[:cells] = first_tap.astype(BF)
    odd_ref[cells:] = even[cells - MOVED :]


def now_body(
    cols, wide_ref, mid_ref, second_ref, taps_ref, skip_hbm_ref, out_ref, tap_ref, skip_ref, sems
):
    copies = [
        pltpu.make_async_copy(skip_hbm_ref, skip_ref, sems.at[0]),
        pltpu.make_async_copy(taps_ref.at[2], tap_ref, sems.at[1]),
    ]
    for copy in copies:
        copy.start()
    cells = mid_ref.shape[0]
    copies[0].wait()
    skip = dot(mid_ref[...], skip_ref[...])
    copies[1].wait()
    last_tap = conv(wide_ref, lambda row: tap_ref[row], cells, cols) + skip
    out_ref[0] = last_tap
    out_ref[1] = last_tap + second_ref[...]


def odd_body(now_ref, own_ref, arrived_ref, sum_ref):
    cells = now_ref.shape[1]
    before = jnp.where(lax.axis_index("tm") == 0, own_ref[...], arrived_ref[...]).astype(F32)
    sum_ref[:cells] = (now_ref[1] + before[:cells]).astype(BF)
    sum_ref[cells:] = (now_ref[0, cells - MOVED :, :] + before[cells:]).astype(BF)


def last_body(odd_ref, now_ref, own_ref, arrived_ref, out_ref, even_ref, sems):
    cells = now_ref.shape[1]
    odd_copy = pltpu.make_async_copy(odd_ref.at[pl.ds(0, cells)], out_ref.at[1], sems.at[1])
    odd_copy.start()
    before = jnp.where(lax.axis_index("tm") == 0, own_ref[...], arrived_ref[...])
    kept = cells - MOVED
    even_ref[:kept] = (now_ref[0, :kept, :] + before.astype(F32)).astype(BF)
    even_ref[kept:] = odd_ref[cells:]
    even_copy = pltpu.make_async_copy(even_ref, out_ref.at[0], sems.at[0])
    even_copy.start()
    odd_copy.wait()
    even_copy.wait()


def per_device(
    features,
    norm_gain,
    query_weight,
    key_weight,
    value_weight,
    out_weight,
    conv_weight,
    skip_weight,
):
    _, tile_rows, cols, channels = features.shape
    out_channels = conv_weight.shape[-1]
    cells = tile_rows * cols
    devices = lax.axis_size("tile")
    chips = devices // 2
    swap = [(i, i ^ 1) for i in range(devices)]
    own = features.reshape(cells, channels)

    def turned(array, by, flip):
        pairs = [(i, ((i + 2 * by) % devices) ^ flip) for i in range(devices)]
        return lax.ppermute(array, "tile", pairs)

    sums, own, first, second = call(
        stats_body,
        [
            jax.ShapeDtypeStruct((8, channels), F32),
            *[jax.ShapeDtypeStruct((n, channels), BF) for n in (cells, cols, cells - cols)],
        ],
        [pltpu.SemaphoreType.DMA((PIECES,))],
        STATS_COST,
        hbm(own),
        spaces=[pltpu.HBM],
    )
    sums = [sums] + [turned(sums, by, 1) for by in range(1, chips)]
    recv = [turned(own, by, 1) for by in range(1, chips)]
    sums = jnp.concatenate(sums, axis=0)
    first, second, sums = lax.optimization_barrier((first, second, sums))
    sib = [lax.ppermute(part, "tile", swap) for part in (first, second)]
    sums = [sums, lax.ppermute(sums, "tile", swap)]

    exponent = channels ** (-0.5) * 1.4426950408889634
    near = cells + cols
    every = near + cols
    taps = conv_weight.reshape(3, 3, 3 * channels, out_channels)
    first_taps = (2, *taps.shape[1:])
    weights = [norm_gain.reshape(1, channels), query_weight, key_weight, value_weight]
    held = call(
        stage_body,
        [jax.ShapeDtypeStruct(w.shape, w.dtype) for w in weights],
        [pltpu.SemaphoreType.DMA((len(weights),))],
        STAGE_COST,
        sums[0], *[hbm(w) for w in weights],
        spaces=[VMEM] + [pltpu.HBM] * len(weights),
    )
    _, wq, wk, wv = held

    def rows_of(rows, kind=BF, width=channels):
        return jax.ShapeDtypeStruct((rows, width), kind)

    def state_of(rows):
        return [rows_of(rows, F32, 128), rows_of(rows, F32, 128), rows_of(rows, F32)]

    def scratch_of(shapes):
        return [VMEM(shape.shape, shape.dtype) for shape in shapes]

    n_sums = len(sums)
    norm, q, k, v, *rest = call(
        functools.partial(early_body, devices * cells, cols, exponent, n_sums),
        [
            rows_of(8, F32),
            rows_of(near),
            rows_of(2 * cells),
            rows_of(2 * cells),
            *state_of(near),
            jax.ShapeDtypeStruct(out_weight.shape, BF),
            jax.ShapeDtypeStruct(first_taps, BF),
        ],
        [pltpu.SemaphoreType.DMA((2,))],
        EARLY_COST,
        own, *sib, *sums, *held, hbm(out_weight), hbm(taps),
        spaces=[VMEM] * (7 + n_sums) + [pltpu.HBM] * 2,
    )
    state, (wo, held_taps) = rest[:3], rest[3:]

    *recv, norm = lax.optimization_barrier((*recv, norm))
    rsib = [lax.ppermute(block, "tile", swap) for block in recv]
    ends = recv[:1] if chips == 2 else [recv[0], recv[-1]]
    far, q, *state, new_k, new_v = call(
        functools.partial(join_body, cols, exponent, chips == 2),
        [rows_of(cols), rows_of(every), *state_of(every), rows_of(cells), rows_of(cells)],
        [],
        JOIN_COST,
        *ends, norm, wq, wk, wv, q, k, v, *state,
    )
    for block in recv[1:] + rsib[:-1]:
        state = call(
            functools.partial(more_body, exponent),
            state_of(every),
            scratch_of([*state_of(every), rows_of(cells), rows_of(cells)]),
            10**9,
            block, norm, wk, wv, q, *state,
        )
    even, odd, second, wide, mid = call(
        functools.partial(late_body, cols, exponent),
        [
            rows_of(cells - MOVED, BF, out_channels),
            rows_of(cells + MOVED, BF, out_channels),
            rows_of(cells, F32, out_channels),
            rows_of(every, BF, 3 * channels),
            rows_of(cells),
        ],
        scratch_of([rows_of(2 * cells), rows_of(2 * cells), *state_of(every), rows_of(every)]),
        LATE_COST,
        own, *sib, far, rsib[-1], norm, q, *state, new_k, new_v, wk, wv, wo, held_taps,
    )
    spans = lax.axis_size("tm")
    ring = [
        (i * devices + j, (i + 1) * devices + j if i + 1 < spans else j ^ 1)
        for i in range(spans)
        for j in range(devices)
    ]
    arrived_odd = lax.ppermute(odd, ("tm", "tile"), ring)
    arrived_even = lax.ppermute(even, "tm", [(i, i + 1) for i in range(spans - 1)])
    both = jax.ShapeDtypeStruct((2, cells, out_channels), F32)
    now = call(
        functools.partial(now_body, cols),
        both,
        [
            VMEM(taps.shape[1:], BF),
            VMEM(skip_weight.shape, BF),
            pltpu.SemaphoreType.DMA((2,)),
        ],
        NOW_COST,
        wide, mid, second, hbm(taps), hbm(skip_weight),
        spaces=[VMEM] * 3 + [pltpu.HBM] * 2,
    )
    done_odd = call(odd_body, rows_of(cells + MOVED, BF, out_channels), [], 1, now, odd, arrived_odd)
    done_odd, arrived_even = lax.optimization_barrier((done_odd, arrived_even))
    decoded = pl.pallas_call(
        last_body,
        out_shape=jax.ShapeDtypeStruct((2, cells, out_channels), BF),
        in_specs=[spec()] * 4,
        out_specs=spec(pltpu.HBM),
        scratch_shapes=[VMEM((cells, out_channels), BF), pltpu.SemaphoreType.DMA((2,))],
        compiler_params=pltpu.CompilerParams(vmem_limit_bytes=LIMIT),
    )(done_odd, now, even, arrived_even)
    return decoded.reshape(2, tile_rows, cols, out_channels)


def solution(mesh):
    in_specs = (P("tm", "tile", None, None), P(), P(), P(), P(), P(), P(), P())
    out_specs = P("tm", "tile", None, None)
    return jax.shard_map(
        per_device, mesh=mesh, in_specs=in_specs, out_specs=out_specs, check_vma=False
    )
```

```python
import functools

import jax
import jax.numpy as jnp
from jax import lax
from jax.experimental import pallas as pl
from jax.experimental.pallas import tpu as pltpu
from jax.sharding import PartitionSpec as P

GROUPS = 32
BF = jnp.bfloat16
F32 = jnp.float32
VMEM = pltpu.VMEM
LIMIT = 12 * 1024 * 1024
PIECES = 5
MOVED = 48
STATS_COST = 1 << 6
STAGE_COST = 1 << 4
EARLY_COST = 7 * 10**8
JOIN_COST = LATE_COST = NOW_COST = 1 << 15


def dot(left, right):
    return jnp.dot(left, right, preferred_element_type=F32)


def dot_t(left, right):
    return lax.dot_general(left, right, (((1,), (1,)), ((), ())), preferred_element_type=F32)


def spec(space=VMEM):
    return pl.BlockSpec(memory_space=space)


def hbm(array):
    return pltpu.with_memory_space_constraint(array, pltpu.HBM)


def call(body, outs, scratch, cost, *args, spaces=None):
    spaces = spaces or [VMEM] * len(args)
    return pl.pallas_call(
        body,
        out_shape=outs,
        in_specs=[spec(s) for s in spaces],
        out_specs=jax.tree.map(lambda _: spec(), outs),
        scratch_shapes=scratch,
        compiler_params=pltpu.CompilerParams(vmem_limit_bytes=LIMIT),
        cost_estimate=pl.CostEstimate(flops=cost, bytes_accessed=1 << 10, transcendentals=0),
    )(*args)


def core_index():
    return lax.axis_index("tile") % 2


def far_is_inside():
    me = lax.axis_index("tile")
    core = me % 2
    last = lax.axis_size("tile") - 1
    return me != core * last


def stats_body(features_ref, sums_ref, own_ref, first_ref, second_ref, sems):
    rows = own_ref.shape[0] // PIECES
    copies = []
    for i in range(PIECES):
        piece = pl.ds(i * rows, rows)
        copies.append(
            pltpu.make_async_copy(features_ref.at[piece], own_ref.at[piece], sems.at[i])
        )
        copies[-1].start()
    total = jnp.zeros((1, own_ref.shape[1]), F32)
    squared = total
    for i in range(PIECES):
        copies[i].wait()
        block = own_ref[i * rows : (i + 1) * rows].astype(F32)
        total += jnp.sum(block, axis=0, keepdims=True)
        squared += jnp.sum(block * block, axis=0, keepdims=True)
    sums_ref[...] = jnp.concatenate(
        [total, squared, jnp.zeros((6, own_ref.shape[1]), F32)], axis=0
    )
    first = first_ref.shape[0]
    first_ref[...] = own_ref[:first]
    second_ref[...] = own_ref[first:]


def near_rows(first_ref, second_ref, cols):
    return jnp.where(core_index() == 0, first_ref[:cols], second_ref[second_ref.shape[0] - cols :])


def group_sums(sums, width):
    lane = lax.broadcasted_iota(jnp.int32, sums.shape, 1)
    size = sums.shape[1]
    step = 1
    while step < width:
        low = pltpu.roll(sums, size - step, 1)
        high = pltpu.roll(sums, step, 1)
        sums = sums + jnp.where((lane & step) == 0, low, high)
        step *= 2
    return sums


def moments(sum_refs, cells):
    sums = 0.0
    for ref in sum_refs:
        for first in range(0, ref.shape[0], 8):
            sums = sums + ref[first : first + 8]
    width = sums.shape[1] // GROUPS
    sums = group_sums(sums, width)
    population = cells * width
    mean = sums[0:1] / population
    var = sums[1:2] / population - mean * mean
    return mean, lax.rsqrt(var + 1e-06)


def normalise(block, mean, inverse, gain):
    return ((block.astype(F32) - mean) * inverse * gain).astype(BF)


def attend(queries, keys, values, exponent, peak_ref, sum_ref, mix_ref):
    scores = dot_t(queries, keys)
    if callable(values):
        values = values()
    peak = jnp.max(scores, axis=1, keepdims=True)
    unnormed = jnp.exp2((scores - peak) * exponent)
    peak_ref[...] = jnp.broadcast_to(peak, peak_ref.shape)
    sum_ref[...] = jnp.broadcast_to(jnp.sum(unnormed, axis=1, keepdims=True), sum_ref.shape)
    mix_ref[...] = dot(unnormed.astype(BF), values)


def merge(old, new, out_refs, exponent, last):
    peak = jnp.maximum(old[0][...], new[0][...])
    fade_old = jnp.exp2((old[0][...] - peak) * exponent)
    fade_new = jnp.exp2((new[0][...] - peak) * exponent)
    total = old[1][...] * fade_old + new[1][...] * fade_new
    if last:
        scale = 1.0 / total
        fade_old = fade_old * scale
        fade_new = fade_new * scale
    else:
        out_refs[0][...] = peak
        out_refs[1][...] = total
    width = peak.shape[1]
    for first in range(0, old[2].shape[1], width):
        lanes = slice(first, first + width)
        mixed = old[2][:, lanes] * fade_old + new[2][:, lanes] * fade_new
        out_refs[-1][:, lanes] = mixed.astype(out_refs[-1].dtype)


def stage_body(*refs):
    refs, sems = refs[1:-1], refs[-1]
    count = len(refs) // 2
    copies = [
        pltpu.make_async_copy(refs[i], refs[count + i], sems.at[i]) for i in range(count)
    ]
    for copy in copies:
        copy.start()
    for copy in copies:
        copy.wait()


def early_body(
    cells_all, cols, exponent, n_sums,
    own_ref, sib_first_ref, sib_second_ref, *refs,
):
    sum_refs, refs = refs[:n_sums], refs[n_sums:]
    gain_ref, wq_ref, wk_ref, wv_ref, wo_hbm_ref, taps_hbm_ref, refs = *refs[:6], refs[6:]
    norm_ref, q_ref, k_ref, v_ref, *state_refs = refs[:7]
    wo_ref, taps_ref, sems = refs[7:]
    copies = [
        pltpu.make_async_copy(wo_hbm_ref, wo_ref, sems.at[0]),
        pltpu.make_async_copy(taps_hbm_ref.at[pl.ds(0, 2)], taps_ref, sems.at[1]),
    ]
    for copy in copies:
        copy.start()
    mean, inverse = moments(sum_refs, cells_all)
    gain = gain_ref[...]
    norm_ref[...] = jnp.concatenate(
        [mean, inverse, gain, jnp.zeros((5, mean.shape[1]), F32)], axis=0
    )
    own = normalise(own_ref[...], mean, inverse, gain)
    sib = jnp.concatenate([sib_first_ref[...], sib_second_ref[...]], axis=0)
    sib = normalise(sib, mean, inverse, gain)
    halo = normalise(near_rows(sib_first_ref, sib_second_ref, cols), mean, inverse, gain)
    both = jnp.concatenate([own, sib], axis=0)
    q_ref[...] = dot(jnp.concatenate([own, halo], axis=0), wq_ref[...]).astype(BF)
    k_ref[...] = dot(both, wk_ref[...]).astype(BF)

    def values():
        v_ref[...] = dot(both, wv_ref[...]).astype(BF)
        return v_ref[...]

    attend(q_ref[...], k_ref[...], values, exponent, *state_refs)
    for copy in copies:
        copy.wait()


def normal_of(norm_ref):
    return norm_ref[0:1], norm_ref[1:2], norm_ref[2:3]


def far_rows(first_ref, last_ref, cols):
    core = core_index()
    far = pl.multiple_of((1 - core) * (first_ref.shape[0] - cols), 16)
    first = first_ref[pl.ds(far, cols), :]
    if last_ref is None:
        return first
    return jnp.where(core == 0, first, last_ref[pl.ds(far, cols), :])


def project(block_ref, norm_ref, wk_ref, wv_ref, k_ref, v_ref):
    normed = normalise(block_ref[...], *normal_of(norm_ref))
    k_ref[...] = dot(normed, wk_ref[...]).astype(BF)
    v_ref[...] = dot(normed, wv_ref[...]).astype(BF)


def join_body(cols, exponent, single, *refs):
    first_ref, refs = refs[0], refs[1:]
    last_ref, refs = (None, refs) if single else (refs[0], refs[1:])
    (norm_ref, wq_ref, wk_ref, wv_ref, q_ref, k_ref, v_ref, peak_ref, sum_ref, mix_ref,
     far_ref, all_q_ref, all_peak_ref, all_sum_ref, all_mix_ref, new_k_ref, new_v_ref) = refs
    near = q_ref.shape[0]
    far = far_rows(first_ref, last_ref, cols)
    far_ref[...] = far
    far_q = dot(normalise(far, *normal_of(norm_ref)), wq_ref[...]).astype(BF)
    all_q_ref[:near] = q_ref[...]
    all_q_ref[near:] = far_q
    every = (all_peak_ref, all_sum_ref, all_mix_ref)
    for old, new in zip((peak_ref, sum_ref, mix_ref), every, strict=True):
        new[:near] = old[...]

    def values():
        project(first_ref, norm_ref, wk_ref, wv_ref, new_k_ref, new_v_ref)
        return v_ref[...]

    attend(far_q, k_ref[...], values, exponent, *[ref.at[pl.ds(near, cols)] for ref in every])


def more_body(exponent, block_ref, norm_ref, wk_ref, wv_ref, q_ref, *refs):
    old, out, new = refs[:3], refs[3:6], refs[6:9]
    k_ref, v_ref = refs[9:]
    project(block_ref, norm_ref, wk_ref, wv_ref, k_ref, v_ref)
    attend(q_ref[...], k_ref[...], v_ref[...], exponent, *new)
    merge(old, new, out, exponent, False)


def spread(act, cols):
    size = act.shape[0]
    col = lax.broadcasted_iota(jnp.int32, act.shape, 0) % cols
    left = jnp.where(col == 0, 0.0, pltpu.roll(act, 1, 0))
    right = jnp.where(col == cols - 1, 0.0, pltpu.roll(act, size - 1, 0))
    return jnp.concatenate([left.astype(BF), act.astype(BF), right.astype(BF)], axis=1)


def conv(wide_ref, taps, out_cells, cols):
    total = None
    for row in range(3):
        term = dot(wide_ref[row * cols : row * cols + out_cells, :], taps(row))
        total = term if total is None else total + term
    return total


def late_body(
    cols, exponent,
    own_ref, sib_first_ref, sib_second_ref, far_ref, block_ref, norm_ref, q_ref, peak_ref, sum_ref, mix_ref,
    k_ref, v_ref, wk_ref, wv_ref, wo_ref, taps_ref,
    even_ref, odd_ref, second_ref, wide_ref, mid_ref,
    keys_ref, values_ref, new_peak_ref, new_sum_ref, new_mix_ref, attended_ref,
):
    cells = own_ref.shape[0]
    core = core_index()
    normed = normalise(block_ref[...], *normal_of(norm_ref))
    keys_ref[:cells] = k_ref[...]
    keys_ref[cells:] = dot(normed, wk_ref[...]).astype(BF)

    def values():
        values_ref[:cells] = v_ref[...]
        values_ref[cells:] = dot(normed, wv_ref[...]).astype(BF)
        return values_ref[...]

    new = (new_peak_ref, new_sum_ref, new_mix_ref)
    attend(q_ref[...], keys_ref[...], values, exponent, *new)
    merge((peak_ref, sum_ref, mix_ref), new, (attended_ref,), exponent, True)
    change = dot(attended_ref[...], wo_ref[...])
    near = near_rows(sib_first_ref, sib_second_ref, cols)
    base = jnp.concatenate([own_ref[...], near, far_ref[...]], axis=0)
    mid = (base.astype(F32) + change).astype(BF)
    mid_ref[...] = mid[:cells]
    act = jax.nn.silu(mid.astype(F32)).astype(BF).astype(F32)
    far_act = jnp.where(far_is_inside(), act[cells + cols :], 0.0)
    above = pl.multiple_of(core * (cells + cols), 16)
    below = pl.multiple_of((1 - core) * (cells + cols), 16)
    for row in range(0, cells, cols):
        wide_ref[cols + row : 2 * cols + row] = spread(act[row : row + cols], cols)
    wide_ref[pl.ds(below, cols), :] = spread(act[cells : cells + cols], cols)
    wide_ref[pl.ds(above, cols), :] = spread(far_act, cols)
    first_tap = conv(wide_ref, lambda row: taps_ref[0, row], cells, cols)
    second_tap = conv(wide_ref, lambda row: taps_ref[1, row], cells, cols)
    second_ref[...] = second_tap
    even = (first_tap + second_tap).astype(BF)
    even_ref[...] = even[: cells - MOVED]
    odd_ref[:cells] = first_tap.astype(BF)
    odd_ref[cells:] = even[cells - MOVED :]


def now_body(
    cols, wide_ref, mid_ref, second_ref, taps_ref, skip_hbm_ref, out_ref, tap_ref, skip_ref, sems
):
    copies = [
        pltpu.make_async_copy(skip_hbm_ref, skip_ref, sems.at[0]),
        pltpu.make_async_copy(taps_ref.at[2], tap_ref, sems.at[1]),
    ]
    for copy in copies:
        copy.start()
    cells = mid_ref.shape[0]
    copies[0].wait()
    skip = dot(mid_ref[...], skip_ref[...])
    copies[1].wait()
    last_tap = conv(wide_ref, lambda row: tap_ref[row], cells, cols) + skip
    out_ref[0] = last_tap
    out_ref[1] = last_tap + second_ref[...]


def odd_body(now_ref, own_ref, arrived_ref, sum_ref):
    cells = now_ref.shape[1]
    before = jnp.where(lax.axis_index("tm") == 0, own_ref[...], arrived_ref[...]).astype(F32)
    sum_ref[:cells] = (now_ref[1] + before[:cells]).astype(BF)
    sum_ref[cells:] = (now_ref[0, cells - MOVED :, :] + before[cells:]).astype(BF)


def last_body(odd_ref, now_ref, own_ref, arrived_ref, out_ref, even_ref, sems):
    cells = now_ref.shape[1]
    odd_copy = pltpu.make_async_copy(odd_ref.at[pl.ds(0, cells)], out_ref.at[1], sems.at[1])
    odd_copy.start()
    before = jnp.where(lax.axis_index("tm") == 0, own_ref[...], arrived_ref[...])
    kept = cells - MOVED
    even_ref[:kept] = (now_ref[0, :kept, :] + before.astype(F32)).astype(BF)
    even_ref[kept:] = odd_ref[cells:]
    even_copy = pltpu.make_async_copy(even_ref, out_ref.at[0], sems.at[0])
    even_copy.start()
    odd_copy.wait()
    even_copy.wait()


def per_device(
    features,
    norm_gain,
    query_weight,
    key_weight,
    value_weight,
    out_weight,
    conv_weight,
    skip_weight,
):
    _, tile_rows, cols, channels = features.shape
    out_channels = conv_weight.shape[-1]
    cells = tile_rows * cols
    devices = lax.axis_size("tile")
    chips = devices // 2
    swap = [(i, i ^ 1) for i in range(devices)]
    own = features.reshape(cells, channels)

    def turned(array, by, flip):
        pairs = [(i, ((i + 2 * by) % devices) ^ flip) for i in range(devices)]
        return lax.ppermute(array, "tile", pairs)

    sums, own, first, second = call(
        stats_body,
        [
            jax.ShapeDtypeStruct((8, channels), F32),
            *[jax.ShapeDtypeStruct((n, channels), BF) for n in (cells, cols, cells - cols)],
        ],
        [pltpu.SemaphoreType.DMA((PIECES,))],
        STATS_COST,
        hbm(own),
        spaces=[pltpu.HBM],
    )
    sums = [sums] + [turned(sums, by, 1) for by in range(1, chips)]
    recv = [turned(own, by, 1) for by in range(1, chips)]
    sums = jnp.concatenate(sums, axis=0)
    first, second, sums = lax.optimization_barrier((first, second, sums))
    sib = [lax.ppermute(part, "tile", swap) for part in (first, second)]
    sums = [sums, lax.ppermute(sums, "tile", swap)]

    exponent = channels ** (-0.5) * 1.4426950408889634
    near = cells + cols
    every = near + cols
    taps = conv_weight.reshape(3, 3, 3 * channels, out_channels)
    first_taps = (2, *taps.shape[1:])
    weights = [norm_gain.reshape(1, channels), query_weight, key_weight, value_weight]
    held = call(
        stage_body,
        [jax.ShapeDtypeStruct(w.shape, w.dtype) for w in weights],
        [pltpu.SemaphoreType.DMA((len(weights),))],
        STAGE_COST,
        sums[0], *[hbm(w) for w in weights],
        spaces=[VMEM] + [pltpu.HBM] * len(weights),
    )
    _, wq, wk, wv = held

    def rows_of(rows, kind=BF, width=channels):
        return jax.ShapeDtypeStruct((rows, width), kind)

    def state_of(rows):
        return [rows_of(rows, F32, 128), rows_of(rows, F32, 128), rows_of(rows, F32)]

    def scratch_of(shapes):
        return [VMEM(shape.shape, shape.dtype) for shape in shapes]

    n_sums = len(sums)
    norm, q, k, v, *rest = call(
        functools.partial(early_body, devices * cells, cols, exponent, n_sums),
        [
            rows_of(8, F32),
            rows_of(near),
            rows_of(2 * cells),
            rows_of(2 * cells),
            *state_of(near),
            jax.ShapeDtypeStruct(out_weight.shape, BF),
            jax.ShapeDtypeStruct(first_taps, BF),
        ],
        [pltpu.SemaphoreType.DMA((2,))],
        EARLY_COST,
        own, *sib, *sums, *held, hbm(out_weight), hbm(taps),
        spaces=[VMEM] * (7 + n_sums) + [pltpu.HBM] * 2,
    )
    state, (wo, held_taps) = rest[:3], rest[3:]

    *recv, norm = lax.optimization_barrier((*recv, norm))
    rsib = [lax.ppermute(block, "tile", swap) for block in recv]
    ends = recv[:1] if chips == 2 else [recv[0], recv[-1]]
    far, q, *state, new_k, new_v = call(
        functools.partial(join_body, cols, exponent, chips == 2),
        [rows_of(cols), rows_of(every), *state_of(every), rows_of(cells), rows_of(cells)],
        [],
        JOIN_COST,
        *ends, norm, wq, wk, wv, q, k, v, *state,
    )
    for block in recv[1:] + rsib[:-1]:
        state = call(
            functools.partial(more_body, exponent),
            state_of(every),
            scratch_of([*state_of(every), rows_of(cells), rows_of(cells)]),
            10**9,
            block, norm, wk, wv, q, *state,
        )
    even, odd, second, wide, mid = call(
        functools.partial(late_body, cols, exponent),
        [
            rows_of(cells - MOVED, BF, out_channels),
            rows_of(cells + MOVED, BF, out_channels),
            rows_of(cells, F32, out_channels),
            rows_of(every, BF, 3 * channels),
            rows_of(cells),
        ],
        scratch_of([rows_of(2 * cells), rows_of(2 * cells), *state_of(every), rows_of(every)]),
        LATE_COST,
        own, *sib, far, rsib[-1], norm, q, *state, new_k, new_v, wk, wv, wo, held_taps,
    )
    spans = lax.axis_size("tm")
    ring = [
        (i * devices + j, (i + 1) * devices + j if i + 1 < spans else j ^ 1)
        for i in range(spans)
        for j in range(devices)
    ]
    arrived_odd = lax.ppermute(odd, ("tm", "tile"), ring)
    arrived_even = lax.ppermute(even, "tm", [(i, i + 1) for i in range(spans - 1)])
    both = jax.ShapeDtypeStruct((2, cells, out_channels), F32)
    now = call(
        functools.partial(now_body, cols),
        both,
        [
            VMEM(taps.shape[1:], BF),
            VMEM(skip_weight.shape, BF),
            pltpu.SemaphoreType.DMA((2,)),
        ],
        NOW_COST,
        wide, mid, second, hbm(taps), hbm(skip_weight),
        spaces=[VMEM] * 3 + [pltpu.HBM] * 2,
    )
    done_odd = call(odd_body, rows_of(cells + MOVED, BF, out_channels), [], 1, now, odd, arrived_odd)
    done_odd, arrived_even = lax.optimization_barrier((done_odd, arrived_even))
    decoded = pl.pallas_call(
        last_body,
        out_shape=jax.ShapeDtypeStruct((2, cells, out_channels), BF),
        in_specs=[spec()] * 4,
        out_specs=spec(pltpu.HBM),
        scratch_shapes=[VMEM((cells, out_channels), BF), pltpu.SemaphoreType.DMA((2,))],
        compiler_params=pltpu.CompilerParams(vmem_limit_bytes=LIMIT),
    )(done_odd, now, even, arrived_even)
    return decoded.reshape(2, tile_rows, cols, out_channels)


def solution(mesh):
    in_specs = (P("tm", "tile", None, None), P(), P(), P(), P(), P(), P(), P())
    out_specs = P("tm", "tile", None, None)
    return jax.shard_map(
        per_device, mesh=mesh, in_specs=in_specs, out_specs=out_specs, check_vma=False
    )
```

```python
import functools

import jax
import jax.numpy as jnp
from jax import lax
from jax.experimental import pallas as pl
from jax.experimental.pallas import tpu as pltpu
from jax.sharding import PartitionSpec as P

GROUPS = 32
BF = jnp.bfloat16
F32 = jnp.float32
VMEM = pltpu.VMEM
LIMIT = 12 * 1024 * 1024
PIECES = 10
STATS_COST = 1 << 6
STAGE_COST = 1 << 4
EARLY_COST = 7 * 10**8
JOIN_COST = LATE_COST = NOW_COST = 1 << 15


def dot(left, right):
    return jnp.dot(left, right, preferred_element_type=F32)


def dot_t(left, right):
    return lax.dot_general(left, right, (((1,), (1,)), ((), ())), preferred_element_type=F32)


def spec(space=VMEM):
    return pl.BlockSpec(memory_space=space)


def hbm(array):
    return pltpu.with_memory_space_constraint(array, pltpu.HBM)


def call(body, outs, scratch, cost, *args, spaces=None):
    spaces = spaces or [VMEM] * len(args)
    return pl.pallas_call(
        body,
        out_shape=outs,
        in_specs=[spec(s) for s in spaces],
        out_specs=jax.tree.map(lambda _: spec(), outs),
        scratch_shapes=scratch,
        compiler_params=pltpu.CompilerParams(vmem_limit_bytes=LIMIT),
        cost_estimate=pl.CostEstimate(flops=cost, bytes_accessed=1 << 10, transcendentals=0),
    )(*args)


def core_index():
    return lax.axis_index("tile") % 2


def far_is_inside():
    me = lax.axis_index("tile")
    core = me % 2
    last = lax.axis_size("tile") - 1
    return me != core * last


def stats_body(features_ref, sums_ref, own_ref, first_ref, second_ref, sems):
    rows = own_ref.shape[0] // PIECES
    copies = []
    for i in range(PIECES):
        piece = pl.ds(i * rows, rows)
        copies.append(
            pltpu.make_async_copy(features_ref.at[piece], own_ref.at[piece], sems.at[i])
        )
        copies[-1].start()
    total = jnp.zeros((1, own_ref.shape[1]), F32)
    squared = total
    for i in range(PIECES):
        copies[i].wait()
        block = own_ref[i * rows : (i + 1) * rows].astype(F32)
        total += jnp.sum(block, axis=0, keepdims=True)
        squared += jnp.sum(block * block, axis=0, keepdims=True)
    sums_ref[...] = jnp.concatenate(
        [total, squared, jnp.zeros((6, own_ref.shape[1]), F32)], axis=0
    )
    first = first_ref.shape[0]
    first_ref[...] = own_ref[:first]
    second_ref[...] = own_ref[first:]


def near_rows(first_ref, second_ref, cols):
    return jnp.where(core_index() == 0, first_ref[:cols], second_ref[second_ref.shape[0] - cols :])


def group_sums(sums, width):
    lane = lax.broadcasted_iota(jnp.int32, sums.shape, 1)
    size = sums.shape[1]
    step = 1
    while step < width:
        low = pltpu.roll(sums, size - step, 1)
        high = pltpu.roll(sums, step, 1)
        sums = sums + jnp.where((lane & step) == 0, low, high)
        step *= 2
    return sums


def moments(sum_refs, cells):
    sums = 0.0
    for ref in sum_refs:
        for first in range(0, ref.shape[0], 8):
            sums = sums + ref[first : first + 8]
    width = sums.shape[1] // GROUPS
    sums = group_sums(sums, width)
    population = cells * width
    mean = sums[0:1] / population
    var = sums[1:2] / population - mean * mean
    return mean, lax.rsqrt(var + 1e-06)


def normalise(block, mean, inverse, gain):
    return ((block.astype(F32) - mean) * inverse * gain).astype(BF)


def attend(queries, keys, values, exponent, peak_ref, sum_ref, mix_ref):
    scores = dot_t(queries, keys)
    if callable(values):
        values = values()
    peak = jnp.max(scores, axis=1, keepdims=True)
    unnormed = jnp.exp2((scores - peak) * exponent)
    peak_ref[...] = jnp.broadcast_to(peak, peak_ref.shape)
    sum_ref[...] = jnp.broadcast_to(jnp.sum(unnormed, axis=1, keepdims=True), sum_ref.shape)
    mix_ref[...] = dot(unnormed.astype(BF), values)


def merge(old, new, out_refs, exponent, last):
    peak = jnp.maximum(old[0][...], new[0][...])
    fade_old = jnp.exp2((old[0][...] - peak) * exponent)
    fade_new = jnp.exp2((new[0][...] - peak) * exponent)
    total = old[1][...] * fade_old + new[1][...] * fade_new
    if last:
        scale = 1.0 / total
        fade_old = fade_old * scale
        fade_new = fade_new * scale
    else:
        out_refs[0][...] = peak
        out_refs[1][...] = total
    width = peak.shape[1]
    for first in range(0, old[2].shape[1], width):
        lanes = slice(first, first + width)
        mixed = old[2][:, lanes] * fade_old + new[2][:, lanes] * fade_new
        out_refs[-1][:, lanes] = mixed.astype(out_refs[-1].dtype)


def stage_body(*refs):
    refs, sems = refs[1:-1], refs[-1]
    count = len(refs) // 2
    copies = [
        pltpu.make_async_copy(refs[i], refs[count + i], sems.at[i]) for i in range(count)
    ]
    for copy in copies:
        copy.start()
    for copy in copies:
        copy.wait()


def early_body(
    cells_all, cols, exponent, n_sums,
    own_ref, sib_first_ref, sib_second_ref, *refs,
):
    sum_refs, refs = refs[:n_sums], refs[n_sums:]
    gain_ref, wq_ref, wk_ref, wv_ref, wo_hbm_ref, taps_hbm_ref, refs = *refs[:6], refs[6:]
    norm_ref, q_ref, k_ref, v_ref, *state_refs = refs[:7]
    wo_ref, taps_ref, sems = refs[7:]
    copies = [
        pltpu.make_async_copy(wo_hbm_ref, wo_ref, sems.at[0]),
        pltpu.make_async_copy(taps_hbm_ref.at[pl.ds(0, 2)], taps_ref, sems.at[1]),
    ]
    for copy in copies:
        copy.start()
    mean, inverse = moments(sum_refs, cells_all)
    gain = gain_ref[...]
    norm_ref[...] = jnp.concatenate(
        [mean, inverse, gain, jnp.zeros((5, mean.shape[1]), F32)], axis=0
    )
    own = normalise(own_ref[...], mean, inverse, gain)
    sib = jnp.concatenate([sib_first_ref[...], sib_second_ref[...]], axis=0)
    sib = normalise(sib, mean, inverse, gain)
    halo = normalise(near_rows(sib_first_ref, sib_second_ref, cols), mean, inverse, gain)
    both = jnp.concatenate([own, sib], axis=0)
    q_ref[...] = dot(jnp.concatenate([own, halo], axis=0), wq_ref[...]).astype(BF)
    k_ref[...] = dot(both, wk_ref[...]).astype(BF)

    def values():
        v_ref[...] = dot(both, wv_ref[...]).astype(BF)
        return v_ref[...]

    attend(q_ref[...], k_ref[...], values, exponent, *state_refs)
    for copy in copies:
        copy.wait()


def normal_of(norm_ref):
    return norm_ref[0:1], norm_ref[1:2], norm_ref[2:3]


def far_rows(first_ref, last_ref, cols):
    core = core_index()
    far = pl.multiple_of((1 - core) * (first_ref.shape[0] - cols), 16)
    first = first_ref[pl.ds(far, cols), :]
    if last_ref is None:
        return first
    return jnp.where(core == 0, first, last_ref[pl.ds(far, cols), :])


def project(block_ref, norm_ref, wk_ref, wv_ref, k_ref, v_ref):
    normed = normalise(block_ref[...], *normal_of(norm_ref))
    k_ref[...] = dot(normed, wk_ref[...]).astype(BF)
    v_ref[...] = dot(normed, wv_ref[...]).astype(BF)


def join_body(cols, exponent, single, *refs):
    first_ref, refs = refs[0], refs[1:]
    last_ref, refs = (None, refs) if single else (refs[0], refs[1:])
    (norm_ref, wq_ref, wk_ref, wv_ref, q_ref, k_ref, v_ref, peak_ref, sum_ref, mix_ref,
     far_ref, all_q_ref, all_peak_ref, all_sum_ref, all_mix_ref, new_k_ref, new_v_ref) = refs
    near = q_ref.shape[0]
    far = far_rows(first_ref, last_ref, cols)
    far_ref[...] = far
    far_q = dot(normalise(far, *normal_of(norm_ref)), wq_ref[...]).astype(BF)
    all_q_ref[:near] = q_ref[...]
    all_q_ref[near:] = far_q
    every = (all_peak_ref, all_sum_ref, all_mix_ref)
    for old, new in zip((peak_ref, sum_ref, mix_ref), every, strict=True):
        new[:near] = old[...]

    def values():
        project(first_ref, norm_ref, wk_ref, wv_ref, new_k_ref, new_v_ref)
        return v_ref[...]

    attend(far_q, k_ref[...], values, exponent, *[ref.at[pl.ds(near, cols)] for ref in every])


def more_body(exponent, block_ref, norm_ref, wk_ref, wv_ref, q_ref, *refs):
    old, out, new = refs[:3], refs[3:6], refs[6:9]
    k_ref, v_ref = refs[9:]
    project(block_ref, norm_ref, wk_ref, wv_ref, k_ref, v_ref)
    attend(q_ref[...], k_ref[...], v_ref[...], exponent, *new)
    merge(old, new, out, exponent, False)


def spread(act, cols):
    size = act.shape[0]
    col = lax.broadcasted_iota(jnp.int32, act.shape, 0) % cols
    left = jnp.where(col == 0, 0.0, pltpu.roll(act, 1, 0))
    right = jnp.where(col == cols - 1, 0.0, pltpu.roll(act, size - 1, 0))
    return jnp.concatenate([left.astype(BF), act.astype(BF), right.astype(BF)], axis=1)


def conv(wide_ref, taps, out_cells, cols):
    total = None
    for row in range(3):
        term = dot(wide_ref[row * cols : row * cols + out_cells, :], taps(row))
        total = term if total is None else total + term
    return total


def late_body(
    cols, exponent,
    own_ref, sib_first_ref, sib_second_ref, far_ref, block_ref, norm_ref, q_ref, peak_ref, sum_ref, mix_ref,
    k_ref, v_ref, wk_ref, wv_ref, wo_ref, taps_ref,
    even_ref, odd_ref, second_ref, wide_ref, mid_ref,
    keys_ref, values_ref, new_peak_ref, new_sum_ref, new_mix_ref, attended_ref,
):
    cells = own_ref.shape[0]
    core = core_index()
    normed = normalise(block_ref[...], *normal_of(norm_ref))
    keys_ref[:cells] = k_ref[...]
    keys_ref[cells:] = dot(normed, wk_ref[...]).astype(BF)

    def values():
        values_ref[:cells] = v_ref[...]
        values_ref[cells:] = dot(normed, wv_ref[...]).astype(BF)
        return values_ref[...]

    new = (new_peak_ref, new_sum_ref, new_mix_ref)
    attend(q_ref[...], keys_ref[...], values, exponent, *new)
    merge((peak_ref, sum_ref, mix_ref), new, (attended_ref,), exponent, True)
    change = dot(attended_ref[...], wo_ref[...])
    near = near_rows(sib_first_ref, sib_second_ref, cols)
    base = jnp.concatenate([own_ref[...], near, far_ref[...]], axis=0)
    mid = (base.astype(F32) + change).astype(BF)
    mid_ref[...] = mid[:cells]
    act = jax.nn.silu(mid.astype(F32)).astype(BF).astype(F32)
    far_act = jnp.where(far_is_inside(), act[cells + cols :], 0.0)
    above = pl.multiple_of(core * (cells + cols), 16)
    below = pl.multiple_of((1 - core) * (cells + cols), 16)
    for row in range(0, cells, cols):
        wide_ref[cols + row : 2 * cols + row] = spread(act[row : row + cols], cols)
    wide_ref[pl.ds(below, cols), :] = spread(act[cells : cells + cols], cols)
    wide_ref[pl.ds(above, cols), :] = spread(far_act, cols)
    first_tap = conv(wide_ref, lambda row: taps_ref[0, row], cells, cols)
    second_tap = conv(wide_ref, lambda row: taps_ref[1, row], cells, cols)
    second_ref[...] = second_tap
    even_ref[...] = (first_tap + second_tap).astype(BF)
    odd_ref[...] = first_tap.astype(BF)


def now_body(
    cols, wide_ref, mid_ref, second_ref, taps_ref, skip_hbm_ref, out_ref, tap_ref, skip_ref, sems
):
    copies = [
        pltpu.make_async_copy(skip_hbm_ref, skip_ref, sems.at[0]),
        pltpu.make_async_copy(taps_ref.at[2], tap_ref, sems.at[1]),
    ]
    for copy in copies:
        copy.start()
    cells = mid_ref.shape[0]
    copies[0].wait()
    skip = dot(mid_ref[...], skip_ref[...])
    copies[1].wait()
    last_tap = conv(wide_ref, lambda row: tap_ref[row], cells, cols) + skip
    out_ref[0] = last_tap
    out_ref[1] = last_tap + second_ref[...]


def odd_body(now_ref, own_ref, arrived_ref, sum_ref):
    before = jnp.where(lax.axis_index("tm") == 0, own_ref[...], arrived_ref[...])
    sum_ref[...] = (now_ref[1] + before.astype(F32)).astype(BF)


def last_body(odd_ref, now_ref, own_ref, arrived_ref, out_ref, even_ref, sems):
    odd_copy = pltpu.make_async_copy(odd_ref, out_ref.at[1], sems.at[1])
    odd_copy.start()
    before = jnp.where(lax.axis_index("tm") == 0, own_ref[...], arrived_ref[...])
    even_ref[...] = (now_ref[0] + before.astype(F32)).astype(BF)
    even_copy = pltpu.make_async_copy(even_ref, out_ref.at[0], sems.at[0])
    even_copy.start()
    odd_copy.wait()
    even_copy.wait()


def per_device(
    features,
    norm_gain,
    query_weight,
    key_weight,
    value_weight,
    out_weight,
    conv_weight,
    skip_weight,
):
    _, tile_rows, cols, channels = features.shape
    out_channels = conv_weight.shape[-1]
    cells = tile_rows * cols
    devices = lax.axis_size("tile")
    chips = devices // 2
    swap = [(i, i ^ 1) for i in range(devices)]
    own = features.reshape(cells, channels)

    def turned(array, by, flip):
        pairs = [(i, ((i + 2 * by) % devices) ^ flip) for i in range(devices)]
        return lax.ppermute(array, "tile", pairs)

    sums, own, first, second = call(
        stats_body,
        [
            jax.ShapeDtypeStruct((8, channels), F32),
            *[jax.ShapeDtypeStruct((n, channels), BF) for n in (cells, cols, cells - cols)],
        ],
        [pltpu.SemaphoreType.DMA((PIECES,))],
        STATS_COST,
        hbm(own),
        spaces=[pltpu.HBM],
    )
    sums = [sums] + [turned(sums, by, 1) for by in range(1, chips)]
    recv = [turned(own, by, 1) for by in range(1, chips)]
    sums = jnp.concatenate(sums, axis=0)
    first, second, sums = lax.optimization_barrier((first, second, sums))
    sib = [lax.ppermute(part, "tile", swap) for part in (first, second)]
    sums = [sums, lax.ppermute(sums, "tile", swap)]

    exponent = channels ** (-0.5) * 1.4426950408889634
    near = cells + cols
    every = near + cols
    taps = conv_weight.reshape(3, 3, 3 * channels, out_channels)
    first_taps = (2, *taps.shape[1:])
    weights = [norm_gain.reshape(1, channels), query_weight, key_weight, value_weight]
    held = call(
        stage_body,
        [jax.ShapeDtypeStruct(w.shape, w.dtype) for w in weights],
        [pltpu.SemaphoreType.DMA((len(weights),))],
        STAGE_COST,
        sums[0], *[hbm(w) for w in weights],
        spaces=[VMEM] + [pltpu.HBM] * len(weights),
    )
    _, wq, wk, wv = held

    def rows_of(rows, kind=BF, width=channels):
        return jax.ShapeDtypeStruct((rows, width), kind)

    def state_of(rows):
        return [rows_of(rows, F32, 128), rows_of(rows, F32, 128), rows_of(rows, F32)]

    def scratch_of(shapes):
        return [VMEM(shape.shape, shape.dtype) for shape in shapes]

    n_sums = len(sums)
    norm, q, k, v, *rest = call(
        functools.partial(early_body, devices * cells, cols, exponent, n_sums),
        [
            rows_of(8, F32),
            rows_of(near),
            rows_of(2 * cells),
            rows_of(2 * cells),
            *state_of(near),
            jax.ShapeDtypeStruct(out_weight.shape, BF),
            jax.ShapeDtypeStruct(first_taps, BF),
        ],
        [pltpu.SemaphoreType.DMA((2,))],
        EARLY_COST,
        own, *sib, *sums, *held, hbm(out_weight), hbm(taps),
        spaces=[VMEM] * (7 + n_sums) + [pltpu.HBM] * 2,
    )
    state, (wo, held_taps) = rest[:3], rest[3:]

    *recv, norm = lax.optimization_barrier((*recv, norm))
    rsib = [lax.ppermute(block, "tile", swap) for block in recv]
    ends = recv[:1] if chips == 2 else [recv[0], recv[-1]]
    far, q, *state, new_k, new_v = call(
        functools.partial(join_body, cols, exponent, chips == 2),
        [rows_of(cols), rows_of(every), *state_of(every), rows_of(cells), rows_of(cells)],
        [],
        JOIN_COST,
        *ends, norm, wq, wk, wv, q, k, v, *state,
    )
    for block in recv[1:] + rsib[:-1]:
        state = call(
            functools.partial(more_body, exponent),
            state_of(every),
            scratch_of([*state_of(every), rows_of(cells), rows_of(cells)]),
            10**9,
            block, norm, wk, wv, q, *state,
        )
    even, odd, second, wide, mid = call(
        functools.partial(late_body, cols, exponent),
        [
            rows_of(cells, BF, out_channels),
            rows_of(cells, BF, out_channels),
            rows_of(cells, F32, out_channels),
            rows_of(every, BF, 3 * channels),
            rows_of(cells),
        ],
        scratch_of([rows_of(2 * cells), rows_of(2 * cells), *state_of(every), rows_of(every)]),
        LATE_COST,
        own, *sib, far, rsib[-1], norm, q, *state, new_k, new_v, wk, wv, wo, held_taps,
    )
    spans = lax.axis_size("tm")
    arrived_odd = lax.ppermute(odd, "tm", [(i, (i + 1) % spans) for i in range(spans)])
    arrived_even = lax.ppermute(even, "tm", [(i, i + 1) for i in range(spans - 1)])
    both = jax.ShapeDtypeStruct((2, cells, out_channels), F32)
    now = call(
        functools.partial(now_body, cols),
        both,
        [
            VMEM(taps.shape[1:], BF),
            VMEM(skip_weight.shape, BF),
            pltpu.SemaphoreType.DMA((2,)),
        ],
        NOW_COST,
        wide, mid, second, hbm(taps), hbm(skip_weight),
        spaces=[VMEM] * 3 + [pltpu.HBM] * 2,
    )
    share = rows_of(cells, BF, out_channels)
    done_odd = call(odd_body, share, [], 1, now, odd, arrived_odd)
    done_odd, arrived_even = lax.optimization_barrier((done_odd, arrived_even))
    decoded = pl.pallas_call(
        last_body,
        out_shape=jax.ShapeDtypeStruct((2, cells, out_channels), BF),
        in_specs=[spec()] * 4,
        out_specs=spec(pltpu.HBM),
        scratch_shapes=[VMEM((cells, out_channels), BF), pltpu.SemaphoreType.DMA((2,))],
        compiler_params=pltpu.CompilerParams(vmem_limit_bytes=LIMIT),
    )(done_odd, now, even, arrived_even)
    return decoded.reshape(2, tile_rows, cols, out_channels)


def solution(mesh):
    in_specs = (P("tm", "tile", None, None), P(), P(), P(), P(), P(), P(), P())
    out_specs = P("tm", "tile", None, None)
    return jax.shard_map(
        per_device, mesh=mesh, in_specs=in_specs, out_specs=out_specs, check_vma=False
    )
```
